32 devices in a mesh: dp: 4 (over y, x), fsdp: 8 (over z, core).
Axes of the slice: x: 2, y: 2, z: 4, core: 2. Of those that a mesh axis runs over, the one named last changes fastest.
Arguments:
- tokens: bfloat16 [34816, 512], P(('dp', 'fsdp')), may hold values from -6 to 6
- frame_counts: int32 [32], P(('dp', 'fsdp')), may hold values from 1 to 17, as said below
- cotangent: bfloat16 [34816, 512], P(('dp', 'fsdp')), may hold values from -6 to 6
- w_qkv: float32 [2, 512, 1536], P(None, ('dp', 'fsdp'))
- w_out: float32 [2, 512, 512], P(None, ('dp', 'fsdp'))
- w_up: float32 [2, 512, 2048], P(None, ('dp', 'fsdp'))
- w_down: float32 [2, 2048, 512], P(None, ('dp', 'fsdp'))
- norm_params: float32 [2, 2, 2, 512], P(None, None, None, ('dp', 'fsdp'))
- first_qkv: float32 [2, 512, 1536], P(None, ('dp', 'fsdp')), may hold values from -448 to 448
- first_out: float32 [2, 512, 512], P(None, ('dp', 'fsdp')), may hold values from -448 to 448
- first_up: float32 [2, 512, 2048], P(None, ('dp', 'fsdp')), may hold values from -448 to 448
- first_down: float32 [2, 2048, 512], P(None, ('dp', 'fsdp')), may hold values from -512 to 512
- first_norm: float32 [2, 2, 2, 512], P(None, None, None, ('dp', 'fsdp')), may hold values from -1024 to 1024
- second_qkv: float32 [2, 512, 1536], P(None, ('dp', 'fsdp')), may hold values from 2785.28 to 44564.48
- second_out: float32 [2, 512, 512], P(None, ('dp', 'fsdp')), may hold values from 2785.28 to 44564.48
- second_up: float32 [2, 512, 2048], P(None, ('dp', 'fsdp')), may hold values from 2785.28 to 44564.48
- second_down: float32 [2, 2048, 512], P(None, ('dp', 'fsdp')), may hold values from 4177.92 to 69632
- second_norm: float32 [2, 2, 2, 512], P(None, None, None, ('dp', 'fsdp')), may hold values from 17408 to 278528
Outputs:
- block_out: bfloat16 [34816, 512], P(('dp', 'fsdp'))
- tokens_grad: float32 [34816, 512], P(('dp', 'fsdp'))
- new_qkv: float32 [2, 512, 1536], P(None, ('dp', 'fsdp'))
- new_out: float32 [2, 512, 512], P(None, ('dp', 'fsdp'))
- new_up: float32 [2, 512, 2048], P(None, ('dp', 'fsdp'))
- new_down: float32 [2, 2048, 512], P(None, ('dp', 'fsdp'))
- new_norm: float32 [2, 2, 2, 512], P(None, None, None, ('dp', 'fsdp'))
- copy_qkv: bfloat16 [2, 512, 1536], P(None, ('dp', 'fsdp'))
- copy_out: bfloat16 [2, 512, 512], P(None, ('dp', 'fsdp'))
- copy_up: bfloat16 [2, 512, 2048], P(None, ('dp', 'fsdp'))
- copy_down: bfloat16 [2, 2048, 512], P(None, ('dp', 'fsdp'))
- first_qkv_next: float32 [2, 512, 1536], P(None, ('dp', 'fsdp'))
- first_out_next: float32 [2, 512, 512], P(None, ('dp', 'fsdp'))
- first_up_next: float32 [2, 512, 2048], P(None, ('dp', 'fsdp'))
- first_down_next: float32 [2, 2048, 512], P(None, ('dp', 'fsdp'))
- first_norm_next: float32 [2, 2, 2, 512], P(None, None, None, ('dp', 'fsdp'))
- second_qkv_next: float32 [2, 512, 1536], P(None, ('dp', 'fsdp'))
- second_out_next: float32 [2, 512, 512], P(None, ('dp', 'fsdp'))
- second_up_next: float32 [2, 512, 2048], P(None, ('dp', 'fsdp'))
- second_down_next: float32 [2, 2048, 512], P(None, ('dp', 'fsdp'))
- second_norm_next: float32 [2, 2, 2, 512], P(None, None, None, ('dp', 'fsdp'))
- matrix_norms: float32 [2, 4, 2], replicated
The draws below stay inside these ranges and needn't reach their ends.
Inputs may be any that keep to these rules, and one draw needn't show every extreme that they name: `frame_counts`: in every draw some clip holds 17 video frames and some clip holds 1.
All inputs are finite; a program needn't handle non-finite values.
Results may differ from the reference program's by a relative error of at most 0.02.
The reference program's roundings to bfloat16 on the way count: a program that leaves them out, or rounds other values in their place, can miss the bound.
Values may be sent and summed in bfloat16 or wider, within the bound.
No kernel may reach another device: no remote copies, remote signals or barrier semaphores. Data moves between devices by JAX's collectives and lax.ppermute only.
A program may use at most 256 MiB of HBM per device.

```python
import math
import jax
import jax.numpy as jnp
from jax import lax

D = 512
HEADS = 8
HEAD_DIM = 64
FF = 2048
FRAMES = 17
WIN = 64
STEP = 5
CLIPS = 32
TOKENS = 34816


def rising(count, top):
    ramp = 1.0 + (top - 1.0) * jnp.arange(count, dtype=jnp.float32) / (count - 1)
    return ramp / jnp.sqrt((1.0 + top + top * top) / 3.0)


def draw_frame_counts(key, part):
    key = jax.random.fold_in(key, 6)
    keys = jax.random.split(key, 3)
    counts = jax.random.randint(keys[0], (CLIPS,), 1, FRAMES + 1)
    longest = jax.random.randint(keys[1], (), 0, CLIPS)
    shortest = (longest + jax.random.randint(keys[2], (), 1, CLIPS)) % CLIPS
    return counts.at[longest].set(FRAMES).at[shortest].set(1).astype(jnp.int32)


def draw_w_qkv(key, part):
    key = jax.random.fold_in(key, 1)
    base = jax.random.normal(key, (2, D, 3 * D), jnp.float32)
    top = 3.0
    return base * rising(D, top)[None, :, None] * D ** (-0.5)


def draw_w_out(key, part):
    key = jax.random.fold_in(key, 2)
    base = jax.random.normal(key, (2, D, D), jnp.float32)
    top = 3.0
    return base * rising(D, top)[None, :, None] * 3.0 * D ** (-0.5)


def draw_w_up(key, part):
    key = jax.random.fold_in(key, 3)
    base = jax.random.normal(key, (2, D, FF), jnp.float32)
    top = 3.0
    return base * rising(D, top)[None, :, None] * D ** (-0.5)


def draw_w_down(key, part):
    key = jax.random.fold_in(key, 4)
    base = jax.random.normal(key, (2, FF, D), jnp.float32)
    top = 3.0
    return base * rising(FF, top)[None, :, None] * FF ** (-0.5)


def draw_norm_params(key, part):
    key = jax.random.fold_in(key, 5)
    keys = jax.random.split(key, 2)
    gain_noise = jax.random.normal(keys[0], (2, 2, D), jnp.float32)
    shift_noise = jax.random.normal(keys[1], (2, 2, D), jnp.float32)
    top = 3.0
    gains = rising(D, top)[None, None, :] * (1.0 + 0.1 * gain_noise)
    return jnp.stack([gains, 0.3 * shift_noise], axis=2)


def steps_of(rng, dims, shards, low, top_value):
    loudness, own = 1.0, jax.random.fold_in(rng, 6)
    for axis_at, blocks in shards:
        steps = jnp.exp(jax.random.uniform(jax.random.fold_in(own, axis_at), (blocks,), jnp.float32, low / len(shards), top_value / len(shards)))
        loudness = loudness * jnp.repeat(steps, dims[axis_at] // blocks).reshape([-1 if axis == axis_at else 1 for axis in range(len(dims))])
    return loudness


def bell_draw(own_key, dims, deviation, reach, cuts=(), kind=jnp.bfloat16):
    array = deviation * jax.random.normal(own_key, dims, jnp.float32)
    if cuts:
        array = array * steps_of(own_key, dims, cuts, -0.22, 0.18)
    return jnp.clip(array, -reach, reach).astype(kind)


def setup_inputs(seed: int = 0) -> dict:
    seeds = jax.random.split(jax.random.key(seed), 19)
    return {
        "tokens": bell_draw(seeds[0], (TOKENS, D), 1.0, 6.0, ((0, 32),)),
        "frame_counts": draw_frame_counts(jax.random.fold_in(seeds[18], 71), 0),
        "cotangent": bell_draw(seeds[2], (TOKENS, D), 1.0, 6.0, ((0, 32),)),
        "w_qkv": draw_w_qkv(jax.random.fold_in(seeds[18], 71), 0),
        "w_out": draw_w_out(jax.random.fold_in(seeds[18], 71), 0),
        "w_up": draw_w_up(jax.random.fold_in(seeds[18], 71), 0),
        "w_down": draw_w_down(jax.random.fold_in(seeds[18], 71), 0),
        "norm_params": draw_norm_params(jax.random.fold_in(seeds[18], 71), 0),
        "first_qkv": bell_draw(seeds[8], (2, D, 3 * D), (0.4 * TOKENS ** 0.5), 448.0, ((1, 32),), jnp.float32),
        "first_out": bell_draw(seeds[9], (2, D, D), (0.4 * TOKENS ** 0.5), 448.0, ((1, 32),), jnp.float32),
        "first_up": bell_draw(seeds[10], (2, D, FF), (0.4 * TOKENS ** 0.5), 448.0, ((1, 32),), jnp.float32),
        "first_down": bell_draw(seeds[11], (2, FF, D), (0.5 * TOKENS ** 0.5), 512.0, ((1, 32),), jnp.float32),
        "first_norm": bell_draw(seeds[12], (2, 2, 2, D), (TOKENS ** 0.5), 1024.0, ((3, 32),), jnp.float32),
        "second_qkv": jnp.clip(jnp.exp(math.log(44564.48) - 2.7725887 * jax.random.uniform(seeds[13], (2, D, 3 * D), jnp.float32) ** steps_of(seeds[13], (2, D, 3 * D), ((1, 32),), -0.2, 0.2)), 2785.28, 44564.48),
        "second_out": jnp.clip(jnp.exp(math.log(44564.48) - 2.7725887 * jax.random.uniform(seeds[14], (2, D, D), jnp.float32) ** steps_of(seeds[14], (2, D, D), ((1, 32),), -0.2, 0.2)), 2785.28, 44564.48),
        "second_up": jnp.clip(jnp.exp(math.log(44564.48) - 2.7725887 * jax.random.uniform(seeds[15], (2, D, FF), jnp.float32) ** steps_of(seeds[15], (2, D, FF), ((1, 32),), -0.2, 0.2)), 2785.28, 44564.48),
        "second_down": jnp.clip(jnp.exp(math.log(69632.0) - 2.8134107 * jax.random.uniform(seeds[16], (2, FF, D), jnp.float32) ** steps_of(seeds[16], (2, FF, D), ((1, 32),), -0.2, 0.2)), 4177.92, 69632.0),
        "second_norm": jnp.clip(jnp.exp(math.log(278528.0) - 2.7725887 * jax.random.uniform(seeds[17], (2, 2, 2, D), jnp.float32) ** steps_of(seeds[17], (2, 2, 2, D), ((3, 32),), -0.2, 0.2)), 17408.0, 278528.0),
    }


@jax.custom_vjp
def low(v):
    return lax.optimization_barrier(v.astype(jnp.bfloat16)).astype(jnp.float32)

@jax.custom_vjp
def low_back(v):
    return v

def low_keep(v):
    return (low(v), None)

def low_pass(kept, grad):
    return (grad,)

def back_keep(v):
    return (v, None)

def back_low(kept, grad):
    return (low(grad),)
low.defvjp(low_keep, low_pass)
low_back.defvjp(back_keep, back_low)
NORM_EPS = 1e-05
ADAM_EPS = 1e-06
BETA_FIRST = 0.5
BETA_SECOND = 0.5
RATE = 0.25
DECAY_RATE = 0.01
MASKED = -1e+30
HIGH = lax.Precision.HIGHEST
SPATIAL_FORMS = ('fqhd,fkhd->fhqk', 'fhqk,fkhd->fqhd')
TEMPORAL_FORMS = ('qphd,kphd->phqk', 'phqk,kphd->qphd')

def layer_norm(inputs, gain_row, shift_row):
    center = inputs - lax.optimization_barrier(jnp.mean(inputs, axis=-1, keepdims=True))
    spread = lax.optimization_barrier(jnp.mean(center * center, axis=-1, keepdims=True))
    return center * lax.rsqrt(spread + NORM_EPS) * gain_row + shift_row

def product(left, right):
    return jnp.dot(left, right, precision=HIGH, preferred_element_type=jnp.float32)

def attention(projected, allowed, einsum_forms):
    columns = projected.shape[1] // 3
    layout = (FRAMES, WIN, HEADS, HEAD_DIM)
    queries = projected[:, :columns].reshape(layout)
    key_rows = projected[:, columns:2 * columns].reshape(layout)
    values = projected[:, 2 * columns:].reshape(layout)
    scores = low_back(jnp.einsum(einsum_forms[0], queries, key_rows, precision=HIGH) * HEAD_DIM ** (-0.5))
    scores = jnp.where(allowed, scores, MASKED)
    summit = lax.optimization_barrier(jnp.max(scores, axis=-1, keepdims=True))
    raised = jnp.exp(scores - summit)
    weights = low(raised / lax.optimization_barrier(jnp.sum(raised, axis=-1, keepdims=True)))
    attended = jnp.einsum(einsum_forms[1], weights, values, precision=HIGH)
    return attended.reshape(projected.shape[0], columns)

def block(inputs, matrices, gains, allowed, frame_gate, einsum_forms):
    weight_qkv, weight_out, weight_up, weight_down = matrices
    normed = low(layer_norm(inputs, gains[0, 0], gains[0, 1]))
    projected = low_back(low(product(normed, weight_qkv)))
    attended = low_back(low(attention(projected, allowed, einsum_forms)))
    branch = low_back(product(attended, weight_out))
    middle = inputs + branch * frame_gate
    hidden_in = low(layer_norm(middle, gains[1, 0], gains[1, 1]))
    upward = low_back(product(hidden_in, weight_up))
    hidden = low(jax.nn.gelu(upward, approximate=False))
    return middle + low_back(product(hidden, weight_down))

def forward(parameters, inputs, frame_count):
    frame_ids = jnp.arange(FRAMES)
    is_video = frame_ids < frame_count
    allowed = (frame_ids[None, :] <= frame_ids[:, None]) & (is_video[:, None] & is_video[None, :] | (frame_ids[:, None] == frame_ids[None, :]))
    frame_gate = jnp.repeat(is_video.astype(inputs.dtype), WIN)[:, None]
    lowered = tuple((low(member) for member in parameters))
    spatial = block(inputs, tuple((member[0] for member in lowered[:4])), lowered[4][0], True, 1.0, SPATIAL_FORMS)
    return block(spatial, tuple((member[1] for member in lowered[:4])), lowered[4][1], allowed, frame_gate, TEMPORAL_FORMS)

def adam_parts(weight_array, gradient, first_moment, second_moment):
    first_next = BETA_FIRST * first_moment + (1.0 - BETA_FIRST) * gradient
    second_next = BETA_SECOND * second_moment + (1.0 - BETA_SECOND) * gradient * gradient
    direction = first_next / (1.0 - BETA_FIRST ** STEP) / (jnp.sqrt(second_next / (1.0 - BETA_SECOND ** STEP)) + ADAM_EPS)
    return (first_next, second_next, direction)

def reference(tokens, frame_counts, cotangent, w_qkv, w_out, w_up, w_down, norm_params, first_qkv, first_out, first_up, first_down, first_norm, second_qkv, second_out, second_up, second_down, second_norm):
    parameters = (w_qkv, w_out, w_up, w_down, norm_params)
    clip_rows = FRAMES * WIN
    features = tokens.shape[1]
    inputs = tokens.astype(jnp.float32).reshape(-1, clip_rows, features)
    cotangents = cotangent.astype(jnp.float32).reshape(-1, clip_rows, features)

    def one_clip(running, member):
        clip_in, frame_count, clip_back = member
        result, backward = jax.vjp(lambda weight_set, values: forward(weight_set, values, frame_count), parameters, clip_in)
        gradients, input_grad = backward(clip_back)
        return (tuple((summed + gradient for summed, gradient in zip(running, gradients))), (result, input_grad))
    zero_grads = tuple((jnp.zeros_like(member) for member in parameters))
    gradients, (results, input_grads) = lax.scan(one_clip, zero_grads, (inputs, frame_counts, cotangents))
    firsts = (first_qkv, first_out, first_up, first_down)
    seconds = (second_qkv, second_out, second_up, second_down)
    updated, first_new, second_new, norm_rows = ([], [], [], [])
    for matrix_index in range(4):
        first_next, second_next, direction = adam_parts(parameters[matrix_index], gradients[matrix_index], firsts[matrix_index], seconds[matrix_index])
        direction = direction + DECAY_RATE * parameters[matrix_index]
        weight_norm = jnp.sqrt(lax.optimization_barrier(jnp.sum(parameters[matrix_index] * parameters[matrix_index], axis=(1, 2))))
        step_norm = jnp.sqrt(lax.optimization_barrier(jnp.sum(direction * direction, axis=(1, 2))))
        updated.append(parameters[matrix_index] - RATE * (weight_norm / step_norm)[:, None, None] * direction)
        first_new.append(first_next)
        second_new.append(second_next)
        norm_rows.append(jnp.stack([weight_norm, step_norm], axis=1))
    norm_first, norm_second, norm_direction = adam_parts(norm_params, gradients[4], first_norm, second_norm)
    norm_updated = norm_params - RATE * norm_direction
    matrix_norms = jnp.stack(norm_rows, axis=1)
    return (results.reshape(tokens.shape).astype(jnp.bfloat16), input_grads.reshape(tokens.shape), updated[0], updated[1], updated[2], updated[3], norm_updated, updated[0].astype(jnp.bfloat16), updated[1].astype(jnp.bfloat16), updated[2].astype(jnp.bfloat16), updated[3].astype(jnp.bfloat16), first_new[0], first_new[1], first_new[2], first_new[3], norm_first, second_new[0], second_new[1], second_new[2], second_new[3], norm_second, matrix_norms)
```

```python
import jax
import jax.numpy as jnp
from jax import lax
from jax.sharding import PartitionSpec as P

HEADS = 8
HEAD_DIM = 64
FRAMES = 17
WIN = 64
STEP = 5


NORM_EPS = 1e-05
ADAM_EPS = 1e-06
BETA_FIRST = 0.5
BETA_SECOND = 0.5
RATE = 0.25
DECAY_RATE = 0.01
MASKED = -1e30
SPATIAL_FORMS = (
    "gqhd,gkhd->ghqk",
    "ghqk,gkhd->gqhd",
    "ghqk,gqhd->gkhd",
    "gqhd,gkhd->ghqk",
    "ghqk,gkhd->gqhd",
    "ghqk,gqhd->gkhd",
)
TEMPORAL_FORMS = (
    "cqphd,ckphd->cphqk",
    "cphqk,ckphd->cqphd",
    "cphqk,cqphd->ckphd",
    "cqphd,ckphd->cphqk",
    "cphqk,ckphd->cqphd",
    "cphqk,cqphd->ckphd",
)


def layer_norm(inputs, gain_row, shift_row):
    center = inputs - jnp.mean(inputs, axis=-1, keepdims=True)
    spread = jnp.mean(center * center, axis=-1, keepdims=True)
    return center * lax.rsqrt(spread + NORM_EPS) * gain_row + shift_row


def gelu_pair(upward):
    cumulative = 0.5 * (1.0 + lax.erf(upward * 0.7071067811865476))
    return (
        upward * cumulative,
        cumulative + upward * jnp.exp(-0.5 * upward * upward) * 0.3989422804014327,
    )


def split_heads(projected, layout):
    columns = projected.shape[1] // 3
    return (
        projected[:, :columns].reshape(layout),
        projected[:, columns : 2 * columns].reshape(layout),
        projected[:, 2 * columns :].reshape(layout),
    )


def attend(projected, allowed, layout, einsum_forms):
    queries, key_rows, values = split_heads(projected, layout)
    scores = jnp.einsum(
        einsum_forms[0], queries, key_rows, preferred_element_type=jnp.float32
    ) * HEAD_DIM ** (-0.5)
    scores = jnp.where(allowed, scores, MASKED)
    summit = jnp.max(scores, axis=-1, keepdims=True)
    raised = jnp.exp(scores - summit)
    running = jnp.sum(raised, axis=-1, keepdims=True)
    weights = (raised / running).astype(jnp.bfloat16)
    attended = jnp.einsum(einsum_forms[1], weights, values, preferred_element_type=jnp.float32)
    return (
        attended.reshape(projected.shape[0], -1).astype(jnp.bfloat16),
        summit + jnp.log(running),
    )


def attend_back(projected, out_grad, log_total, allowed, layout, einsum_forms):
    queries, key_rows, values = split_heads(projected, layout)
    scale_factor = HEAD_DIM ** (-0.5)
    scores = (
        jnp.einsum(einsum_forms[0], queries, key_rows, preferred_element_type=jnp.float32)
        * scale_factor
    )
    scores = jnp.where(allowed, scores, MASKED)
    weights = jnp.exp(scores - log_total)
    out_heads = out_grad.reshape(queries.shape)
    value_grad = jnp.einsum(
        einsum_forms[2], weights.astype(jnp.bfloat16), out_heads, preferred_element_type=jnp.float32
    )
    weight_grad = jnp.einsum(einsum_forms[3], out_heads, values, preferred_element_type=jnp.float32)
    score_grad = (
        weights * (weight_grad - jnp.sum(weight_grad * weights, axis=-1, keepdims=True))
    ).astype(jnp.bfloat16)
    query_grad = (
        jnp.einsum(einsum_forms[4], score_grad, key_rows, preferred_element_type=jnp.float32)
        * scale_factor
    )
    key_grad = (
        jnp.einsum(einsum_forms[5], score_grad, queries, preferred_element_type=jnp.float32)
        * scale_factor
    )
    row_count = projected.shape[0]
    return jnp.concatenate(
        [
            query_grad.reshape(row_count, -1),
            key_grad.reshape(row_count, -1),
            value_grad.reshape(row_count, -1),
        ],
        axis=1,
    ).astype(jnp.bfloat16)


def pack_weights(part_qkv, part_out, part_up, part_down):
    return jnp.concatenate(
        [part_qkv[:, 512 * i : 512 * i + 512] for i in range(3)]
        + [part_out]
        + [part_up[:, 512 * i : 512 * i + 512] for i in range(4)]
        + [part_down],
        axis=0,
    ).astype(jnp.bfloat16)


def unpack_shards(packed, rows):
    pieces = [packed[:, rows * i : rows * i + rows].reshape(-1, 512) for i in range(8)]
    return (
        jnp.concatenate(pieces[:3], axis=1),
        pieces[3],
        jnp.concatenate(pieces[4:], axis=1),
        packed[:, 8 * rows :].reshape(-1, 512),
    )


def pack_grads(grad_qkv, grad_out, grad_up, grad_down, shards):
    def cut(matrix):
        return matrix.reshape(shards, -1, 512)

    return jnp.concatenate(
        [cut(grad_qkv[:, 512 * i : 512 * i + 512]) for i in range(3)]
        + [cut(grad_out)]
        + [cut(grad_up[:, 512 * i : 512 * i + 512]) for i in range(4)]
        + [cut(grad_down)],
        axis=1,
    ).astype(jnp.bfloat16)


def block_forward(stream, gathered, allowed, frame_gate, layout, einsum_forms):
    weight_qkv, weight_out, weight_up, weight_down, gain_rows = gathered
    gains = gain_rows.astype(jnp.float32)
    normed = layer_norm(stream, gains[0, 0], gains[0, 1]).astype(jnp.bfloat16)
    projected = jnp.dot(normed, weight_qkv, preferred_element_type=jnp.float32).astype(jnp.bfloat16)
    attended, log_total = attend(projected, allowed, layout, einsum_forms)
    branch = jnp.dot(attended, weight_out, preferred_element_type=jnp.float32)
    middle = stream + branch * frame_gate
    hidden_in = layer_norm(middle, gains[1, 0], gains[1, 1]).astype(jnp.bfloat16)
    upward = jnp.dot(hidden_in, weight_up, preferred_element_type=jnp.float32)
    value_part, gelu_slope = gelu_pair(upward)
    hidden = value_part.astype(jnp.bfloat16)
    result = middle + jnp.dot(hidden, weight_down, preferred_element_type=jnp.float32)
    return (
        result,
        (stream, normed, projected, attended, log_total, middle, hidden_in, hidden, gelu_slope),
    )


def block_backward(upstream, kept, gathered, allowed, frame_gate, layout, einsum_forms):
    stream, normed, projected, attended, log_total, middle, hidden_in, hidden, gelu_slope = kept
    weight_qkv, weight_out, weight_up, weight_down, gain_rows = gathered
    gains = gain_rows.astype(jnp.float32)
    out_grad = upstream.astype(jnp.bfloat16)
    grad_down = jnp.einsum("tf,td->fd", hidden, out_grad, preferred_element_type=jnp.float32)
    hidden_grad = jnp.einsum("td,fd->tf", out_grad, weight_down, preferred_element_type=jnp.float32)
    up_grad = (hidden_grad * gelu_slope).astype(jnp.bfloat16)
    grad_up = jnp.einsum("td,tf->df", hidden_in, up_grad, preferred_element_type=jnp.float32)
    hidden_in_grad = jnp.einsum("tf,df->td", up_grad, weight_up, preferred_element_type=jnp.float32)
    ignored, pull_second = jax.vjp(layer_norm, middle, gains[1, 0], gains[1, 1])
    middle_part, gain_second, shift_second = pull_second(hidden_in_grad)
    middle_grad = upstream + middle_part
    branch_grad = (middle_grad * frame_gate).astype(jnp.bfloat16)
    grad_out = jnp.einsum("ti,tj->ij", attended, branch_grad, preferred_element_type=jnp.float32)
    attended_grad = jnp.einsum(
        "tj,ij->ti", branch_grad, weight_out, preferred_element_type=jnp.float32
    ).astype(jnp.bfloat16)
    projected_grad = attend_back(projected, attended_grad, log_total, allowed, layout, einsum_forms)
    grad_qkv = jnp.einsum("ti,tj->ij", normed, projected_grad, preferred_element_type=jnp.float32)
    normed_grad = jnp.einsum(
        "tj,ij->ti", projected_grad, weight_qkv, preferred_element_type=jnp.float32
    )
    unused, pull_first = jax.vjp(layer_norm, stream, gains[0, 0], gains[0, 1])
    stream_part, gain_first, shift_first = pull_first(normed_grad)
    grad_norm = jnp.stack(
        [jnp.stack([gain_first, shift_first]), jnp.stack([gain_second, shift_second])]
    )
    return (middle_grad + stream_part, (grad_qkv, grad_out, grad_up, grad_down, grad_norm))


def adam_parts(gradient, first_moment, second_moment):
    first_next = BETA_FIRST * first_moment + (1.0 - BETA_FIRST) * gradient
    second_next = BETA_SECOND * second_moment + (1.0 - BETA_SECOND) * gradient * gradient
    direction = (
        first_next
        / (1.0 - BETA_FIRST**STEP)
        / (jnp.sqrt(second_next / (1.0 - BETA_SECOND**STEP)) + ADAM_EPS)
    )
    return (first_next, second_next, direction)


def body(
    tokens,
    frame_counts,
    cotangent,
    w_qkv,
    w_out,
    w_up,
    w_down,
    norm_params,
    first_qkv,
    first_out,
    first_up,
    first_down,
    first_norm,
    second_qkv,
    second_out,
    second_up,
    second_down,
    second_norm,
):
    masters = (w_qkv, w_out, w_up, w_down, norm_params)
    frame_ids = jnp.arange(FRAMES)
    is_video = frame_ids[None, :] < frame_counts[:, None]
    allowed = (frame_ids[None, None, :] <= frame_ids[None, :, None]) & (
        is_video[:, :, None] & is_video[:, None, :]
        | (frame_ids[None, :, None] == frame_ids[None, None, :])
    )
    allowed = allowed[:, None, None, :, :]
    frame_gate = jnp.broadcast_to(
        is_video.astype(jnp.float32)[:, :, None], is_video.shape + (WIN,)
    ).reshape(-1, 1)
    settings = (
        ((-1, WIN, HEADS, HEAD_DIM), SPATIAL_FORMS, True, 1.0),
        ((-1, FRAMES, WIN, HEADS, HEAD_DIM), TEMPORAL_FORMS, allowed, frame_gate),
    )
    stream = tokens.astype(jnp.float32)
    axes = ("dp", "fsdp")
    shards = lax.axis_size("dp") * lax.axis_size("fsdp")
    rows = w_out.shape[1]
    norm_rows = jnp.pad(
        norm_params.astype(jnp.bfloat16).reshape(1, -1), ((0, rows - 1), (0, 512 - 8 * rows))
    )
    saved = []
    fetched = []
    for layer_index in range(2):
        layout, einsum_forms, layer_allowed, layer_gate = settings[layer_index]
        packed = pack_weights(
            w_qkv[layer_index], w_out[layer_index], w_up[layer_index], w_down[layer_index]
        )
        if layer_index == 0:
            packed = jnp.concatenate([packed, norm_rows], axis=0)
        packed = lax.all_gather(packed, axes, axis=0)
        if layer_index == 0:
            gains_all = packed[:, 12 * rows, : 8 * rows].reshape(shards, 2, 2, 2, rows)
            gains_all = gains_all.transpose(1, 2, 3, 0, 4).reshape(2, 2, 2, -1)
            packed = packed[:, : 12 * rows]
        gathered = unpack_shards(packed, rows) + (gains_all[layer_index],)
        stream, kept = block_forward(
            stream, gathered, layer_allowed, layer_gate, layout, einsum_forms
        )
        saved.append(kept)
        fetched.append(gathered)
    block_out = stream.astype(jnp.bfloat16)
    upstream = cotangent.astype(jnp.float32)
    reduced = [None, None]
    norm_grads = [None, None]
    for layer_index in (1, 0):
        layout, einsum_forms, layer_allowed, layer_gate = settings[layer_index]
        upstream, local_grads = block_backward(
            upstream,
            saved[layer_index],
            fetched[layer_index],
            layer_allowed,
            layer_gate,
            layout,
            einsum_forms,
        )
        norm_grads[layer_index] = local_grads[4]
        packed = pack_grads(*local_grads[:4], shards)
        summed = lax.psum_scatter(packed, axes, scatter_dimension=0, tiled=False)
        reduced[layer_index] = unpack_shards(summed[None].astype(jnp.float32), rows)
    norm_parts = jnp.stack(norm_grads).reshape(8, shards, rows).transpose(1, 0, 2)
    stacked = [
        jnp.stack([reduced[0][member_index], reduced[1][member_index]]) for member_index in range(4)
    ]
    firsts = (first_qkv, first_out, first_up, first_down, first_norm)
    seconds = (second_qkv, second_out, second_up, second_down, second_norm)
    updates = [
        adam_parts(stacked[member_index], firsts[member_index], seconds[member_index])
        for member_index in range(4)
    ]
    directions = [
        updates[member_index][2] + DECAY_RATE * masters[member_index] for member_index in range(4)
    ]
    step_squares = jnp.stack(
        [jnp.sum(direction * direction, axis=(1, 2)) for direction in directions], axis=1
    )
    local_squares = jnp.stack(
        [
            jnp.stack([jnp.sum(matrix * matrix, axis=(1, 2)) for matrix in masters[:4]], axis=1),
            step_squares,
        ],
        axis=2,
    )
    message = jnp.concatenate(
        [
            norm_parts.reshape(shards, -1),
            jnp.broadcast_to(local_squares.reshape(1, 16), (shards, 16)),
        ],
        axis=1,
    )
    arrived = jnp.sum(lax.all_to_all(message, axes, 0, 0, tiled=True), axis=0)
    matrix_norms = jnp.sqrt(arrived[-16:].reshape(2, 4, 2))
    updates.append(
        adam_parts(arrived[:-16].reshape(2, 2, 2, rows), firsts[4], seconds[4])
    )
    updated = [
        masters[member_index]
        - RATE
        * (matrix_norms[:, member_index, 0] / matrix_norms[:, member_index, 1])[:, None, None]
        * directions[member_index]
        for member_index in range(4)
    ]
    norm_updated = norm_params - RATE * updates[4][2]
    return (
        block_out,
        upstream,
        updated[0],
        updated[1],
        updated[2],
        updated[3],
        norm_updated,
        updated[0].astype(jnp.bfloat16),
        updated[1].astype(jnp.bfloat16),
        updated[2].astype(jnp.bfloat16),
        updated[3].astype(jnp.bfloat16),
        updates[0][0],
        updates[1][0],
        updates[2][0],
        updates[3][0],
        updates[4][0],
        updates[0][1],
        updates[1][1],
        updates[2][1],
        updates[3][1],
        updates[4][1],
        matrix_norms,
    )


def solution(mesh):
    in_specs = (
        P(("dp", "fsdp"), None),
        P(("dp", "fsdp")),
        P(("dp", "fsdp"), None),
        P(None, ("dp", "fsdp"), None),
        P(None, ("dp", "fsdp"), None),
        P(None, ("dp", "fsdp"), None),
        P(None, ("dp", "fsdp"), None),
        P(None, None, None, ("dp", "fsdp")),
        P(None, ("dp", "fsdp"), None),
        P(None, ("dp", "fsdp"), None),
        P(None, ("dp", "fsdp"), None),
        P(None, ("dp", "fsdp"), None),
        P(None, None, None, ("dp", "fsdp")),
        P(None, ("dp", "fsdp"), None),
        P(None, ("dp", "fsdp"), None),
        P(None, ("dp", "fsdp"), None),
        P(None, ("dp", "fsdp"), None),
        P(None, None, None, ("dp", "fsdp")),
    )
    out_specs = (
        P(("dp", "fsdp"), None),
        P(("dp", "fsdp"), None),
        P(None, ("dp", "fsdp"), None),
        P(None, ("dp", "fsdp"), None),
        P(None, ("dp", "fsdp"), None),
        P(None, ("dp", "fsdp"), None),
        P(None, None, None, ("dp", "fsdp")),
        P(None, ("dp", "fsdp"), None),
        P(None, ("dp", "fsdp"), None),
        P(None, ("dp", "fsdp"), None),
        P(None, ("dp", "fsdp"), None),
        P(None, ("dp", "fsdp"), None),
        P(None, ("dp", "fsdp"), None),
        P(None, ("dp", "fsdp"), None),
        P(None, ("dp", "fsdp"), None),
        P(None, None, None, ("dp", "fsdp")),
        P(None, ("dp", "fsdp"), None),
        P(None, ("dp", "fsdp"), None),
        P(None, ("dp", "fsdp"), None),
        P(None, ("dp", "fsdp"), None),
        P(None, None, None, ("dp", "fsdp")),
        P(),
    )
    return jax.shard_map(body, mesh=mesh, in_specs=in_specs, out_specs=out_specs, check_vma=False)
```

```python
import jax
import jax.numpy as jnp
from jax import lax
from jax.experimental import pallas as pl
from jax.experimental.pallas import tpu as pltpu
from jax.sharding import PartitionSpec as P

HEADS = 8
HEAD_DIM = 64
FRAMES = 17
WIN = 64
STEP = 5
WIDTH = 512
BLOCKS = 32
SLAB = WIDTH // BLOCKS
TILES = 4
TILE = FRAMES * WIN // TILES
SPOTS = WIN // TILES
SCALE = HEAD_DIM ** (-0.5)
VMEM_BYTES = 56 * 2**20
COST = pl.CostEstimate(flops=10**8, bytes_accessed=10**5, transcendentals=0)

NORM_EPS = 1e-05
ADAM_EPS = 1e-06
BETA_FIRST = 0.5
BETA_SECOND = 0.5
RATE = 0.25
DECAY_RATE = 0.01
MASKED = -1e30


def row_norm(inputs):
    center = inputs - jnp.mean(inputs, axis=-1, keepdims=True)
    spread = jnp.mean(center * center, axis=-1, keepdims=True)
    scale = lax.rsqrt(spread + NORM_EPS)
    return center * scale, scale


def row_norm_back(grad, gain_row, normal, scale):
    scaled = grad * gain_row
    first = jnp.mean(scaled, axis=-1, keepdims=True)
    second = jnp.mean(scaled * normal, axis=-1, keepdims=True)
    return scale * (scaled - first - normal * second)


def fold_rows(array):
    return jnp.sum(array.reshape(-1, 8, array.shape[-1]), axis=0)


def gelu_pair(upward):
    bell = jnp.exp(-0.5 * upward * upward)
    place = 1.0 / (1.0 + 0.23164189 * jnp.abs(upward))
    tail = 0.5 * 1.061405429
    for factor in (-1.453152027, 1.421413741, -0.284496736, 0.254829592):
        tail = tail * place + 0.5 * factor
    tail = tail * place * bell
    cumulative = jnp.where(upward >= 0.0, 1.0 - tail, tail)
    return upward * cumulative, cumulative + 0.3989422804014327 * upward * bell


def dot_nn(left, right):
    return lax.dot_general(
        left, right, (((1,), (0,)), ((), ())), preferred_element_type=jnp.float32
    )


def dot_nt(left, right):
    return lax.dot_general(
        left, right, (((1,), (1,)), ((), ())), preferred_element_type=jnp.float32
    )


def dot_tn(left, right):
    return lax.dot_general(
        left, right, (((0,), (0,)), ((), ())), preferred_element_type=jnp.float32
    )


def slab(weights, index):
    return weights[:, SLAB * index : SLAB * index + SLAB, :].reshape(WIDTH, WIDTH)


def down_rows(weights, index):
    part = BLOCKS // 4
    return weights[part * index : part * index + part].reshape(WIDTH, WIDTH)


def weight_spec(array, index):
    return pl.BlockSpec(
        (BLOCKS, 4 * SLAB, WIDTH), lambda i: (0, index, 0), pipeline_mode=pl.Buffered(1)
    )


def stack_heads(pair):
    lane = lax.broadcasted_iota(jnp.int32, pair.shape, 1)
    zero = jnp.zeros_like(pair)
    return jnp.concatenate(
        [jnp.where(lane < HEAD_DIM, pair, zero), jnp.where(lane < HEAD_DIM, zero, pair)], axis=0
    )


def merge_heads(stacked):
    rows = stacked.shape[0] // 2
    lane = lax.broadcasted_iota(jnp.int32, (rows, 2 * HEAD_DIM), 1)
    return jnp.where(lane < HEAD_DIM, stacked[:rows], stacked[rows:])


def soft_weights(scores):
    raised = jnp.exp(scores - jnp.max(scores, axis=-1, keepdims=True))
    return raised * (1.0 / jnp.sum(raised, axis=-1, keepdims=True))


def attention_grads(weights, out_grad, queries, keys, values):
    value_grad = dot_tn(weights.astype(jnp.bfloat16), out_grad)
    weight_grad = dot_nt(out_grad, values)
    weights = weights.astype(jnp.float32)
    total = jnp.sum(weight_grad * weights, axis=-1, keepdims=True)
    score_grad = (weights * (weight_grad - total)).astype(jnp.bfloat16)
    query_grad = merge_heads(dot_nn(score_grad, keys)) * SCALE
    key_grad = dot_tn(score_grad, queries)
    return query_grad, key_grad, value_grad


def first_attention_kernel(
    tokens, weights, gains, normed_out, projected_out, probs, attended, middle_out, hidden_in_out,
    projected,
):
    step = pl.program_id(0)

    @pl.when(step < TILES)
    def _():
        normal, _ = row_norm(tokens[...].astype(jnp.float32))
        normed = (normal * gains[0:1, :] + gains[1:2, :]).astype(jnp.bfloat16)
        normed_out[...] = normed
        rows = pl.ds(pl.multiple_of(step * TILE, TILE), TILE)
        for index in range(3):
            part = dot_nn(normed, slab(weights, index)).astype(jnp.bfloat16)
            projected[rows, WIDTH * index : WIDTH * index + WIDTH] = part
            projected_out[:, WIDTH * index : WIDTH * index + WIDTH] = part

    @pl.when(step == TILES)
    def _():
        def one_frame(frame, carry):
            rows = pl.ds(pl.multiple_of(frame * WIN, WIN), WIN)
            for pair in range(HEADS // 2):
                lanes = 128 * pair
                queries = stack_heads(projected[rows, lanes : lanes + 128] * SCALE)
                keys = projected[rows, WIDTH + lanes : WIDTH + lanes + 128]
                values = projected[rows, 2 * WIDTH + lanes : 2 * WIDTH + lanes + 128]
                share = soft_weights(dot_nt(queries, keys)).astype(jnp.bfloat16)
                probs[frame, pair] = share
                attended[rows, lanes : lanes + 128] = merge_heads(dot_nn(share, values)).astype(
                    jnp.bfloat16
                )
            return carry

        lax.fori_loop(0, FRAMES, one_frame, 0)

    @pl.when(step > TILES)
    def _():
        rows = pl.ds(pl.multiple_of((step - TILES - 1) * TILE, TILE), TILE)
        middle = tokens[...].astype(jnp.float32) + dot_nn(attended[rows, :], slab(weights, 3))
        middle_out[...] = middle
        normal, _ = row_norm(middle)
        hidden_in_out[...] = (normal * gains[2:3, :] + gains[3:4, :]).astype(jnp.bfloat16)


def first_attention(tokens, weights, gains):
    count = tokens.shape[0]

    def early(width):
        return pl.BlockSpec((TILE, width), lambda i: (jnp.minimum(i, TILES - 1), 0))

    def late(width):
        return pl.BlockSpec((TILE, width), lambda i: (jnp.maximum(i - TILES - 1, 0), 0))

    def whole_out(*shape):
        return pl.BlockSpec(shape, lambda i: (0,) * len(shape))

    def out(width, kind):
        return jax.ShapeDtypeStruct((count, width), kind)

    return pl.pallas_call(
        first_attention_kernel,
        grid=(2 * TILES + 1,),
        in_specs=[
            pl.BlockSpec(
                (TILE, WIDTH), lambda i: (jnp.where(i < TILES, i, jnp.maximum(i - TILES - 1, 0)), 0)
            ),
            weight_spec(weights, 0),
            whole_out(4, WIDTH),
        ],
        out_specs=[
            early(WIDTH),
            early(3 * WIDTH),
            whole_out(FRAMES, HEADS // 2, 2 * WIN, WIN),
            whole_out(count, WIDTH),
            late(WIDTH),
            late(WIDTH),
        ],
        out_shape=[
            out(WIDTH, jnp.bfloat16),
            out(3 * WIDTH, jnp.bfloat16),
            jax.ShapeDtypeStruct((FRAMES, HEADS // 2, 2 * WIN, WIN), jnp.bfloat16),
            out(WIDTH, jnp.bfloat16),
            out(WIDTH, jnp.float32),
            out(WIDTH, jnp.bfloat16),
        ],
        scratch_shapes=[pltpu.VMEM((count, 3 * WIDTH), jnp.bfloat16)],
        compiler_params=pltpu.CompilerParams(vmem_limit_bytes=VMEM_BYTES),
        cost_estimate=COST,
        name="first_attention",
    )(tokens, weights, gains)


def first_mlp_kernel(middle, hidden_in, weights_up, weights_down, hidden_out, slope_out, result_out):
    result = middle[...]
    for index in range(4):
        columns = slice(WIDTH * index, WIDTH * index + WIDTH)
        value, slope = gelu_pair(dot_nn(hidden_in[...], slab(weights_up, index)))
        hidden = value.astype(jnp.bfloat16)
        hidden_out[:, columns] = hidden
        slope_out[:, columns] = slope.astype(jnp.bfloat16)
        result = result + dot_nn(hidden, down_rows(weights_down, index))
    result_out[...] = result


def first_mlp(middle, hidden_in, weights, weights_at):
    count = middle.shape[0]

    def tile(width):
        return pl.BlockSpec((TILE, width), lambda i: (i, 0))

    return pl.pallas_call(
        first_mlp_kernel,
        grid=(TILES,),
        in_specs=[
            tile(WIDTH),
            tile(WIDTH),
            weight_spec(weights, weights_at),
            weight_spec(weights, weights_at + 1),
        ],
        out_specs=[tile(4 * WIDTH), tile(4 * WIDTH), tile(WIDTH)],
        out_shape=[
            jax.ShapeDtypeStruct((count, 4 * WIDTH), jnp.bfloat16),
            jax.ShapeDtypeStruct((count, 4 * WIDTH), jnp.bfloat16),
            jax.ShapeDtypeStruct((count, WIDTH), jnp.float32),
        ],
        compiler_params=pltpu.CompilerParams(vmem_limit_bytes=VMEM_BYTES),
        cost_estimate=COST,
        name="first_mlp",
    )(middle, hidden_in, weights, weights)


def second_kernel(
    frame_count, inputs, cotangent, weights, weights_up, weights_down, gains, result_out, grad_out, normed_out, projected_grad_out,
    attended_out, branch_grad_out, hidden_in_out, up_grad_out, hidden_out, sums, caps, projected,
    slopes,
):
    @pl.when(pl.program_id(0) == 0)
    def _():
        row = lax.broadcasted_iota(jnp.int32, caps.shape, 0)
        column = lax.broadcasted_iota(jnp.int32, caps.shape, 1)
        late, soon = row // SPOTS, column // SPOTS
        video = (late < frame_count[0]) & (soon < frame_count[0])
        allowed = (row % SPOTS == column % SPOTS) & ((soon == late) | ((soon < late) & video))
        caps[...] = jnp.where(allowed, 3.0e38, MASKED)
        sums[...] = jnp.zeros_like(sums)

    def flat(ref):
        return ref[...].reshape(TILE, ref.shape[-1])

    def keep(ref, value):
        ref[...] = value.reshape(ref.shape).astype(ref.dtype)

    inside = lax.broadcasted_iota(jnp.int32, (TILE, 1), 0) // SPOTS < frame_count[0]
    gate = jnp.where(inside, 1.0, 0.0)
    stream = flat(inputs)
    normal_first, scale_first = row_norm(stream)
    normed = (normal_first * gains[0:1, :] + gains[1:2, :]).astype(jnp.bfloat16)
    keep(normed_out, normed)
    for index in range(3):
        part = dot_nn(normed, slab(weights, index))
        projected[:, WIDTH * index : WIDTH * index + WIDTH] = (
            part * SCALE if index == 0 else part
        ).astype(jnp.bfloat16)
    for pair in range(HEADS // 2):
        lanes = 128 * pair
        queries = stack_heads(projected[:, lanes : lanes + 128])
        keys = projected[:, WIDTH + lanes : WIDTH + lanes + 128]
        values = projected[:, 2 * WIDTH + lanes : 2 * WIDTH + lanes + 128]
        scores = dot_nt(queries, keys)
        cap = caps[...]
        share = soft_weights(jnp.minimum(scores, jnp.concatenate([cap, cap], axis=0)))
        part = merge_heads(dot_nn(share.astype(jnp.bfloat16), values)).astype(jnp.bfloat16)
        attended_out[:, :, lanes : lanes + 128] = part.reshape(FRAMES, SPOTS, 128)
    attended = flat(attended_out)
    middle = stream + gate * dot_nn(attended, slab(weights, 3))
    normal_second, scale_second = row_norm(middle)
    hidden_in = (normal_second * gains[2:3, :] + gains[3:4, :]).astype(jnp.bfloat16)
    keep(hidden_in_out, hidden_in)
    result = middle
    for index in range(4):
        columns = slice(WIDTH * index, WIDTH * index + WIDTH)
        value, slope = gelu_pair(dot_nn(hidden_in, slab(weights_up, index)))
        hidden = value.astype(jnp.bfloat16)
        hidden_out[:, :, columns] = hidden.reshape(FRAMES, SPOTS, WIDTH)
        slopes[:, columns] = slope
        result = result + dot_nn(hidden, down_rows(weights_down, index))
    keep(result_out, result)

    out_grad = flat(cotangent)
    hidden_in_grad = jnp.zeros((TILE, WIDTH), jnp.float32)
    for index in range(4):
        columns = slice(WIDTH * index, WIDTH * index + WIDTH)
        up_grad = (dot_nt(out_grad, down_rows(weights_down, index)) * slopes[:, columns]).astype(
            jnp.bfloat16
        )
        up_grad_out[:, :, columns] = up_grad.reshape(FRAMES, SPOTS, WIDTH)
        hidden_in_grad = hidden_in_grad + dot_nt(up_grad, slab(weights_up, index))
    sums[2] += fold_rows(hidden_in_grad * normal_second)
    sums[3] += fold_rows(hidden_in_grad)
    middle_grad = out_grad.astype(jnp.float32) + row_norm_back(
        hidden_in_grad, gains[2:3, :], normal_second, scale_second
    )
    branch_grad = (middle_grad * gate).astype(jnp.bfloat16)
    keep(branch_grad_out, branch_grad)
    attended_grad = dot_nt(branch_grad, slab(weights, 3)).astype(jnp.bfloat16)
    for pair in range(HEADS // 2):
        lanes = 128 * pair
        queries = stack_heads(projected[:, lanes : lanes + 128])
        keys = projected[:, WIDTH + lanes : WIDTH + lanes + 128]
        values = projected[:, 2 * WIDTH + lanes : 2 * WIDTH + lanes + 128]
        scores = dot_nt(queries, keys)
        cap = caps[...]
        share = soft_weights(jnp.minimum(scores, jnp.concatenate([cap, cap], axis=0)))
        parts = attention_grads(
            share, stack_heads(attended_grad[:, lanes : lanes + 128]), queries, keys, values
        )
        for index in range(3):
            start = WIDTH * index + lanes
            projected_grad_out[:, :, start : start + 128] = (
                parts[index].astype(jnp.bfloat16).reshape(FRAMES, SPOTS, 128)
            )
    normed_grad = jnp.zeros((TILE, WIDTH), jnp.float32)
    for index in range(3):
        part = projected_grad_out[:, :, WIDTH * index : WIDTH * index + WIDTH]
        normed_grad = normed_grad + dot_nt(part.reshape(TILE, WIDTH), slab(weights, index))
    sums[0] += fold_rows(normed_grad * normal_first)
    sums[1] += fold_rows(normed_grad)
    keep(
        grad_out,
        middle_grad + row_norm_back(normed_grad, gains[0:1, :], normal_first, scale_first),
    )


def second_block(frame_counts, inputs, cotangent, weights, gains):
    def tile(width):
        return pl.BlockSpec((FRAMES, SPOTS, width), lambda i: (0, i, 0))

    def whole(*shape):
        return pl.BlockSpec(shape, lambda i: (0,) * len(shape), pipeline_mode=pl.Buffered(1))

    widths = (
        (1, jnp.bfloat16),
        (1, jnp.float32),
        (1, jnp.bfloat16),
        (3, jnp.bfloat16),
        (1, jnp.bfloat16),
        (1, jnp.bfloat16),
        (1, jnp.bfloat16),
        (4, jnp.bfloat16),
        (4, jnp.bfloat16),
    )
    outs = pl.pallas_call(
        second_kernel,
        grid=(WIN // SPOTS,),
        in_specs=[
            pl.BlockSpec(memory_space=pltpu.SMEM),
            tile(WIDTH),
            tile(WIDTH),
            weight_spec(weights, 0),
            weight_spec(weights, 1),
            weight_spec(weights, 2),
            whole(4, WIDTH),
        ],
        out_specs=[tile(width * WIDTH) for width, kind in widths]
        + [pl.BlockSpec((4, 8, WIDTH), lambda i: (0, 0, 0))],
        out_shape=[
            jax.ShapeDtypeStruct((FRAMES, WIN, width * WIDTH), kind) for width, kind in widths
        ]
        + [jax.ShapeDtypeStruct((4, 8, WIDTH), jnp.float32)],
        scratch_shapes=[
            pltpu.VMEM((TILE, TILE), jnp.float32),
            pltpu.VMEM((TILE, 3 * WIDTH), jnp.bfloat16),
            pltpu.VMEM((TILE, 4 * WIDTH), jnp.float32),
        ],
        compiler_params=pltpu.CompilerParams(vmem_limit_bytes=VMEM_BYTES),
        cost_estimate=COST,
        name="second_block",
    )(
        frame_counts,
        inputs.reshape(FRAMES, WIN, WIDTH),
        cotangent.reshape(FRAMES, WIN, WIDTH),
        weights,
        weights,
        weights,
        gains,
    )
    return [array.reshape(FRAMES * WIN, -1) for array in outs[:-1]] + [outs[-1]]


def first_back_kernel(
    upstream, slopes, middle, weights, weights_up, weights_down, gains, out_grad_out, up_grad_out, branch_grad_out,
    attended_grad_out, middle_grad_out, sums,
):
    @pl.when(pl.program_id(0) == 0)
    def _():
        sums[...] = jnp.zeros_like(sums)

    out_grad = upstream[...].astype(jnp.bfloat16)
    out_grad_out[...] = out_grad
    hidden_in_grad = jnp.zeros((TILE, WIDTH), jnp.float32)
    for index in range(4):
        columns = slice(WIDTH * index, WIDTH * index + WIDTH)
        up_grad = (dot_nt(out_grad, down_rows(weights_down, index)) * slopes[:, columns]).astype(
            jnp.bfloat16
        )
        up_grad_out[:, columns] = up_grad
        hidden_in_grad = hidden_in_grad + dot_nt(up_grad, slab(weights_up, index))
    normal, scale = row_norm(middle[...])
    sums[0] += fold_rows(hidden_in_grad * normal)
    sums[1] += fold_rows(hidden_in_grad)
    middle_grad = upstream[...] + row_norm_back(hidden_in_grad, gains[2:3, :], normal, scale)
    middle_grad_out[...] = middle_grad
    branch_grad = middle_grad.astype(jnp.bfloat16)
    branch_grad_out[...] = branch_grad
    attended_grad_out[...] = dot_nt(branch_grad, slab(weights, 3)).astype(jnp.bfloat16)


def first_back(upstream, slopes, middle, weights, late_weights, late_at, gains):
    count = upstream.shape[0]

    def tile(width):
        return pl.BlockSpec((TILE, width), lambda i: (i, 0))

    def whole(*shape):
        return pl.BlockSpec(shape, lambda i: (0,) * len(shape), pipeline_mode=pl.Buffered(1))

    def out(width, kind):
        return jax.ShapeDtypeStruct((count, width), kind)

    return pl.pallas_call(
        first_back_kernel,
        grid=(TILES,),
        in_specs=[
            tile(WIDTH),
            tile(4 * WIDTH),
            tile(WIDTH),
            weight_spec(weights, 0),
            weight_spec(late_weights, late_at),
            weight_spec(late_weights, late_at + 1),
            whole(4, WIDTH),
        ],
        out_specs=[tile(WIDTH), tile(4 * WIDTH), tile(WIDTH), tile(WIDTH), tile(WIDTH)]
        + [pl.BlockSpec((2, 8, WIDTH), lambda i: (0, 0, 0))],
        out_shape=[
            out(WIDTH, jnp.bfloat16),
            out(4 * WIDTH, jnp.bfloat16),
            out(WIDTH, jnp.bfloat16),
            out(WIDTH, jnp.bfloat16),
            out(WIDTH, jnp.float32),
            jax.ShapeDtypeStruct((2, 8, WIDTH), jnp.float32),
        ],
        compiler_params=pltpu.CompilerParams(vmem_limit_bytes=VMEM_BYTES),
        cost_estimate=COST,
        name="first_back",
    )(upstream, slopes, middle, weights, late_weights, late_weights, gains)


def first_attention_back_kernel(projected, probs, attended_grad, projected_grad):
    def one_frame(frame, carry):
        rows = pl.ds(pl.multiple_of(frame * WIN, WIN), WIN)
        for pair in range(HEADS // 2):
            lanes = 128 * pair
            parts = attention_grads(
                probs[frame, pair],
                stack_heads(attended_grad[rows, lanes : lanes + 128]),
                stack_heads(projected[rows, lanes : lanes + 128] * SCALE),
                projected[rows, WIDTH + lanes : WIDTH + lanes + 128],
                projected[rows, 2 * WIDTH + lanes : 2 * WIDTH + lanes + 128],
            )
            for index in range(3):
                start = WIDTH * index + lanes
                projected_grad[rows, start : start + 128] = parts[index].astype(jnp.bfloat16)
        return carry

    lax.fori_loop(0, FRAMES, one_frame, 0)


def first_attention_back(projected, probs, attended_grad):
    return pl.pallas_call(
        first_attention_back_kernel,
        out_shape=jax.ShapeDtypeStruct(projected.shape, jnp.bfloat16),
        compiler_params=pltpu.CompilerParams(vmem_limit_bytes=VMEM_BYTES),
        cost_estimate=COST,
        name="first_attention_back",
    )(projected, probs, attended_grad)


def first_input_back_kernel(projected_grad, tokens, middle_grad, weights, gains, grad_out, sums):
    @pl.when(pl.program_id(0) == 0)
    def _():
        sums[...] = jnp.zeros_like(sums)

    normed_grad = jnp.zeros((TILE, WIDTH), jnp.float32)
    for index in range(3):
        part = projected_grad[:, WIDTH * index : WIDTH * index + WIDTH]
        normed_grad = normed_grad + dot_nt(part, slab(weights, index))
    normal, scale = row_norm(tokens[...].astype(jnp.float32))
    sums[0] += fold_rows(normed_grad * normal)
    sums[1] += fold_rows(normed_grad)
    grad_out[...] = middle_grad[...] + row_norm_back(normed_grad, gains[0:1, :], normal, scale)


def first_input_back(projected_grad, tokens, middle_grad, weights, gains):
    count = tokens.shape[0]

    def tile(width):
        return pl.BlockSpec((TILE, width), lambda i: (i, 0))

    def whole(*shape):
        return pl.BlockSpec(shape, lambda i: (0,) * len(shape), pipeline_mode=pl.Buffered(1))

    return pl.pallas_call(
        first_input_back_kernel,
        grid=(TILES,),
        in_specs=[
            tile(3 * WIDTH),
            tile(WIDTH),
            tile(WIDTH),
            whole(BLOCKS, 3 * SLAB, WIDTH),
            whole(4, WIDTH),
        ],
        out_specs=[tile(WIDTH), pl.BlockSpec((2, 8, WIDTH), lambda i: (0, 0, 0))],
        out_shape=[
            jax.ShapeDtypeStruct((count, WIDTH), jnp.float32),
            jax.ShapeDtypeStruct((2, 8, WIDTH), jnp.float32),
        ],
        compiler_params=pltpu.CompilerParams(vmem_limit_bytes=VMEM_BYTES),
        cost_estimate=COST,
        name="first_input_back",
    )(projected_grad, tokens, middle_grad, weights, gains)


def outer_kernel(core, left, right, mine, other):
    first = core[0] == 0
    for half in range(2):
        columns = slice(256 * half, 256 * half + 256)
        part = dot_tn(left[:, columns], right[...]).astype(jnp.bfloat16)
        blocks = mine.shape[0] // 2
        part = part.reshape(blocks, 2, -1, WIDTH)
        even, odd = part[:, 0], part[:, 1]
        place = slice(blocks * half, blocks * half + blocks)
        mine[place] = jnp.where(first, even, odd)
        other[place] = jnp.where(first, odd, even)


def outer_call(core, left, right, left_spec, right_spec, parts, out_spec, rows, name):
    count = left.shape[0]
    return pl.pallas_call(
        outer_kernel,
        grid=(parts,),
        in_specs=[pl.BlockSpec(memory_space=pltpu.SMEM), left_spec, right_spec],
        out_specs=[out_spec, out_spec],
        out_shape=[jax.ShapeDtypeStruct((BLOCKS // 2, rows, WIDTH), jnp.bfloat16)] * 2,
        compiler_params=pltpu.CompilerParams(vmem_limit_bytes=VMEM_BYTES),
        cost_estimate=COST,
        name=name,
    )(core, left, right)


def outer_columns(core, left, right, name):
    count, width = right.shape
    parts = width // WIDTH
    return outer_call(
        core,
        left,
        right,
        pl.BlockSpec((count, WIDTH), lambda i: (0, 0)),
        pl.BlockSpec((count, WIDTH), lambda i: (0, i)),
        parts,
        pl.BlockSpec((BLOCKS // 2, SLAB, WIDTH), lambda i: (0, i, 0)),
        SLAB * parts,
        name,
    )


def outer_rows(core, left, right, name):
    count, width = left.shape
    parts = width // WIDTH
    return outer_call(
        core,
        left,
        right,
        pl.BlockSpec((count, WIDTH), lambda i: (0, i)),
        pl.BlockSpec((count, WIDTH), lambda i: (0, 0)),
        parts,
        pl.BlockSpec((BLOCKS // 2 // parts, width // BLOCKS, WIDTH), lambda i: (i, 0, 0)),
        width // BLOCKS,
        name,
    )


def fold_cores_kernel(place, *refs):
    ins, outs = refs[:-4], refs[-4:]
    for which in range(4):

        @pl.when(pl.program_id(0) == which)
        def _(out=outs[which]):
            start = 0
            for index in range(0, len(ins), 2):
                rows = ins[index].shape[-2]
                out[:, start : start + rows, :] = (
                    ins[index][0].astype(jnp.float32) + ins[index + 1][0].astype(jnp.float32)
                ).astype(jnp.bfloat16)
                start += rows


def fold_cores(place, pairs, name):
    flat = [array.reshape(4, 4, -1, WIDTH) for pair in pairs for array in pair]
    total = sum(pair[0].shape[1] for pair in pairs)
    return pl.pallas_call(
        fold_cores_kernel,
        grid_spec=pltpu.PrefetchScalarGridSpec(
            num_scalar_prefetch=1,
            grid=(4,),
            in_specs=[
                pl.BlockSpec((1,) + array.shape[1:], lambda i, place: (place[0] ^ i, 0, 0, 0))
                for array in flat
            ],
            out_specs=[pl.BlockSpec((4, total, WIDTH), lambda i, place: (0, 0, 0))] * 4,
        ),
        out_shape=[jax.ShapeDtypeStruct((4, total, WIDTH), jnp.bfloat16)] * 4,
        compiler_params=pltpu.CompilerParams(vmem_limit_bytes=VMEM_BYTES),
        cost_estimate=COST,
        name=name,
    )(place, *flat)


def fold_planes_kernel(place, *refs):
    ins, outs = refs[:4], refs[4:]
    for which in range(4):
        block = place[1] ^ which
        total = ins[0][block].astype(jnp.float32)
        for ref in ins[1:]:
            total = total + ref[block].astype(jnp.float32)
        outs[which][...] = total.astype(jnp.bfloat16)


def fold_planes(place, pieces, name):
    total = pieces[0].shape[1]
    return pl.pallas_call(
        fold_planes_kernel,
        in_specs=[pl.BlockSpec(memory_space=pltpu.SMEM)]
        + [pl.BlockSpec(memory_space=pltpu.VMEM)] * 4,
        out_shape=[jax.ShapeDtypeStruct((total, WIDTH), jnp.bfloat16)] * 4,
        compiler_params=pltpu.CompilerParams(vmem_limit_bytes=VMEM_BYTES),
        cost_estimate=COST,
        name=name,
    )(place, *pieces)


def arrange_kernel(place, *refs):
    ins, out = refs[:-1], refs[-1]
    across, plane, core = place[0], place[1], place[2]
    for index, ref in enumerate(ins):
        column = (across ^ (index % 4)) * 8 + (core ^ (index // 4))
        for way in range(4):
            out[column + (plane ^ way) * 2] = ref[way]


def arrange(place, pieces, name):
    rows = pieces[0].shape[1]
    return pl.pallas_call(
        arrange_kernel,
        in_specs=[pl.BlockSpec(memory_space=pltpu.SMEM)]
        + [pl.BlockSpec(memory_space=pltpu.VMEM)] * 8,
        out_shape=jax.ShapeDtypeStruct((BLOCKS, rows, WIDTH), jnp.bfloat16),
        compiler_params=pltpu.CompilerParams(vmem_limit_bytes=VMEM_BYTES),
        cost_estimate=COST,
        name=name,
    )(place, *pieces)


def adam_parts(gradient, first_moment, second_moment):
    first_next = BETA_FIRST * first_moment + (1.0 - BETA_FIRST) * gradient
    second_next = BETA_SECOND * second_moment + (1.0 - BETA_SECOND) * gradient * gradient
    direction = (
        first_next
        / (1.0 - BETA_FIRST**STEP)
        / (jnp.sqrt(second_next / (1.0 - BETA_SECOND**STEP)) + ADAM_EPS)
    )
    return (first_next, second_next, direction)


def pack_weights(part_qkv, part_out, part_up, part_down):
    return jnp.concatenate(
        [part_qkv[:, WIDTH * i : WIDTH * i + WIDTH] for i in range(3)]
        + [part_out]
        + [part_up[:, WIDTH * i : WIDTH * i + WIDTH] for i in range(4)]
        + [part_down],
        axis=0,
    ).astype(jnp.bfloat16)


def to_blocks(packed, rows):
    if rows == SLAB:
        return packed
    packed = packed[:, : 12 * rows]
    slabs = packed[:, : 8 * rows].reshape(BLOCKS, -1, 8, rows, WIDTH).transpose(0, 2, 1, 3, 4)
    return jnp.concatenate(
        [
            slabs.reshape(BLOCKS, 8 * SLAB, WIDTH),
            packed[:, 8 * rows :].reshape(BLOCKS, 4 * SLAB, WIDTH),
        ],
        axis=1,
    )


def from_blocks(grads, rows, narrow):
    if rows == SLAB:
        return grads
    slabs = grads[:, : narrow * SLAB].reshape(BLOCKS, narrow, -1, rows, WIDTH)
    slabs = slabs.transpose(0, 2, 1, 3, 4).reshape(-1, narrow * rows, WIDTH)
    if grads.shape[1] == narrow * SLAB:
        return slabs
    wide = grads[:, narrow * SLAB :].reshape(slabs.shape[0], -1, WIDTH)
    return jnp.concatenate([slabs, wide], axis=1)


def swap(array, mask):
    count = lax.axis_size("dp") * lax.axis_size("fsdp")
    return lax.ppermute(array, ("dp", "fsdp"), [(device, device ^ mask) for device in range(count)])


def after(value, *others):
    return lax.optimization_barrier((value, *others))[0]


def gather_by_chips(shards):
    results = []
    steps = [(), ()]
    for shard in shards:
        shard = after(shard, *steps[0])
        steps[0] = [swap(shard, 2 * way) for way in (1, 2, 3)]
        pieces = after(jnp.stack([shard] + steps[0]), *steps[1])
        steps[1] = [swap(pieces, 8 * way) for way in (1, 2, 3)]
        results.append([pieces] + steps[1])
    return results


def gather_cores(pieces, place, name):
    return arrange(place, pieces + [swap(piece, 1) for piece in pieces], "arrange_" + name)


def scatter_cores(pairs, place, name):
    return fold_cores(place, [(mine, swap(other, 1)) for mine, other in pairs], "cores_" + name)


def scatter_chips(pieces, place, name, *others):
    pieces = [pieces[0]] + [swap(pieces[way], 8 * way) for way in (3, 1, 2)]
    pieces = [after(pieces[0], *others)] + pieces[1:]
    return fold_planes(place, pieces, "planes_" + name)


def scatter_planes(pieces):
    pieces = [pieces[0]] + [swap(pieces[way], 2 * way) for way in (3, 2, 1)]
    return sum(piece.astype(jnp.float32) for piece in pieces)


def scatter_whole(pairs, rows, narrow):
    grads = jnp.concatenate(
        [jnp.stack(pair, axis=1).reshape(BLOCKS, -1, WIDTH) for pair in pairs], axis=1
    )
    summed = lax.psum_scatter(
        from_blocks(grads, rows, narrow), ("dp", "fsdp"), scatter_dimension=0, tiled=False
    )
    return summed.astype(jnp.float32)


def body(
    tokens,
    frame_counts,
    cotangent,
    w_qkv,
    w_out,
    w_up,
    w_down,
    norm_params,
    first_qkv,
    first_out,
    first_up,
    first_down,
    first_norm,
    second_qkv,
    second_out,
    second_up,
    second_down,
    second_norm,
):
    masters = (w_qkv, w_out, w_up, w_down)
    axes = ("dp", "fsdp")
    shards = lax.axis_size("dp") * lax.axis_size("fsdp")
    rows = w_out.shape[1]
    by_chips = (lax.axis_size("dp"), lax.axis_size("fsdp")) == (4, 8)
    fsdp = lax.axis_index("fsdp")
    place = jnp.stack([lax.axis_index("dp"), fsdp // 2, fsdp % 2]).astype(jnp.int32)
    norm_rows = jnp.pad(
        norm_params.astype(jnp.bfloat16).reshape(1, -1), ((0, rows - 1), (0, WIDTH - 8 * rows))
    )
    shard = pack_weights(w_qkv[0], w_out[0], w_up[0], w_down[0])
    second_shard = pack_weights(w_qkv[1], w_out[1], w_up[1], w_down[1])
    if by_chips:
        early, late_pieces = gather_by_chips(
            [jnp.concatenate([shard[: 4 * rows], norm_rows], axis=0), shard[4 * rows :]]
        )
        early = gather_cores(early, place, "early")
        norm_values = early[:, 4 * rows, : 8 * rows]
    else:
        gathered = lax.all_gather(jnp.concatenate([shard, norm_rows], axis=0), axes, axis=0)
        norm_values = gathered[:, 12 * rows, : 8 * rows]
        early = to_blocks(gathered, rows)
    gains = norm_values.reshape(shards, 2, 4, rows)
    gains = gains.transpose(1, 2, 0, 3).reshape(2, 4, WIDTH).astype(jnp.float32)
    weights_second = to_blocks(lax.all_gather(second_shard, axes, axis=0), rows)

    normed, projected, probs, attended, middle, hidden_in = first_attention(tokens, early, gains[0])
    if by_chips:
        late_pieces = [after(piece, hidden_in) for piece in late_pieces]
        late, late_at = gather_cores(late_pieces, place, "late"), 0
    else:
        late, late_at = early, 1
    hidden, slopes, stream = first_mlp(middle, hidden_in, late, late_at)
    (
        block_out,
        upstream,
        normed_second,
        projected_grad_second,
        attended_second,
        branch_grad_second,
        hidden_in_second,
        up_grad_second,
        hidden_second,
        sums_second,
    ) = second_block(frame_counts, stream, cotangent, weights_second, gains[1])
    core = place[2:] if by_chips else jnp.zeros((1,), jnp.int32)
    up_pair = outer_columns(core, hidden_in_second, up_grad_second, "outer_up")
    down_pair = outer_rows(core, after(hidden_second, *up_pair), cotangent, "outer_down")
    qkv_pair = outer_columns(
        core, after(normed_second, *down_pair), projected_grad_second, "outer_qkv"
    )
    out_pair = outer_columns(
        core, after(attended_second, *qkv_pair), branch_grad_second, "outer_out"
    )
    pairs_second = [up_pair, out_pair, qkv_pair, down_pair]
    out_grad, up_grad, branch_grad, attended_grad, middle_grad, sums_late = first_back(
        after(upstream, *out_pair), slopes, middle, early, late, late_at, gains[0]
    )
    if by_chips:
        second = scatter_cores(pairs_second, place, "second")
        up_grad = after(up_grad, *second)
    up_pair = outer_columns(core, hidden_in, up_grad, "outer_up")
    down_pair = outer_rows(core, after(hidden, *up_pair), out_grad, "outer_down")
    out_pair = outer_columns(core, after(attended, *down_pair), branch_grad, "outer_out")
    pairs_first = [up_pair, out_pair, down_pair]
    if by_chips:
        first = scatter_cores(pairs_first, place, "first")
        attended_grad = after(attended_grad, *first)
    projected_grad = first_attention_back(projected, probs, attended_grad)
    if by_chips:
        second = scatter_chips(second, place, "second", projected_grad)
        normed = after(normed, *second)
    pairs_last = [outer_columns(core, normed, projected_grad, "outer_qkv")]
    if by_chips:
        first = scatter_chips(first, place, "first", *pairs_last[0])
        last = scatter_cores(pairs_last, place, "last")
        projected_grad = after(projected_grad, *last)
    tokens_grad, sums_early = first_input_back(
        projected_grad, tokens, middle_grad, early, gains[0]
    )
    if by_chips:
        last = scatter_chips(last, place, "last")
        reduced_second, reduced_first, reduced_last = (
            scatter_planes(pieces) for pieces in (second, first, last)
        )
    else:
        reduced_second = scatter_whole(pairs_second, rows, 8)
        reduced_first = scatter_whole(pairs_first, rows, 5)
        reduced_last = scatter_whole(pairs_last, rows, 3)

    def columns(packed, first, last):
        return jnp.concatenate(
            [packed[rows * index : rows * index + rows] for index in range(first, last)], axis=1
        )

    reduced_first = (
        columns(reduced_last, 0, 3),
        columns(reduced_first, 4, 5),
        columns(reduced_first, 0, 4),
        reduced_first[5 * rows :],
    )
    reduced_second = (
        columns(reduced_second, 5, 8),
        columns(reduced_second, 4, 5),
        columns(reduced_second, 0, 4),
        reduced_second[8 * rows :],
    )

    norm_parts = jnp.concatenate(
        [jnp.sum(part, axis=1) for part in (sums_early, sums_late, sums_second)]
    )
    norm_parts = norm_parts.reshape(8, shards, rows).transpose(1, 0, 2).reshape(shards, -1)
    stacked = [jnp.stack(pair) for pair in zip(reduced_first, reduced_second)]
    firsts = (first_qkv, first_out, first_up, first_down)
    seconds = (second_qkv, second_out, second_up, second_down)
    updates = [adam_parts(*parts) for parts in zip(stacked, firsts, seconds)]
    directions = [update[2] + DECAY_RATE * master for update, master in zip(updates, masters)]
    local_squares = jnp.stack(
        [
            jnp.stack([jnp.sum(matrix * matrix, axis=(1, 2)) for matrix in group], axis=1)
            for group in (masters, directions)
        ],
        axis=2,
    )
    message = jnp.concatenate(
        [norm_parts, jnp.broadcast_to(local_squares.reshape(1, 16), (shards, 16))], axis=1
    )
    arrived = jnp.sum(lax.all_to_all(message, axes, 0, 0, tiled=True), axis=0)
    matrix_norms = jnp.sqrt(arrived[-16:].reshape(2, 4, 2))
    norm_update = adam_parts(arrived[:-16].reshape(2, 2, 2, rows), first_norm, second_norm)
    updates.append(norm_update)
    updated = [
        masters[index]
        - RATE
        * (matrix_norms[:, index, 0] / matrix_norms[:, index, 1])[:, None, None]
        * directions[index]
        for index in range(4)
    ]
    return (
        block_out,
        tokens_grad,
        *updated,
        norm_params - RATE * norm_update[2],
        *(array.astype(jnp.bfloat16) for array in updated),
        *(update[0] for update in updates),
        *(update[1] for update in updates),
        matrix_norms,
    )


def solution(mesh):
    in_specs = (
        P(("dp", "fsdp"), None),
        P(("dp", "fsdp")),
        P(("dp", "fsdp"), None),
        P(None, ("dp", "fsdp"), None),
        P(None, ("dp", "fsdp"), None),
        P(None, ("dp", "fsdp"), None),
        P(None, ("dp", "fsdp"), None),
        P(None, None, None, ("dp", "fsdp")),
        P(None, ("dp", "fsdp"), None),
        P(None, ("dp", "fsdp"), None),
        P(None, ("dp", "fsdp"), None),
        P(None, ("dp", "fsdp"), None),
        P(None, None, None, ("dp", "fsdp")),
        P(None, ("dp", "fsdp"), None),
        P(None, ("dp", "fsdp"), None),
        P(None, ("dp", "fsdp"), None),
        P(None, ("dp", "fsdp"), None),
        P(None, None, None, ("dp", "fsdp")),
    )
    out_specs = (
        P(("dp", "fsdp"), None),
        P(("dp", "fsdp"), None),
        P(None, ("dp", "fsdp"), None),
        P(None, ("dp", "fsdp"), None),
        P(None, ("dp", "fsdp"), None),
        P(None, ("dp", "fsdp"), None),
        P(None, None, None, ("dp", "fsdp")),
        P(None, ("dp", "fsdp"), None),
        P(None, ("dp", "fsdp"), None),
        P(None, ("dp", "fsdp"), None),
        P(None, ("dp", "fsdp"), None),
        P(None, ("dp", "fsdp"), None),
        P(None, ("dp", "fsdp"), None),
        P(None, ("dp", "fsdp"), None),
        P(None, ("dp", "fsdp"), None),
        P(None, None, None, ("dp", "fsdp")),
        P(None, ("dp", "fsdp"), None),
        P(None, ("dp", "fsdp"), None),
        P(None, ("dp", "fsdp"), None),
        P(None, ("dp", "fsdp"), None),
        P(None, None, None, ("dp", "fsdp")),
        P(),
    )
    return jax.shard_map(body, mesh=mesh, in_specs=in_specs, out_specs=out_specs, check_vma=False)
```

```python
import jax
import jax.numpy as jnp
from jax import lax
from jax.experimental import pallas as pl
from jax.experimental.pallas import tpu as pltpu
from jax.sharding import PartitionSpec as P

HEADS = 8
HEAD_DIM = 64
FRAMES = 17
WIN = 64
STEP = 5
WIDTH = 512
BLOCKS = 32
SLAB = WIDTH // BLOCKS
TILES = 4
TILE = FRAMES * WIN // TILES
SPOTS = WIN // TILES
HALF = TILE // 2
GROUP = 9
SCALE = HEAD_DIM ** (-0.5)
VMEM_BYTES = 56 * 2**20
COST = pl.CostEstimate(flops=10**8, bytes_accessed=10**5, transcendentals=0)

NORM_EPS = 1e-05
ADAM_EPS = 1e-06
BETA_FIRST = 0.5
BETA_SECOND = 0.5
RATE = 0.25
DECAY_RATE = 0.01
MASKED = -1e30


def row_norm(inputs):
    center = inputs - jnp.mean(inputs, axis=-1, keepdims=True)
    spread = jnp.mean(center * center, axis=-1, keepdims=True)
    scale = lax.rsqrt(spread + NORM_EPS)
    return center * scale, scale


def row_norm_back(grad, gain_row, normal, scale):
    scaled = grad * gain_row
    first = jnp.mean(scaled, axis=-1, keepdims=True)
    second = jnp.mean(scaled * normal, axis=-1, keepdims=True)
    return scale * (scaled - first - normal * second)


def fold_rows(array):
    return jnp.sum(array.reshape(-1, 8, array.shape[-1]), axis=0)


def gelu_pair(upward):
    bell = jnp.exp(-0.5 * upward * upward)
    place = 1.0 / (1.0 + 0.23164189 * jnp.abs(upward))
    tail = 0.5 * 1.061405429
    for factor in (-1.453152027, 1.421413741, -0.284496736, 0.254829592):
        tail = tail * place + 0.5 * factor
    tail = tail * place * bell
    cumulative = jnp.where(upward >= 0.0, 1.0 - tail, tail)
    return upward * cumulative, cumulative + 0.3989422804014327 * upward * bell


def dot_nn(left, right):
    return lax.dot_general(
        left, right, (((1,), (0,)), ((), ())), preferred_element_type=jnp.float32
    )


def dot_nt(left, right):
    return lax.dot_general(
        left, right, (((1,), (1,)), ((), ())), preferred_element_type=jnp.float32
    )


def dot_tn(left, right):
    return lax.dot_general(
        left, right, (((0,), (0,)), ((), ())), preferred_element_type=jnp.float32
    )


def slab(weights, index):
    return weights[:, SLAB * index : SLAB * index + SLAB, :].reshape(WIDTH, WIDTH)


def down_rows(weights, index):
    part = BLOCKS // 4
    return weights[part * index : part * index + part].reshape(WIDTH, WIDTH)


def weight_spec(array, index):
    return pl.BlockSpec(
        (BLOCKS, 4 * SLAB, WIDTH), lambda i: (0, index, 0), pipeline_mode=pl.Buffered(1)
    )


def stack_heads(pair):
    lane = lax.broadcasted_iota(jnp.int32, pair.shape, 1)
    zero = jnp.zeros_like(pair)
    return jnp.concatenate(
        [jnp.where(lane < HEAD_DIM, pair, zero), jnp.where(lane < HEAD_DIM, zero, pair)], axis=0
    )


def merge_heads(stacked):
    rows = stacked.shape[0] // 2
    lane = lax.broadcasted_iota(jnp.int32, (rows, 2 * HEAD_DIM), 1)
    return jnp.where(lane < HEAD_DIM, stacked[:rows], stacked[rows:])


def soft_weights(scores, axis):
    raised = jnp.exp(scores - jnp.max(scores, axis=axis, keepdims=True))
    return raised * (1.0 / jnp.sum(raised, axis=axis, keepdims=True))


def pair_caps():
    row = lax.broadcasted_iota(jnp.int32, (4 * WIN, 2 * WIN), 0)
    column = lax.broadcasted_iota(jnp.int32, (4 * WIN, 2 * WIN), 1)
    return jnp.where(row // WIN % 2 == column // WIN, 3.0e38, MASKED)


def frame_pairs():
    return [min(2 * index, FRAMES - 2) for index in range((FRAMES + 1) // 2)]


def outer_store(core, left, right, mine, other, block, row, rows):
    first = core[0] == 0
    count = 128 // rows
    for half in range(2):
        part = dot_tn(left[:, 256 * half : 256 * half + 256], right).astype(jnp.bfloat16)
        part = part.reshape(count, 2, rows, WIDTH)
        even, odd = part[:, 0], part[:, 1]
        place = pl.ds(block + count * half, count), pl.ds(row, rows)
        mine[place] = jnp.where(first, even, odd)
        other[place] = jnp.where(first, odd, even)


def slab_row(step, first):
    return pl.multiple_of((step - first) * SLAB, SLAB)


def grad_specs(rows):
    return [pl.BlockSpec((BLOCKS // 2, rows, WIDTH), lambda i: (0, 0, 0))] * 2


def grad_shapes(rows):
    return [jax.ShapeDtypeStruct((BLOCKS // 2, rows, WIDTH), jnp.bfloat16)] * 2


def part_of(step, first):
    return pl.ds(pl.multiple_of((step - first) * WIDTH, WIDTH), WIDTH)


def first_attention_kernel(
    tokens, weights, gains, normed_out, projected_out, probs, attended, middle_out, hidden_in_out,
    projected,
):
    step = pl.program_id(0)

    @pl.when(step < TILES)
    def _():
        normal, _ = row_norm(tokens[...].astype(jnp.float32))
        normed = (normal * gains[0:1, :] + gains[1:2, :]).astype(jnp.bfloat16)
        normed_out[...] = normed
        rows = pl.ds(pl.multiple_of(step * TILE, TILE), TILE)
        for index in range(3):
            part = dot_nn(normed, slab(weights, index)).astype(jnp.bfloat16)
            projected[rows, WIDTH * index : WIDTH * index + WIDTH] = part
            projected_out[:, WIDTH * index : WIDTH * index + WIDTH] = part

    @pl.when(step == TILES)
    def _():
        caps = pair_caps()
        for index, frame in enumerate(frame_pairs()):
            rows = slice(WIN * frame, WIN * frame + 2 * WIN)
            lanes = [slice(128 * pair, 128 * pair + 128) for pair in range(HEADS // 2)]
            queries = [stack_heads(projected[rows, lane] * SCALE) for lane in lanes]
            keys = [projected[rows, WIDTH + 128 * pair : WIDTH + 128 * pair + 128] for pair in range(4)]
            scores = [jnp.minimum(dot_nt(*both), caps) for both in zip(queries, keys)]
            shares = [soft_weights(score, -1).astype(jnp.bfloat16) for score in scores]
            for pair, share in enumerate(shares):
                probs[index, pair] = share
                values = projected[rows, 2 * WIDTH + 128 * pair : 2 * WIDTH + 128 * pair + 128]
                attended[rows, lanes[pair]] = merge_heads(dot_nn(share, values)).astype(jnp.bfloat16)

    @pl.when(step > TILES)
    def _():
        rows = pl.ds(pl.multiple_of((step - TILES - 1) * TILE, TILE), TILE)
        middle = tokens[...].astype(jnp.float32) + dot_nn(attended[rows, :], slab(weights, 3))
        middle_out[...] = middle
        normal, _ = row_norm(middle)
        hidden_in_out[...] = (normal * gains[2:3, :] + gains[3:4, :]).astype(jnp.bfloat16)


def first_attention(tokens, weights, gains):
    count = tokens.shape[0]

    def early(width):
        return pl.BlockSpec((TILE, width), lambda i: (jnp.minimum(i, TILES - 1), 0))

    def late(width):
        return pl.BlockSpec((TILE, width), lambda i: (jnp.maximum(i - TILES - 1, 0), 0))

    def whole_out(*shape):
        return pl.BlockSpec(shape, lambda i: (0,) * len(shape))

    def out(width, kind):
        return jax.ShapeDtypeStruct((count, width), kind)

    return pl.pallas_call(
        first_attention_kernel,
        grid=(2 * TILES + 1,),
        in_specs=[
            pl.BlockSpec(
                (TILE, WIDTH), lambda i: (jnp.where(i < TILES, i, jnp.maximum(i - TILES - 1, 0)), 0)
            ),
            weight_spec(weights, 0),
            whole_out(4, WIDTH),
        ],
        out_specs=[
            early(WIDTH),
            early(3 * WIDTH),
            whole_out((FRAMES + 1) // 2, HEADS // 2, 4 * WIN, 2 * WIN),
            whole_out(count, WIDTH),
            late(WIDTH),
            late(WIDTH),
        ],
        out_shape=[
            out(WIDTH, jnp.bfloat16),
            out(3 * WIDTH, jnp.bfloat16),
            jax.ShapeDtypeStruct(((FRAMES + 1) // 2, HEADS // 2, 4 * WIN, 2 * WIN), jnp.bfloat16),
            out(WIDTH, jnp.bfloat16),
            out(WIDTH, jnp.float32),
            out(WIDTH, jnp.bfloat16),
        ],
        scratch_shapes=[pltpu.VMEM((count, 3 * WIDTH), jnp.bfloat16)],
        compiler_params=pltpu.CompilerParams(vmem_limit_bytes=VMEM_BYTES),
        cost_estimate=COST,
        name="first_attention",
    )(tokens, weights, gains)


def first_mlp_kernel(middle, hidden_in, weights_up, weights_down, hidden_out, slope_out, result_out):
    result = middle[...]
    for index in range(4):
        columns = slice(WIDTH * index, WIDTH * index + WIDTH)
        value, slope = gelu_pair(dot_nn(hidden_in[...], slab(weights_up, index)))
        hidden = value.astype(jnp.bfloat16)
        hidden_out[:, columns] = hidden
        slope_out[:, columns] = slope.astype(jnp.bfloat16)
        result = result + dot_nn(hidden, down_rows(weights_down, index))
    result_out[...] = result


def first_mlp(middle, hidden_in, weights, weights_at):
    count = middle.shape[0]

    def tile(width):
        return pl.BlockSpec((TILE, width), lambda i: (i, 0))

    return pl.pallas_call(
        first_mlp_kernel,
        grid=(TILES,),
        in_specs=[
            tile(WIDTH),
            tile(WIDTH),
            weight_spec(weights, weights_at),
            weight_spec(weights, weights_at + 1),
        ],
        out_specs=[tile(4 * WIDTH), tile(4 * WIDTH), tile(WIDTH)],
        out_shape=[
            jax.ShapeDtypeStruct((count, 4 * WIDTH), jnp.bfloat16),
            jax.ShapeDtypeStruct((count, 4 * WIDTH), jnp.bfloat16),
            jax.ShapeDtypeStruct((count, WIDTH), jnp.float32),
        ],
        compiler_params=pltpu.CompilerParams(vmem_limit_bytes=VMEM_BYTES),
        cost_estimate=COST,
        name="first_mlp",
    )(middle, hidden_in, weights, weights)


def second_kernel(
    frame_count, core, inputs, cotangent, weights, weights_up, weights_down, gains, result_out,
    grad_out, sums, mine, other,
    caps, query_rows, key_rows, value_rows, probs, slopes, normed, projected_grads, attended,
    branch_grads, hidden_in, up_grads, hidden, out_grads,
):
    step = pl.program_id(0)

    @pl.when(step == 0)
    def _():
        row = lax.broadcasted_iota(jnp.int32, caps.shape, 0)
        column = lax.broadcasted_iota(jnp.int32, caps.shape, 1) % HALF
        soon, late = row // 8, column // 8
        video = (late < frame_count[0]) & (soon < frame_count[0])
        allowed = (row % 8 == column % 8) & ((soon == late) | ((soon < late) & video))
        caps[...] = jnp.where(allowed, 3.0e38, MASKED)
        sums[...] = jnp.zeros_like(sums)

    def flat(ref):
        array = ref[...].astype(jnp.float32)
        return jnp.concatenate(
            [array[:, :8].reshape(HALF, WIDTH), array[:, 8:].reshape(HALF, WIDTH)], axis=0
        )

    def keep(ref, value):
        halves = [value[HALF * half : HALF * half + HALF] for half in range(2)]
        ref[...] = jnp.concatenate(
            [half.reshape(FRAMES, 8, WIDTH) for half in halves], axis=1
        ).astype(ref.dtype)

    @pl.when(step < TILES)
    def _():
        rows = pl.ds(pl.multiple_of(step * TILE, TILE), TILE)
        inside = lax.broadcasted_iota(jnp.int32, (TILE, 1), 0) % HALF // 8 < frame_count[0]
        gate = jnp.where(inside, 1.0, 0.0)
        stream = flat(inputs)
        normal_first, scale_first = row_norm(stream)
        normed_tile = (normal_first * gains[0:1, :] + gains[1:2, :]).astype(jnp.bfloat16)
        normed[rows, :] = normed_tile
        for index, ref in enumerate((query_rows, key_rows, value_rows)):
            part = dot_nn(normed_tile, slab(weights, index))
            for half in range(2):
                piece = part[HALF * half : HALF * half + HALF]
                if index == 0:
                    for pair in range(HEADS // 2):
                        stacked = stack_heads(piece[:, 128 * pair : 128 * pair + 128] * SCALE)
                        ref[half, pair] = stacked.astype(jnp.bfloat16)
                else:
                    ref[half] = piece.astype(jnp.bfloat16)
        units = [
            (half, pair, slice(128 * pair, 128 * pair + 128))
            for half in range(2)
            for pair in range(HEADS // 2)
        ]
        scores = [
            dot_nt(key_rows[half, :, lanes], query_rows[half, pair]) for half, pair, lanes in units
        ]
        shares = [
            soft_weights(jnp.minimum(score, caps[...]), 0).astype(jnp.bfloat16) for score in scores
        ]
        for share, (half, pair, _) in zip(shares, units):
            probs[half, pair] = share
        parts = [
            merge_heads(dot_tn(share, value_rows[half, :, lanes]))
            for share, (half, _, lanes) in zip(shares, units)
        ]
        halves = [jnp.concatenate(parts[4 * half : 4 * half + 4], axis=1) for half in range(2)]
        attended_tile = jnp.concatenate(halves, axis=0).astype(jnp.bfloat16)
        attended[rows, :] = attended_tile
        middle = stream + gate * dot_nn(attended_tile, slab(weights, 3))
        normal_second, scale_second = row_norm(middle)
        hidden_in_tile = (normal_second * gains[2:3, :] + gains[3:4, :]).astype(jnp.bfloat16)
        hidden_in[rows, :] = hidden_in_tile
        result = middle
        for index in range(4):
            columns = slice(WIDTH * index, WIDTH * index + WIDTH)
            value, slope = gelu_pair(dot_nn(hidden_in_tile, slab(weights_up, index)))
            hidden_tile = value.astype(jnp.bfloat16)
            hidden[rows, columns] = hidden_tile
            slopes[:, columns] = slope
            result = result + dot_nn(hidden_tile, down_rows(weights_down, index))
        keep(result_out, result)

        upstream = flat(cotangent)
        out_grad = upstream.astype(jnp.bfloat16)
        out_grads[rows, :] = out_grad
        hidden_in_grad = jnp.zeros((TILE, WIDTH), jnp.float32)
        for index in range(4):
            columns = slice(WIDTH * index, WIDTH * index + WIDTH)
            up_grad = (dot_nt(out_grad, down_rows(weights_down, index)) * slopes[:, columns]).astype(
                jnp.bfloat16
            )
            up_grads[rows, columns] = up_grad
            hidden_in_grad = hidden_in_grad + dot_nt(up_grad, slab(weights_up, index))
        sums[2] += fold_rows(hidden_in_grad * normal_second)
        sums[3] += fold_rows(hidden_in_grad)
        middle_grad = upstream + row_norm_back(
            hidden_in_grad, gains[2:3, :], normal_second, scale_second
        )
        branch_grad = (middle_grad * gate).astype(jnp.bfloat16)
        branch_grads[rows, :] = branch_grad
        attended_grad = dot_nt(branch_grad, slab(weights, 3))
        grads = [
            stack_heads(attended_grad[HALF * half : HALF * half + HALF, lanes]).astype(jnp.bfloat16)
            for half, _, lanes in units
        ]
        share_grads = [
            dot_nt(value_rows[half, :, lanes], grad) for grad, (half, _, lanes) in zip(grads, units)
        ]
        value_grads = [
            dot_nn(probs[half, pair], grad) for grad, (half, pair, _) in zip(grads, units)
        ]
        score_grads = []
        for share_grad, (half, pair, _) in zip(share_grads, units):
            share = probs[half, pair].astype(jnp.float32)
            total = jnp.sum(share_grad * share, axis=0, keepdims=True)
            score_grads.append((share * (share_grad - total)).astype(jnp.bfloat16))
        query_grads = [
            dot_tn(grad, key_rows[half, :, lanes])
            for grad, (half, _, lanes) in zip(score_grads, units)
        ]
        key_grads = [
            dot_nn(grad, query_rows[half, pair]) for grad, (half, pair, _) in zip(score_grads, units)
        ]
        query_grads = [merge_heads(grad) * SCALE for grad in query_grads]
        halves = [
            jnp.concatenate(
                [
                    part
                    for parts in (query_grads, key_grads, value_grads)
                    for part in parts[4 * half : 4 * half + 4]
                ],
                axis=1,
            )
            for half in range(2)
        ]
        projected_grad = jnp.concatenate(halves, axis=0).astype(jnp.bfloat16)
        projected_grads[rows, :] = projected_grad
        normed_grad = jnp.zeros((TILE, WIDTH), jnp.float32)
        for index in range(3):
            part = projected_grad[:, WIDTH * index : WIDTH * index + WIDTH]
            normed_grad = normed_grad + dot_nt(part, slab(weights, index))
        sums[0] += fold_rows(normed_grad * normal_first)
        sums[1] += fold_rows(normed_grad)
        keep(
            grad_out,
            middle_grad + row_norm_back(normed_grad, gains[0:1, :], normal_first, scale_first),
        )

    @pl.when((step >= TILES) & (step < TILES + 4))
    def _():
        right = up_grads[:, part_of(step, TILES)]
        outer_store(core, hidden_in, right, mine, other, 0, slab_row(step, TILES), SLAB)

    @pl.when((step >= TILES + 4) & (step < TILES + 7))
    def _():
        right = projected_grads[:, part_of(step, TILES + 4)]
        outer_store(core, normed, right, mine, other, 0, slab_row(step, TILES - 1), SLAB)

    @pl.when((step >= TILES + 7) & (step < TILES + 11))
    def _():
        left = hidden[:, part_of(step, TILES + 7)]
        block = (step - TILES - 7) * 4
        outer_store(core, left, out_grads[...], mine, other, block, 8 * SLAB, 4 * SLAB)

    @pl.when(step == TILES + 11)
    def _():
        outer_store(core, attended, branch_grads[...], mine, other, 0, 4 * SLAB, SLAB)


def second_block(frame_counts, core, inputs, cotangent, weights, gains):
    def tile(width):
        return pl.BlockSpec((FRAMES, SPOTS, width), lambda i: (0, jnp.minimum(i, TILES - 1), 0))

    def held(width):
        return pltpu.VMEM((FRAMES * WIN, width * WIDTH), jnp.bfloat16)

    whole = (FRAMES, WIN, WIDTH)
    outs = pl.pallas_call(
        second_kernel,
        grid=(TILES + 12,),
        in_specs=[
            pl.BlockSpec(memory_space=pltpu.SMEM),
            pl.BlockSpec(memory_space=pltpu.SMEM),
            tile(WIDTH),
            tile(WIDTH),
            weight_spec(weights, 0),
            weight_spec(weights, 1),
            weight_spec(weights, 2),
            pl.BlockSpec((4, WIDTH), lambda i: (0, 0)),
        ],
        out_specs=[
            tile(WIDTH),
            tile(WIDTH),
            pl.BlockSpec((4, 8, WIDTH), lambda i: (0, 0, 0)),
            *grad_specs(12 * SLAB),
        ],
        out_shape=[
            jax.ShapeDtypeStruct(whole, jnp.bfloat16),
            jax.ShapeDtypeStruct(whole, jnp.float32),
            jax.ShapeDtypeStruct((4, 8, WIDTH), jnp.float32),
            *grad_shapes(12 * SLAB),
        ],
        scratch_shapes=[
            pltpu.VMEM((HALF, 2 * HALF), jnp.float32),
            pltpu.VMEM((2, HEADS // 2, 2 * HALF, 128), jnp.bfloat16),
            pltpu.VMEM((2, HALF, WIDTH), jnp.bfloat16),
            pltpu.VMEM((2, HALF, WIDTH), jnp.bfloat16),
            pltpu.VMEM((2, HEADS // 2, HALF, 2 * HALF), jnp.bfloat16),
            pltpu.VMEM((TILE, 4 * WIDTH), jnp.float32),
            held(1),
            held(3),
            held(1),
            held(1),
            held(1),
            held(4),
            held(4),
            held(1),
        ],
        compiler_params=pltpu.CompilerParams(vmem_limit_bytes=VMEM_BYTES),
        cost_estimate=COST,
        name="second_block",
    )(
        frame_counts,
        core,
        inputs.reshape(whole),
        cotangent.reshape(whole),
        weights,
        weights,
        weights,
        gains,
    )
    return (
        outs[0].reshape(-1, WIDTH),
        outs[1].reshape(-1, WIDTH),
        outs[2],
        tuple(outs[3:]),
    )


def first_back_kernel(
    core, upstream, slopes, middle, weights, weights_up, weights_down, gains, hidden, hidden_in,
    attended, attended_grad_out, middle_grad_out, sums, mine, other, up_grads, out_grads, branch_grads,
):
    step = pl.program_id(0)

    @pl.when(step == 0)
    def _():
        sums[...] = jnp.zeros_like(sums)

    @pl.when(step < TILES)
    def _():
        rows = pl.ds(pl.multiple_of(step * TILE, TILE), TILE)
        out_grad = upstream[...].astype(jnp.bfloat16)
        out_grads[rows, :] = out_grad
        hidden_in_grad = jnp.zeros((TILE, WIDTH), jnp.float32)
        for index in range(4):
            columns = slice(WIDTH * index, WIDTH * index + WIDTH)
            up_grad = (dot_nt(out_grad, down_rows(weights_down, index)) * slopes[:, columns]).astype(
                jnp.bfloat16
            )
            up_grads[rows, columns] = up_grad
            hidden_in_grad = hidden_in_grad + dot_nt(up_grad, slab(weights_up, index))
        normal, scale = row_norm(middle[...])
        sums[0] += fold_rows(hidden_in_grad * normal)
        sums[1] += fold_rows(hidden_in_grad)
        middle_grad = upstream[...] + row_norm_back(hidden_in_grad, gains[2:3, :], normal, scale)
        middle_grad_out[...] = middle_grad
        branch_grad = middle_grad.astype(jnp.bfloat16)
        branch_grads[rows, :] = branch_grad
        attended_grad_out[...] = dot_nt(branch_grad, slab(weights, 3)).astype(jnp.bfloat16)

    @pl.when((step >= TILES) & (step < TILES + 4))
    def _():
        right = up_grads[:, part_of(step, TILES)]
        outer_store(core, hidden_in, right, mine, other, 0, slab_row(step, TILES), SLAB)

    @pl.when((step >= TILES + 4) & (step < TILES + 8))
    def _():
        block = (step - TILES - 4) * 4
        outer_store(core, hidden, out_grads[...], mine, other, block, 5 * SLAB, 4 * SLAB)

    @pl.when(step == TILES + 8)
    def _():
        outer_store(core, attended, branch_grads[...], mine, other, 0, 4 * SLAB, SLAB)


def first_back(
    core, upstream, slopes, middle, weights, late_weights, late_at, gains, hidden, hidden_in, attended
):
    count = upstream.shape[0]

    def tile(width):
        return pl.BlockSpec((TILE, width), lambda i: (jnp.minimum(i, TILES - 1), 0))

    def whole(*shape):
        return pl.BlockSpec(shape, lambda i: (0,) * len(shape))

    outs = pl.pallas_call(
        first_back_kernel,
        grid=(TILES + 9,),
        in_specs=[
            pl.BlockSpec(memory_space=pltpu.SMEM),
            tile(WIDTH),
            tile(4 * WIDTH),
            tile(WIDTH),
            weight_spec(weights, 0),
            weight_spec(late_weights, late_at),
            weight_spec(late_weights, late_at + 1),
            whole(4, WIDTH),
            pl.BlockSpec((count, WIDTH), lambda i: (0, jnp.clip(i - TILES - 4, 0, 3))),
            whole(count, WIDTH),
            whole(count, WIDTH),
        ],
        out_specs=[
            tile(WIDTH),
            tile(WIDTH),
            whole(2, 8, WIDTH),
            *grad_specs(9 * SLAB),
        ],
        out_shape=[
            jax.ShapeDtypeStruct((count, WIDTH), jnp.bfloat16),
            jax.ShapeDtypeStruct((count, WIDTH), jnp.float32),
            jax.ShapeDtypeStruct((2, 8, WIDTH), jnp.float32),
            *grad_shapes(9 * SLAB),
        ],
        scratch_shapes=[
            pltpu.VMEM((count, 4 * WIDTH), jnp.bfloat16),
            pltpu.VMEM((count, WIDTH), jnp.bfloat16),
            pltpu.VMEM((count, WIDTH), jnp.bfloat16),
        ],
        compiler_params=pltpu.CompilerParams(vmem_limit_bytes=VMEM_BYTES),
        cost_estimate=COST,
        name="first_back",
    )(
        core, upstream, slopes, middle, weights, late_weights, late_weights, gains, hidden, hidden_in,
        attended,
    )
    return (*outs[:3], tuple(outs[3:]))


def first_attention_back_kernel(
    core, queries_in, keys_in, values_in, probs, attended_grad, normed, projected_grad_out, mine,
    other, projected_grads,
):
    step = pl.program_id(0)

    @pl.when(step < HEADS // 2)
    def _():
        frames = list(enumerate(frame_pairs()))
        for some in (frames[at : at + GROUP] for at in range(0, len(frames), GROUP)):
            rows = [slice(WIN * frame, WIN * frame + 2 * WIN) for _, frame in some]
            out_grads = [stack_heads(attended_grad[row, :]) for row in rows]
            share_grads = [dot_nt(grad, values_in[row, :]) for grad, row in zip(out_grads, rows)]
            shares = [probs[index, 0] for index, _ in some]
            value_grads = [dot_tn(share, grad) for share, grad in zip(shares, out_grads)]
            score_grads = []
            for share, share_grad in zip(shares, share_grads):
                weights = share.astype(jnp.float32)
                total = jnp.sum(share_grad * weights, axis=-1, keepdims=True)
                score_grads.append((weights * (share_grad - total)).astype(jnp.bfloat16))
            query_grads = [dot_nn(grad, keys_in[row, :]) for grad, row in zip(score_grads, rows)]
            key_grads = [
                dot_tn(grad, stack_heads(queries_in[row, :] * SCALE))
                for grad, row in zip(score_grads, rows)
            ]
            query_grads = [merge_heads(grad) * SCALE for grad in query_grads]
            for index, grads in enumerate((query_grads, key_grads, value_grads)):
                lanes = pl.ds(pl.multiple_of(step * 128 + WIDTH * index, 128), 128)
                for row, grad in zip(rows, grads):
                    projected_grads[row, lanes] = grad.astype(jnp.bfloat16)

    @pl.when(step >= HEADS // 2)
    def _():
        right = projected_grads[:, part_of(step, HEADS // 2)]
        projected_grad_out[...] = right
        outer_store(core, normed, right, mine, other, 0, slab_row(step, HEADS // 2), SLAB)


def first_attention_back(core, projected, probs, attended_grad, normed):
    count = projected.shape[0]
    pairs = HEADS // 2

    def lanes(first):
        return pl.BlockSpec((count, 128), lambda i: (0, first + jnp.minimum(i, pairs - 1)))

    outs = pl.pallas_call(
        first_attention_back_kernel,
        grid=(pairs + 3,),
        in_specs=[
            pl.BlockSpec(memory_space=pltpu.SMEM),
            lanes(0),
            lanes(pairs),
            lanes(2 * pairs),
            pl.BlockSpec(
                ((FRAMES + 1) // 2, 1, 4 * WIN, 2 * WIN),
                lambda i: (0, jnp.minimum(i, pairs - 1), 0, 0),
            ),
            lanes(0),
            pl.BlockSpec((count, WIDTH), lambda i: (0, 0)),
        ],
        out_specs=[
            pl.BlockSpec((count, WIDTH), lambda i: (0, jnp.clip(i - pairs, 0, 2))),
            *grad_specs(3 * SLAB),
        ],
        out_shape=[
            jax.ShapeDtypeStruct((count, 3 * WIDTH), jnp.bfloat16),
            *grad_shapes(3 * SLAB),
        ],
        scratch_shapes=[pltpu.VMEM((count, 3 * WIDTH), jnp.bfloat16)],
        compiler_params=pltpu.CompilerParams(vmem_limit_bytes=VMEM_BYTES),
        cost_estimate=COST,
        name="first_attention_back",
    )(core, projected, projected, projected, probs, attended_grad, normed)
    return outs[0], tuple(outs[1:])


def first_input_back_kernel(projected_grad, tokens, middle_grad, weights, gains, grad_out, sums):
    @pl.when(pl.program_id(0) == 0)
    def _():
        sums[...] = jnp.zeros_like(sums)

    normed_grad = jnp.zeros((TILE, WIDTH), jnp.float32)
    for index in range(3):
        part = projected_grad[:, WIDTH * index : WIDTH * index + WIDTH]
        normed_grad = normed_grad + dot_nt(part, slab(weights, index))
    normal, scale = row_norm(tokens[...].astype(jnp.float32))
    sums[0] += fold_rows(normed_grad * normal)
    sums[1] += fold_rows(normed_grad)
    grad_out[...] = middle_grad[...] + row_norm_back(normed_grad, gains[0:1, :], normal, scale)


def first_input_back(projected_grad, tokens, middle_grad, weights, gains):
    count = tokens.shape[0]

    def tile(width):
        return pl.BlockSpec((TILE, width), lambda i: (i, 0))

    def whole(*shape):
        return pl.BlockSpec(shape, lambda i: (0,) * len(shape), pipeline_mode=pl.Buffered(1))

    return pl.pallas_call(
        first_input_back_kernel,
        grid=(TILES,),
        in_specs=[
            tile(3 * WIDTH),
            tile(WIDTH),
            tile(WIDTH),
            whole(BLOCKS, 3 * SLAB, WIDTH),
            whole(4, WIDTH),
        ],
        out_specs=[tile(WIDTH), pl.BlockSpec((2, 8, WIDTH), lambda i: (0, 0, 0))],
        out_shape=[
            jax.ShapeDtypeStruct((count, WIDTH), jnp.float32),
            jax.ShapeDtypeStruct((2, 8, WIDTH), jnp.float32),
        ],
        compiler_params=pltpu.CompilerParams(vmem_limit_bytes=VMEM_BYTES),
        cost_estimate=COST,
        name="first_input_back",
    )(projected_grad, tokens, middle_grad, weights, gains)


def arrange_kernel(place, *refs):
    ins, out = refs[:-1], refs[-1]
    across, plane, core = place[0], place[1], place[2]
    for index, ref in enumerate(ins):
        column = (across ^ (index % 4)) * 8 + (core ^ (index // 4))
        for way in range(4):
            out[column + (plane ^ way) * 2] = ref[way]


def arrange(place, pieces, name):
    rows = pieces[0].shape[1]
    return pl.pallas_call(
        arrange_kernel,
        in_specs=[pl.BlockSpec(memory_space=pltpu.SMEM)]
        + [pl.BlockSpec(memory_space=pltpu.VMEM)] * 8,
        out_shape=jax.ShapeDtypeStruct((BLOCKS, rows, WIDTH), jnp.bfloat16),
        compiler_params=pltpu.CompilerParams(vmem_limit_bytes=VMEM_BYTES),
        cost_estimate=COST,
        name=name,
    )(place, *pieces)


def adam_parts(gradient, first_moment, second_moment):
    first_next = BETA_FIRST * first_moment + (1.0 - BETA_FIRST) * gradient
    second_next = BETA_SECOND * second_moment + (1.0 - BETA_SECOND) * gradient * gradient
    direction = (
        first_next
        / (1.0 - BETA_FIRST**STEP)
        / (jnp.sqrt(second_next / (1.0 - BETA_SECOND**STEP)) + ADAM_EPS)
    )
    return (first_next, second_next, direction)


def pack_weights(part_qkv, part_out, part_up, part_down):
    return jnp.concatenate(
        [part_qkv[:, WIDTH * i : WIDTH * i + WIDTH] for i in range(3)]
        + [part_out]
        + [part_up[:, WIDTH * i : WIDTH * i + WIDTH] for i in range(4)]
        + [part_down],
        axis=0,
    ).astype(jnp.bfloat16)


def to_blocks(packed, rows):
    if rows == SLAB:
        return packed
    packed = packed[:, : 12 * rows]
    slabs = packed[:, : 8 * rows].reshape(BLOCKS, -1, 8, rows, WIDTH).transpose(0, 2, 1, 3, 4)
    return jnp.concatenate(
        [
            slabs.reshape(BLOCKS, 8 * SLAB, WIDTH),
            packed[:, 8 * rows :].reshape(BLOCKS, 4 * SLAB, WIDTH),
        ],
        axis=1,
    )


def from_blocks(grads, rows, narrow):
    if rows == SLAB:
        return grads
    slabs = grads[:, : narrow * SLAB].reshape(BLOCKS, narrow, -1, rows, WIDTH)
    slabs = slabs.transpose(0, 2, 1, 3, 4).reshape(-1, narrow * rows, WIDTH)
    if grads.shape[1] == narrow * SLAB:
        return slabs
    wide = grads[:, narrow * SLAB :].reshape(slabs.shape[0], -1, WIDTH)
    return jnp.concatenate([slabs, wide], axis=1)


def swap(array, mask):
    count = lax.axis_size("dp") * lax.axis_size("fsdp")
    return lax.ppermute(array, ("dp", "fsdp"), [(device, device ^ mask) for device in range(count)])


def after(value, *others):
    return lax.optimization_barrier((value, *others))[0]


def gather_by_chips(shards):
    results = []
    steps = [(), ()]
    for shard in shards:
        shard = after(shard, *steps[0])
        steps[0] = [swap(shard, 2 * way) for way in (1, 2, 3)]
        pieces = after(jnp.stack([shard] + steps[0]), *steps[1])
        steps[1] = [swap(pieces, 8 * way) for way in (1, 2, 3)]
        results.append([pieces] + steps[1])
    return results


def gather_cores(pieces, place, name):
    return arrange(place, pieces + [swap(piece, 1) for piece in pieces], "arrange_" + name)


def sum_at(arrays, index):
    total = sum(
        lax.dynamic_index_in_dim(array, index, 0, keepdims=False).astype(jnp.float32)
        for array in arrays
    )
    return total.astype(jnp.bfloat16)


def scatter_cores(pair, place):
    both = [array.reshape(4, 4, -1, WIDTH) for array in (pair[0], swap(pair[1], 1))]
    return [sum_at(both, place[0] ^ way) for way in (0, 3, 1, 2)]


def swap_chips(pieces):
    return [pieces[0]] + [swap(piece, 8 * way) for piece, way in zip(pieces[1:], (3, 1, 2))]


def fold_planes(pieces, place):
    return [sum_at(pieces, place[1] ^ way) for way in (0, 3, 2, 1)]


def scatter_planes(pieces, *others):
    pieces = [pieces[0]] + [swap(piece, 2 * way) for piece, way in zip(pieces[1:], (3, 2, 1))]
    pieces[0] = after(pieces[0], *others)
    return sum(piece.astype(jnp.float32) for piece in pieces)


def scatter_whole(pair, rows, narrow):
    grads = jnp.stack(pair, axis=1).reshape(BLOCKS, -1, WIDTH)
    summed = lax.psum_scatter(
        from_blocks(grads, rows, narrow), ("dp", "fsdp"), scatter_dimension=0, tiled=False
    )
    return summed.astype(jnp.float32)


def body(
    tokens,
    frame_counts,
    cotangent,
    w_qkv,
    w_out,
    w_up,
    w_down,
    norm_params,
    first_qkv,
    first_out,
    first_up,
    first_down,
    first_norm,
    second_qkv,
    second_out,
    second_up,
    second_down,
    second_norm,
):
    masters = (w_qkv, w_out, w_up, w_down)
    axes = ("dp", "fsdp")
    shards = lax.axis_size("dp") * lax.axis_size("fsdp")
    rows = w_out.shape[1]
    by_chips = (lax.axis_size("dp"), lax.axis_size("fsdp")) == (4, 8)
    fsdp = lax.axis_index("fsdp")
    place = jnp.stack([lax.axis_index("dp"), fsdp // 2, fsdp % 2]).astype(jnp.int32)
    norm_rows = jnp.pad(
        norm_params.astype(jnp.bfloat16).reshape(1, -1), ((0, rows - 1), (0, WIDTH - 8 * rows))
    )
    shard = pack_weights(w_qkv[0], w_out[0], w_up[0], w_down[0])
    second_shard = pack_weights(w_qkv[1], w_out[1], w_up[1], w_down[1])
    if by_chips:
        early, late_pieces = gather_by_chips(
            [jnp.concatenate([shard[: 4 * rows], norm_rows], axis=0), shard[4 * rows :]]
        )
        early = gather_cores(early, place, "early")
        norm_values = early[:, 4 * rows, : 8 * rows]
    else:
        gathered = lax.all_gather(jnp.concatenate([shard, norm_rows], axis=0), axes, axis=0)
        norm_values = gathered[:, 12 * rows, : 8 * rows]
        early = to_blocks(gathered, rows)
    gains = norm_values.reshape(shards, 2, 4, rows)
    gains = gains.transpose(1, 2, 0, 3).reshape(2, 4, WIDTH).astype(jnp.float32)
    weights_second = to_blocks(lax.all_gather(second_shard, axes, axis=0), rows)

    normed, projected, probs, attended, middle, hidden_in = first_attention(tokens, early, gains[0])
    if by_chips:
        late_pieces = [after(piece, hidden_in) for piece in late_pieces]
        late, late_at = gather_cores(late_pieces, place, "late"), 0
    else:
        late, late_at = early, 1
    hidden, slopes, stream = first_mlp(middle, hidden_in, late, late_at)
    core = place[2:] if by_chips else jnp.zeros((1,), jnp.int32)
    block_out, upstream, sums_second, pair_second = second_block(
        frame_counts, core, stream, cotangent, weights_second, gains[1]
    )
    if by_chips:
        second = scatter_cores(pair_second, place)
        upstream = after(upstream, *second)
        second = swap_chips(second)
    attended_grad, middle_grad, sums_late, pair_first = first_back(
        core, upstream, slopes, middle, early, late, late_at, gains[0], hidden, hidden_in, attended
    )
    if by_chips:
        second[0], *pair_first = lax.optimization_barrier((second[0], *pair_first, *second[1:]))[:3]
        first = scatter_cores(pair_first, place)
        reduced_second = scatter_planes(fold_planes(second, place))
        attended_grad = after(attended_grad, reduced_second, *first)
        first = swap_chips(first)
    projected_grad, pair_last = first_attention_back(core, projected, probs, attended_grad, normed)
    if by_chips:
        first[0], *pair_last = lax.optimization_barrier((first[0], *pair_last, *first[1:]))[:3]
        last = scatter_cores(pair_last, place)
        first[0] = after(first[0], *last)
        last = swap_chips(last)
        first = fold_planes(first, place)
        projected_grad = after(projected_grad, *first)
    tokens_grad, sums_early = first_input_back(
        projected_grad, tokens, middle_grad, early, gains[0]
    )
    if by_chips:
        last[0] = after(last[0], tokens_grad)
        last = fold_planes(last, place)
        reduced_first = scatter_planes(first, *last)
        reduced_last = scatter_planes(last)
    else:
        reduced_second = scatter_whole(pair_second, rows, 8)
        reduced_first = scatter_whole(pair_first, rows, 5)
        reduced_last = scatter_whole(pair_last, rows, 3)

    def columns(packed, first, last):
        return jnp.concatenate(
            [packed[rows * index : rows * index + rows] for index in range(first, last)], axis=1
        )

    reduced_first = (
        columns(reduced_last, 0, 3),
        columns(reduced_first, 4, 5),
        columns(reduced_first, 0, 4),
        reduced_first[5 * rows :],
    )
    reduced_second = (
        columns(reduced_second, 5, 8),
        columns(reduced_second, 4, 5),
        columns(reduced_second, 0, 4),
        reduced_second[8 * rows :],
    )

    norm_parts = jnp.concatenate(
        [jnp.sum(part, axis=1) for part in (sums_early, sums_late, sums_second)]
    )
    norm_parts = norm_parts.reshape(8, shards, rows).transpose(1, 0, 2).reshape(shards, -1)
    stacked = [jnp.stack(pair) for pair in zip(reduced_first, reduced_second)]
    firsts = (first_qkv, first_out, first_up, first_down)
    seconds = (second_qkv, second_out, second_up, second_down)
    updates = [adam_parts(*parts) for parts in zip(stacked, firsts, seconds)]
    directions = [update[2] + DECAY_RATE * master for update, master in zip(updates, masters)]
    local_squares = jnp.stack(
        [
            jnp.stack([jnp.sum(matrix * matrix, axis=(1, 2)) for matrix in group], axis=1)
            for group in (masters, directions)
        ],
        axis=2,
    )
    message = jnp.concatenate(
        [norm_parts, jnp.broadcast_to(local_squares.reshape(1, 16), (shards, 16))], axis=1
    )
    arrived = jnp.sum(lax.all_to_all(message, axes, 0, 0, tiled=True), axis=0)
    matrix_norms = jnp.sqrt(arrived[-16:].reshape(2, 4, 2))
    norm_update = adam_parts(arrived[:-16].reshape(2, 2, 2, rows), first_norm, second_norm)
    updates.append(norm_update)
    updated = [
        masters[index]
        - RATE
        * (matrix_norms[:, index, 0] / matrix_norms[:, index, 1])[:, None, None]
        * directions[index]
        for index in range(4)
    ]
    return (
        block_out,
        tokens_grad,
        *updated,
        norm_params - RATE * norm_update[2],
        *(array.astype(jnp.bfloat16) for array in updated),
        *(update[0] for update in updates),
        *(update[1] for update in updates),
        matrix_norms,
    )


def solution(mesh):
    in_specs = (
        P(("dp", "fsdp"), None),
        P(("dp", "fsdp")),
        P(("dp", "fsdp"), None),
        P(None, ("dp", "fsdp"), None),
        P(None, ("dp", "fsdp"), None),
        P(None, ("dp", "fsdp"), None),
        P(None, ("dp", "fsdp"), None),
        P(None, None, None, ("dp", "fsdp")),
        P(None, ("dp", "fsdp"), None),
        P(None, ("dp", "fsdp"), None),
        P(None, ("dp", "fsdp"), None),
        P(None, ("dp", "fsdp"), None),
        P(None, None, None, ("dp", "fsdp")),
        P(None, ("dp", "fsdp"), None),
        P(None, ("dp", "fsdp"), None),
        P(None, ("dp", "fsdp"), None),
        P(None, ("dp", "fsdp"), None),
        P(None, None, None, ("dp", "fsdp")),
    )
    out_specs = (
        P(("dp", "fsdp"), None),
        P(("dp", "fsdp"), None),
        P(None, ("dp", "fsdp"), None),
        P(None, ("dp", "fsdp"), None),
        P(None, ("dp", "fsdp"), None),
        P(None, ("dp", "fsdp"), None),
        P(None, None, None, ("dp", "fsdp")),
        P(None, ("dp", "fsdp"), None),
        P(None, ("dp", "fsdp"), None),
        P(None, ("dp", "fsdp"), None),
        P(None, ("dp", "fsdp"), None),
        P(None, ("dp", "fsdp"), None),
        P(None, ("dp", "fsdp"), None),
        P(None, ("dp", "fsdp"), None),
        P(None, ("dp", "fsdp"), None),
        P(None, None, None, ("dp", "fsdp")),
        P(None, ("dp", "fsdp"), None),
        P(None, ("dp", "fsdp"), None),
        P(None, ("dp", "fsdp"), None),
        P(None, ("dp", "fsdp"), None),
        P(None, None, None, ("dp", "fsdp")),
        P(),
    )
    return jax.shard_map(body, mesh=mesh, in_specs=in_specs, out_specs=out_specs, check_vma=False)
```

```python
import jax
import jax.numpy as jnp
from jax import lax
from jax.experimental import pallas as pl
from jax.experimental.pallas import tpu as pltpu
from jax.sharding import PartitionSpec as P

HEADS = 8
HEAD_DIM = 64
FRAMES = 17
WIN = 64
STEP = 5
WIDTH = 512
BLOCKS = 32
SLAB = WIDTH // BLOCKS
TILES = 4
TILE = FRAMES * WIN // TILES
SPOTS = WIN // TILES
HALF = TILE // 2
SCALE = HEAD_DIM ** (-0.5)
VMEM_BYTES = 56 * 2**20
COST = pl.CostEstimate(flops=10**8, bytes_accessed=10**5, transcendentals=0)

NORM_EPS = 1e-05
ADAM_EPS = 1e-06
BETA_FIRST = 0.5
BETA_SECOND = 0.5
RATE = 0.25
DECAY_RATE = 0.01
MASKED = -1e30


def row_norm(inputs):
    center = inputs - jnp.mean(inputs, axis=-1, keepdims=True)
    spread = jnp.mean(center * center, axis=-1, keepdims=True)
    scale = lax.rsqrt(spread + NORM_EPS)
    return center * scale, scale


def row_norm_back(grad, gain_row, normal, scale):
    scaled = grad * gain_row
    first = jnp.mean(scaled, axis=-1, keepdims=True)
    second = jnp.mean(scaled * normal, axis=-1, keepdims=True)
    return scale * (scaled - first - normal * second)


def fold_rows(array):
    return jnp.sum(array.reshape(-1, 8, array.shape[-1]), axis=0)


def gelu_pair(upward):
    bell = jnp.exp(-0.5 * upward * upward)
    place = 1.0 / (1.0 + 0.23164189 * jnp.abs(upward))
    tail = 0.5 * 1.061405429
    for factor in (-1.453152027, 1.421413741, -0.284496736, 0.254829592):
        tail = tail * place + 0.5 * factor
    tail = tail * place * bell
    cumulative = jnp.where(upward >= 0.0, 1.0 - tail, tail)
    return upward * cumulative, cumulative + 0.3989422804014327 * upward * bell


def dot_nn(left, right):
    return lax.dot_general(
        left, right, (((1,), (0,)), ((), ())), preferred_element_type=jnp.float32
    )


def dot_nt(left, right):
    return lax.dot_general(
        left, right, (((1,), (1,)), ((), ())), preferred_element_type=jnp.float32
    )


def dot_tn(left, right):
    return lax.dot_general(
        left, right, (((0,), (0,)), ((), ())), preferred_element_type=jnp.float32
    )


def slab(weights, index):
    return weights[:, SLAB * index : SLAB * index + SLAB, :].reshape(WIDTH, WIDTH)


def down_rows(weights, index):
    part = BLOCKS // 4
    return weights[part * index : part * index + part].reshape(WIDTH, WIDTH)


def weight_spec(array, index):
    return pl.BlockSpec(
        (BLOCKS, 4 * SLAB, WIDTH), lambda i: (0, index, 0), pipeline_mode=pl.Buffered(1)
    )


def stack_heads(pair):
    lane = lax.broadcasted_iota(jnp.int32, pair.shape, 1)
    zero = jnp.zeros_like(pair)
    return jnp.concatenate(
        [jnp.where(lane < HEAD_DIM, pair, zero), jnp.where(lane < HEAD_DIM, zero, pair)], axis=0
    )


def merge_heads(stacked):
    rows = stacked.shape[0] // 2
    lane = lax.broadcasted_iota(jnp.int32, (rows, 2 * HEAD_DIM), 1)
    return jnp.where(lane < HEAD_DIM, stacked[:rows], stacked[rows:])


def soft_weights(scores, axis):
    raised = jnp.exp(scores - jnp.max(scores, axis=axis, keepdims=True))
    return raised * (1.0 / jnp.sum(raised, axis=axis, keepdims=True))


def pair_caps():
    row = lax.broadcasted_iota(jnp.int32, (4 * WIN, 2 * WIN), 0)
    column = lax.broadcasted_iota(jnp.int32, (4 * WIN, 2 * WIN), 1)
    return jnp.where(row // WIN % 2 == column // WIN, 3.0e38, MASKED)


def frame_pairs():
    return [min(2 * index, FRAMES - 2) for index in range((FRAMES + 1) // 2)]


def outer_store(core, left, right, mine, other, block, row, rows):
    first = core[0] == 0
    count = 128 // rows
    for half in range(2):
        part = dot_tn(left[:, 256 * half : 256 * half + 256], right).astype(jnp.bfloat16)
        part = part.reshape(count, 2, rows, WIDTH)
        even, odd = part[:, 0], part[:, 1]
        place = pl.ds(block + count * half, count), pl.ds(row, rows)
        mine[place] = jnp.where(first, even, odd)
        other[place] = jnp.where(first, odd, even)


def slab_row(step, first):
    return pl.multiple_of((step - first) * SLAB, SLAB)


def grad_specs(rows):
    return [pl.BlockSpec((BLOCKS // 2, rows, WIDTH), lambda i: (0, 0, 0))] * 2


def grad_shapes(rows):
    return [jax.ShapeDtypeStruct((BLOCKS // 2, rows, WIDTH), jnp.bfloat16)] * 2


def part_of(step, first):
    return pl.ds(pl.multiple_of((step - first) * WIDTH, WIDTH), WIDTH)


def first_attention_kernel(
    tokens, weights, gains, normed_out, projected_out, probs, attended, middle_out, hidden_in_out,
    projected,
):
    step = pl.program_id(0)

    @pl.when(step < TILES)
    def _():
        normal, _ = row_norm(tokens[...].astype(jnp.float32))
        normed = (normal * gains[0:1, :] + gains[1:2, :]).astype(jnp.bfloat16)
        normed_out[...] = normed
        rows = pl.ds(pl.multiple_of(step * TILE, TILE), TILE)
        for index in range(3):
            part = dot_nn(normed, slab(weights, index)).astype(jnp.bfloat16)
            projected[rows, WIDTH * index : WIDTH * index + WIDTH] = part
            projected_out[:, WIDTH * index : WIDTH * index + WIDTH] = part

    @pl.when(step == TILES)
    def _():
        caps = pair_caps()
        for index, frame in enumerate(frame_pairs()):
            rows = slice(WIN * frame, WIN * frame + 2 * WIN)
            lanes = [slice(128 * pair, 128 * pair + 128) for pair in range(HEADS // 2)]
            queries = [stack_heads(projected[rows, lane] * SCALE) for lane in lanes]
            keys = [projected[rows, WIDTH + 128 * pair : WIDTH + 128 * pair + 128] for pair in range(4)]
            scores = [jnp.minimum(dot_nt(*both), caps) for both in zip(queries, keys)]
            shares = [soft_weights(score, -1).astype(jnp.bfloat16) for score in scores]
            for pair, share in enumerate(shares):
                probs[index, pair] = share
                values = projected[rows, 2 * WIDTH + 128 * pair : 2 * WIDTH + 128 * pair + 128]
                attended[rows, lanes[pair]] = merge_heads(dot_nn(share, values)).astype(jnp.bfloat16)

    @pl.when(step > TILES)
    def _():
        rows = pl.ds(pl.multiple_of((step - TILES - 1) * TILE, TILE), TILE)
        middle = tokens[...].astype(jnp.float32) + dot_nn(attended[rows, :], slab(weights, 3))
        middle_out[...] = middle
        normal, _ = row_norm(middle)
        hidden_in_out[...] = (normal * gains[2:3, :] + gains[3:4, :]).astype(jnp.bfloat16)


def first_attention(tokens, weights, gains):
    count = tokens.shape[0]

    def early(width):
        return pl.BlockSpec((TILE, width), lambda i: (jnp.minimum(i, TILES - 1), 0))

    def late(width):
        return pl.BlockSpec((TILE, width), lambda i: (jnp.maximum(i - TILES - 1, 0), 0))

    def whole_out(*shape):
        return pl.BlockSpec(shape, lambda i: (0,) * len(shape))

    def out(width, kind):
        return jax.ShapeDtypeStruct((count, width), kind)

    return pl.pallas_call(
        first_attention_kernel,
        grid=(2 * TILES + 1,),
        in_specs=[
            pl.BlockSpec(
                (TILE, WIDTH), lambda i: (jnp.where(i < TILES, i, jnp.maximum(i - TILES - 1, 0)), 0)
            ),
            weight_spec(weights, 0),
            whole_out(4, WIDTH),
        ],
        out_specs=[
            early(WIDTH),
            early(3 * WIDTH),
            whole_out((FRAMES + 1) // 2, HEADS // 2, 4 * WIN, 2 * WIN),
            whole_out(count, WIDTH),
            late(WIDTH),
            late(WIDTH),
        ],
        out_shape=[
            out(WIDTH, jnp.bfloat16),
            out(3 * WIDTH, jnp.bfloat16),
            jax.ShapeDtypeStruct(((FRAMES + 1) // 2, HEADS // 2, 4 * WIN, 2 * WIN), jnp.bfloat16),
            out(WIDTH, jnp.bfloat16),
            out(WIDTH, jnp.float32),
            out(WIDTH, jnp.bfloat16),
        ],
        scratch_shapes=[pltpu.VMEM((count, 3 * WIDTH), jnp.bfloat16)],
        compiler_params=pltpu.CompilerParams(vmem_limit_bytes=VMEM_BYTES),
        cost_estimate=COST,
        name="first_attention",
    )(tokens, weights, gains)


def first_mlp_kernel(middle, hidden_in, weights_up, weights_down, hidden_out, slope_out, result_out):
    result = middle[...]
    upward = dot_nn(hidden_in[...], slab(weights_up, 0))
    for index in range(4):
        columns = slice(WIDTH * index, WIDTH * index + WIDTH)
        following = dot_nn(hidden_in[...], slab(weights_up, index + 1)) if index < 3 else None
        value, slope = gelu_pair(upward)
        hidden = value.astype(jnp.bfloat16)
        hidden_out[:, columns] = hidden
        slope_out[:, columns] = slope.astype(jnp.bfloat16)
        result = result + dot_nn(hidden, down_rows(weights_down, index))
        upward = following
    result_out[...] = result


def first_mlp(middle, hidden_in, weights, weights_at):
    count = middle.shape[0]

    def tile(width):
        return pl.BlockSpec((TILE, width), lambda i: (i, 0))

    return pl.pallas_call(
        first_mlp_kernel,
        grid=(TILES,),
        in_specs=[
            tile(WIDTH),
            tile(WIDTH),
            weight_spec(weights, weights_at),
            weight_spec(weights, weights_at + 1),
        ],
        out_specs=[tile(4 * WIDTH), tile(4 * WIDTH), tile(WIDTH)],
        out_shape=[
            jax.ShapeDtypeStruct((count, 4 * WIDTH), jnp.bfloat16),
            jax.ShapeDtypeStruct((count, 4 * WIDTH), jnp.bfloat16),
            jax.ShapeDtypeStruct((count, WIDTH), jnp.float32),
        ],
        compiler_params=pltpu.CompilerParams(vmem_limit_bytes=VMEM_BYTES),
        cost_estimate=COST,
        name="first_mlp",
    )(middle, hidden_in, weights, weights)


def second_kernel(
    frame_count, core, inputs, cotangent, weights, weights_up, weights_down, gains, result_out,
    grad_out, sums, mine, other,
    caps, query_rows, key_rows, value_rows, probs, slopes, normed, projected_grads, attended,
    branch_grads, hidden_in, up_grads, hidden, out_grads,
):
    step = pl.program_id(0)

    @pl.when(step == 0)
    def _():
        row = lax.broadcasted_iota(jnp.int32, caps.shape, 0)
        column = lax.broadcasted_iota(jnp.int32, caps.shape, 1) % HALF
        soon, late = row // 8, column // 8
        video = (late < frame_count[0]) & (soon < frame_count[0])
        allowed = (row % 8 == column % 8) & ((soon == late) | ((soon < late) & video))
        caps[...] = jnp.where(allowed, 3.0e38, MASKED)
        sums[...] = jnp.zeros_like(sums)

    def flat(ref):
        array = ref[...].astype(jnp.float32)
        return jnp.concatenate(
            [array[:, :8].reshape(HALF, WIDTH), array[:, 8:].reshape(HALF, WIDTH)], axis=0
        )

    def keep(ref, value):
        halves = [value[HALF * half : HALF * half + HALF] for half in range(2)]
        ref[...] = jnp.concatenate(
            [half.reshape(FRAMES, 8, WIDTH) for half in halves], axis=1
        ).astype(ref.dtype)

    @pl.when(step < TILES)
    def _():
        rows = pl.ds(pl.multiple_of(step * TILE, TILE), TILE)
        inside = lax.broadcasted_iota(jnp.int32, (TILE, 1), 0) % HALF // 8 < frame_count[0]
        gate = jnp.where(inside, 1.0, 0.0)
        stream = flat(inputs)
        normal_first, scale_first = row_norm(stream)
        normed_tile = (normal_first * gains[0:1, :] + gains[1:2, :]).astype(jnp.bfloat16)
        normed[rows, :] = normed_tile
        for index, ref in enumerate((query_rows, key_rows, value_rows)):
            part = dot_nn(normed_tile, slab(weights, index))
            for half in range(2):
                piece = part[HALF * half : HALF * half + HALF]
                if index == 0:
                    for pair in range(HEADS // 2):
                        stacked = stack_heads(piece[:, 128 * pair : 128 * pair + 128] * SCALE)
                        ref[half, pair] = stacked.astype(jnp.bfloat16)
                else:
                    ref[half] = piece.astype(jnp.bfloat16)
        units = [
            (half, pair, slice(128 * pair, 128 * pair + 128))
            for half in range(2)
            for pair in range(HEADS // 2)
        ]
        scores = [
            dot_nt(key_rows[half, :, lanes], query_rows[half, pair]) for half, pair, lanes in units
        ]
        shares = [
            soft_weights(jnp.minimum(score, caps[...]), 0).astype(jnp.bfloat16) for score in scores
        ]
        for share, (half, pair, _) in zip(shares, units):
            probs[half, pair] = share
        parts = [
            merge_heads(dot_tn(share, value_rows[half, :, lanes]))
            for share, (half, _, lanes) in zip(shares, units)
        ]
        halves = [jnp.concatenate(parts[4 * half : 4 * half + 4], axis=1) for half in range(2)]
        attended_tile = jnp.concatenate(halves, axis=0).astype(jnp.bfloat16)
        attended[rows, :] = attended_tile
        middle = stream + gate * dot_nn(attended_tile, slab(weights, 3))
        normal_second, scale_second = row_norm(middle)
        hidden_in_tile = (normal_second * gains[2:3, :] + gains[3:4, :]).astype(jnp.bfloat16)
        hidden_in[rows, :] = hidden_in_tile
        result = middle
        upward = dot_nn(hidden_in_tile, slab(weights_up, 0))
        for index in range(4):
            columns = slice(WIDTH * index, WIDTH * index + WIDTH)
            following = dot_nn(hidden_in_tile, slab(weights_up, index + 1)) if index < 3 else None
            value, slope = gelu_pair(upward)
            hidden_tile = value.astype(jnp.bfloat16)
            hidden[rows, columns] = hidden_tile
            slopes[:, columns] = slope
            result = result + dot_nn(hidden_tile, down_rows(weights_down, index))
            upward = following
        keep(result_out, result)

        upstream = flat(cotangent)
        out_grad = upstream.astype(jnp.bfloat16)
        out_grads[rows, :] = out_grad
        hidden_in_grad = jnp.zeros((TILE, WIDTH), jnp.float32)
        for index in range(4):
            columns = slice(WIDTH * index, WIDTH * index + WIDTH)
            up_grad = (dot_nt(out_grad, down_rows(weights_down, index)) * slopes[:, columns]).astype(
                jnp.bfloat16
            )
            up_grads[rows, columns] = up_grad
            hidden_in_grad = hidden_in_grad + dot_nt(up_grad, slab(weights_up, index))
        sums[2] += fold_rows(hidden_in_grad * normal_second)
        sums[3] += fold_rows(hidden_in_grad)
        middle_grad = upstream + row_norm_back(
            hidden_in_grad, gains[2:3, :], normal_second, scale_second
        )
        branch_grad = (middle_grad * gate).astype(jnp.bfloat16)
        branch_grads[rows, :] = branch_grad
        attended_grad = dot_nt(branch_grad, slab(weights, 3))
        grads = [
            stack_heads(attended_grad[HALF * half : HALF * half + HALF, lanes]).astype(jnp.bfloat16)
            for half, _, lanes in units
        ]
        share_grads = [
            dot_nt(value_rows[half, :, lanes], grad) for grad, (half, _, lanes) in zip(grads, units)
        ]
        value_grads = [
            dot_nn(probs[half, pair], grad) for grad, (half, pair, _) in zip(grads, units)
        ]
        score_grads = []
        for share_grad, (half, pair, _) in zip(share_grads, units):
            share = probs[half, pair].astype(jnp.float32)
            total = jnp.sum(share_grad * share, axis=0, keepdims=True)
            score_grads.append((share * (share_grad - total)).astype(jnp.bfloat16))
        query_grads = [
            dot_tn(grad, key_rows[half, :, lanes])
            for grad, (half, _, lanes) in zip(score_grads, units)
        ]
        key_grads = [
            dot_nn(grad, query_rows[half, pair]) for grad, (half, pair, _) in zip(score_grads, units)
        ]
        query_grads = [merge_heads(grad) * SCALE for grad in query_grads]
        halves = [
            jnp.concatenate(
                [
                    part
                    for parts in (query_grads, key_grads, value_grads)
                    for part in parts[4 * half : 4 * half + 4]
                ],
                axis=1,
            )
            for half in range(2)
        ]
        projected_grad = jnp.concatenate(halves, axis=0).astype(jnp.bfloat16)
        projected_grads[rows, :] = projected_grad
        normed_grad = jnp.zeros((TILE, WIDTH), jnp.float32)
        for index in range(3):
            part = projected_grad[:, WIDTH * index : WIDTH * index + WIDTH]
            normed_grad = normed_grad + dot_nt(part, slab(weights, index))
        sums[0] += fold_rows(normed_grad * normal_first)
        sums[1] += fold_rows(normed_grad)
        keep(
            grad_out,
            middle_grad + row_norm_back(normed_grad, gains[0:1, :], normal_first, scale_first),
        )

    @pl.when((step >= TILES) & (step < TILES + 4))
    def _():
        right = up_grads[:, part_of(step, TILES)]
        outer_store(core, hidden_in, right, mine, other, 0, slab_row(step, TILES), SLAB)

    @pl.when((step >= TILES + 4) & (step < TILES + 7))
    def _():
        right = projected_grads[:, part_of(step, TILES + 4)]
        outer_store(core, normed, right, mine, other, 0, slab_row(step, TILES - 1), SLAB)

    @pl.when((step >= TILES + 7) & (step < TILES + 11))
    def _():
        left = hidden[:, part_of(step, TILES + 7)]
        block = (step - TILES - 7) * 4
        outer_store(core, left, out_grads[...], mine, other, block, 8 * SLAB, 4 * SLAB)

    @pl.when(step == TILES + 11)
    def _():
        outer_store(core, attended, branch_grads[...], mine, other, 0, 4 * SLAB, SLAB)


def second_block(frame_counts, core, inputs, cotangent, weights, gains):
    def tile(width):
        return pl.BlockSpec((FRAMES, SPOTS, width), lambda i: (0, jnp.minimum(i, TILES - 1), 0))

    def held(width):
        return pltpu.VMEM((FRAMES * WIN, width * WIDTH), jnp.bfloat16)

    whole = (FRAMES, WIN, WIDTH)
    outs = pl.pallas_call(
        second_kernel,
        grid=(TILES + 12,),
        in_specs=[
            pl.BlockSpec(memory_space=pltpu.SMEM),
            pl.BlockSpec(memory_space=pltpu.SMEM),
            tile(WIDTH),
            tile(WIDTH),
            weight_spec(weights, 0),
            weight_spec(weights, 1),
            weight_spec(weights, 2),
            pl.BlockSpec((4, WIDTH), lambda i: (0, 0)),
        ],
        out_specs=[
            tile(WIDTH),
            tile(WIDTH),
            pl.BlockSpec((4, 8, WIDTH), lambda i: (0, 0, 0)),
            *grad_specs(12 * SLAB),
        ],
        out_shape=[
            jax.ShapeDtypeStruct(whole, jnp.bfloat16),
            jax.ShapeDtypeStruct(whole, jnp.float32),
            jax.ShapeDtypeStruct((4, 8, WIDTH), jnp.float32),
            *grad_shapes(12 * SLAB),
        ],
        scratch_shapes=[
            pltpu.VMEM((HALF, 2 * HALF), jnp.float32),
            pltpu.VMEM((2, HEADS // 2, 2 * HALF, 128), jnp.bfloat16),
            pltpu.VMEM((2, HALF, WIDTH), jnp.bfloat16),
            pltpu.VMEM((2, HALF, WIDTH), jnp.bfloat16),
            pltpu.VMEM((2, HEADS // 2, HALF, 2 * HALF), jnp.bfloat16),
            pltpu.VMEM((TILE, 4 * WIDTH), jnp.float32),
            held(1),
            held(3),
            held(1),
            held(1),
            held(1),
            held(4),
            held(4),
            held(1),
        ],
        compiler_params=pltpu.CompilerParams(vmem_limit_bytes=VMEM_BYTES),
        cost_estimate=COST,
        name="second_block",
    )(
        frame_counts,
        core,
        inputs.reshape(whole),
        cotangent.reshape(whole),
        weights,
        weights,
        weights,
        gains,
    )
    return (
        outs[0].reshape(-1, WIDTH),
        outs[1].reshape(-1, WIDTH),
        outs[2],
        tuple(outs[3:]),
    )


def first_back_kernel(
    core, upstream, slopes, middle, weights, weights_up, weights_down, gains, hidden, hidden_in,
    attended, queries_in, keys_in, values_in, probs, normed, middle_grad_out, sums, projected_grad_out,
    mine, other, up_grads, out_grads, branch_grads, attended_grads, projected_grads,
):
    step = pl.program_id(0)
    heads_at = TILES + 9
    last_at = heads_at + HEADS // 2

    @pl.when(step == 0)
    def _():
        sums[...] = jnp.zeros_like(sums)

    @pl.when(step < TILES)
    def _():
        rows = pl.ds(pl.multiple_of(step * TILE, TILE), TILE)
        out_grad = upstream[...].astype(jnp.bfloat16)
        out_grads[rows, :] = out_grad
        hidden_in_grad = jnp.zeros((TILE, WIDTH), jnp.float32)
        for index in range(4):
            columns = slice(WIDTH * index, WIDTH * index + WIDTH)
            up_grad = (dot_nt(out_grad, down_rows(weights_down, index)) * slopes[:, columns]).astype(
                jnp.bfloat16
            )
            up_grads[rows, columns] = up_grad
            hidden_in_grad = hidden_in_grad + dot_nt(up_grad, slab(weights_up, index))
        normal, scale = row_norm(middle[...])
        sums[0] += fold_rows(hidden_in_grad * normal)
        sums[1] += fold_rows(hidden_in_grad)
        middle_grad = upstream[...] + row_norm_back(hidden_in_grad, gains[2:3, :], normal, scale)
        middle_grad_out[...] = middle_grad
        branch_grad = middle_grad.astype(jnp.bfloat16)
        branch_grads[rows, :] = branch_grad
        attended_grad = dot_nt(branch_grad, slab(weights, 3)).astype(jnp.bfloat16)
        for pair in range(HEADS // 2):
            attended_grads[pair, rows, :] = attended_grad[:, 128 * pair : 128 * pair + 128]

    @pl.when((step >= TILES) & (step < TILES + 4))
    def _():
        right = up_grads[:, part_of(step, TILES)]
        outer_store(core, hidden_in, right, mine, other, 0, slab_row(step, TILES), SLAB)

    @pl.when((step >= TILES + 4) & (step < TILES + 8))
    def _():
        block = (step - TILES - 4) * 4
        outer_store(core, hidden, out_grads[...], mine, other, block, 8 * SLAB, 4 * SLAB)

    @pl.when(step == TILES + 8)
    def _():
        outer_store(core, attended, branch_grads[...], mine, other, 0, 4 * SLAB, SLAB)

    @pl.when((step >= heads_at) & (step < last_at))
    def _():
        pair = step - heads_at
        frames = list(enumerate(frame_pairs()))
        rows = [slice(WIN * frame, WIN * frame + 2 * WIN) for _, frame in frames]
        grads = [stack_heads(attended_grads[pair, row, :]) for row in rows]
        share_grads = [dot_nt(grad, values_in[row, :]) for grad, row in zip(grads, rows)]
        shares = [probs[index, 0] for index, _ in frames]
        value_grads = [dot_tn(share, grad) for share, grad in zip(shares, grads)]
        score_grads = []
        for share, share_grad in zip(shares, share_grads):
            share = share.astype(jnp.float32)
            total = jnp.sum(share_grad * share, axis=-1, keepdims=True)
            score_grads.append((share * (share_grad - total)).astype(jnp.bfloat16))
        query_grads = [dot_nn(grad, keys_in[row, :]) for grad, row in zip(score_grads, rows)]
        key_grads = [
            dot_tn(grad, stack_heads(queries_in[row, :] * SCALE))
            for grad, row in zip(score_grads, rows)
        ]
        query_grads = [merge_heads(grad) * SCALE for grad in query_grads]
        for index, parts in enumerate((query_grads, key_grads, value_grads)):
            lanes = pl.ds(pl.multiple_of(pair * 128 + WIDTH * index, 128), 128)
            for row, part in zip(rows, parts):
                projected_grads[row, lanes] = part.astype(jnp.bfloat16)

    @pl.when(step >= last_at)
    def _():
        right = projected_grads[:, part_of(step, last_at)]
        projected_grad_out[...] = right
        outer_store(core, normed, right, mine, other, 0, slab_row(step, last_at - 5), SLAB)


def first_back(
    core, upstream, slopes, middle, weights, late_weights, late_at, gains, hidden, hidden_in, attended,
    projected, probs, normed,
):
    count = upstream.shape[0]
    pairs = HEADS // 2
    heads_at = TILES + 9
    last_at = heads_at + pairs

    def tile(width):
        return pl.BlockSpec((TILE, width), lambda i: (jnp.minimum(i, TILES - 1), 0))

    def whole(*shape):
        return pl.BlockSpec(shape, lambda i: (0,) * len(shape), pipeline_mode=pl.Buffered(1))

    def pair_of(step):
        return jnp.clip(step - heads_at, 0, pairs - 1)

    def lanes(first):
        return pl.BlockSpec((count, 128), lambda i: (0, first + pair_of(i)))

    def held(width):
        return pltpu.VMEM((count, width * WIDTH), jnp.bfloat16)

    outs = pl.pallas_call(
        first_back_kernel,
        grid=(last_at + 3,),
        in_specs=[
            pl.BlockSpec(memory_space=pltpu.SMEM),
            tile(WIDTH),
            tile(4 * WIDTH),
            tile(WIDTH),
            weight_spec(weights, 0),
            weight_spec(late_weights, late_at),
            weight_spec(late_weights, late_at + 1),
            whole(4, WIDTH),
            pl.BlockSpec((count, WIDTH), lambda i: (0, jnp.clip(i - TILES - 4, 0, 3))),
            whole(count, WIDTH),
            whole(count, WIDTH),
            lanes(0),
            lanes(pairs),
            lanes(2 * pairs),
            pl.BlockSpec(
                ((FRAMES + 1) // 2, 1, 4 * WIN, 2 * WIN), lambda i: (0, pair_of(i), 0, 0)
            ),
            whole(count, WIDTH),
        ],
        out_specs=[
            tile(WIDTH),
            pl.BlockSpec((2, 8, WIDTH), lambda i: (0, 0, 0)),
            pl.BlockSpec((count, WIDTH), lambda i: (0, jnp.clip(i - last_at, 0, 2))),
            *grad_specs(12 * SLAB),
        ],
        out_shape=[
            jax.ShapeDtypeStruct((count, WIDTH), jnp.float32),
            jax.ShapeDtypeStruct((2, 8, WIDTH), jnp.float32),
            jax.ShapeDtypeStruct((count, 3 * WIDTH), jnp.bfloat16),
            *grad_shapes(12 * SLAB),
        ],
        scratch_shapes=[
            held(4),
            held(1),
            held(1),
            pltpu.VMEM((pairs, count, 128), jnp.bfloat16),
            held(3),
        ],
        compiler_params=pltpu.CompilerParams(vmem_limit_bytes=VMEM_BYTES),
        cost_estimate=COST,
        name="first_back",
    )(
        core, upstream, slopes, middle, weights, late_weights, late_weights, gains, hidden, hidden_in,
        attended, projected, projected, projected, probs, normed,
    )
    return (*outs[:3], tuple(outs[3:]))


def first_input_back_kernel(projected_grad, tokens, middle_grad, weights, gains, grad_out, sums):
    @pl.when(pl.program_id(0) == 0)
    def _():
        sums[...] = jnp.zeros_like(sums)

    normed_grad = jnp.zeros((TILE, WIDTH), jnp.float32)
    for index in range(3):
        part = projected_grad[:, WIDTH * index : WIDTH * index + WIDTH]
        normed_grad = normed_grad + dot_nt(part, slab(weights, index))
    normal, scale = row_norm(tokens[...].astype(jnp.float32))
    sums[0] += fold_rows(normed_grad * normal)
    sums[1] += fold_rows(normed_grad)
    grad_out[...] = middle_grad[...] + row_norm_back(normed_grad, gains[0:1, :], normal, scale)


def first_input_back(projected_grad, tokens, middle_grad, weights, gains):
    count = tokens.shape[0]

    def tile(width):
        return pl.BlockSpec((TILE, width), lambda i: (i, 0))

    def whole(*shape):
        return pl.BlockSpec(shape, lambda i: (0,) * len(shape), pipeline_mode=pl.Buffered(1))

    return pl.pallas_call(
        first_input_back_kernel,
        grid=(TILES,),
        in_specs=[
            tile(3 * WIDTH),
            tile(WIDTH),
            tile(WIDTH),
            whole(BLOCKS, 3 * SLAB, WIDTH),
            whole(4, WIDTH),
        ],
        out_specs=[tile(WIDTH), pl.BlockSpec((2, 8, WIDTH), lambda i: (0, 0, 0))],
        out_shape=[
            jax.ShapeDtypeStruct((count, WIDTH), jnp.float32),
            jax.ShapeDtypeStruct((2, 8, WIDTH), jnp.float32),
        ],
        compiler_params=pltpu.CompilerParams(vmem_limit_bytes=VMEM_BYTES),
        cost_estimate=COST,
        name="first_input_back",
    )(projected_grad, tokens, middle_grad, weights, gains)


def arrange_kernel(place, *refs):
    ins, out = refs[:-1], refs[-1]
    across, plane, core = place[0], place[1], place[2]
    for index, ref in enumerate(ins):
        column = (across ^ (index % 4)) * 8 + (core ^ (index // 4))
        for way in range(4):
            out[column + (plane ^ way) * 2] = ref[way]


def arrange(place, pieces, name):
    rows = pieces[0].shape[1]
    return pl.pallas_call(
        arrange_kernel,
        in_specs=[pl.BlockSpec(memory_space=pltpu.SMEM)]
        + [pl.BlockSpec(memory_space=pltpu.VMEM)] * 8,
        out_shape=jax.ShapeDtypeStruct((BLOCKS, rows, WIDTH), jnp.bfloat16),
        compiler_params=pltpu.CompilerParams(vmem_limit_bytes=VMEM_BYTES),
        cost_estimate=COST,
        name=name,
    )(place, *pieces)


def pack_kernel(w_qkv, w_out, w_up, w_down, norm, early, late, second):
    def narrow(array):
        return array.astype(jnp.bfloat16)

    for block, (start, rest) in enumerate(((early, late), (second, second))):
        for index in range(3):
            columns = slice(WIDTH * index, WIDTH * index + WIDTH)
            start[SLAB * index : SLAB * index + SLAB, :] = narrow(w_qkv[block, :, columns])
        start[3 * SLAB : 4 * SLAB, :] = narrow(w_out[block])
        first = 4 * SLAB * block
        for index in range(4):
            columns = slice(WIDTH * index, WIDTH * index + WIDTH)
            row = first + SLAB * index
            rest[row : row + SLAB, :] = narrow(w_up[block, :, columns])
        rest[first + 4 * SLAB : first + 8 * SLAB, :] = narrow(w_down[block])
    early[4 * SLAB :, :] = narrow(norm[...])


def pack_all(w_qkv, w_out, w_up, w_down, norm_rows):
    return pl.pallas_call(
        pack_kernel,
        out_shape=[
            jax.ShapeDtypeStruct((rows, WIDTH), jnp.bfloat16)
            for rows in (5 * SLAB, 8 * SLAB, 12 * SLAB)
        ],
        compiler_params=pltpu.CompilerParams(vmem_limit_bytes=VMEM_BYTES),
        cost_estimate=COST,
        name="pack",
    )(w_qkv, w_out, w_up, w_down, norm_rows)


def adam_parts(gradient, first_moment, second_moment):
    first_next = BETA_FIRST * first_moment + (1.0 - BETA_FIRST) * gradient
    second_next = BETA_SECOND * second_moment + (1.0 - BETA_SECOND) * gradient * gradient
    direction = (
        first_next
        / (1.0 - BETA_FIRST**STEP)
        / (jnp.sqrt(second_next / (1.0 - BETA_SECOND**STEP)) + ADAM_EPS)
    )
    return (first_next, second_next, direction)


def pack_weights(part_qkv, part_out, part_up, part_down):
    return jnp.concatenate(
        [part_qkv[:, WIDTH * i : WIDTH * i + WIDTH] for i in range(3)]
        + [part_out]
        + [part_up[:, WIDTH * i : WIDTH * i + WIDTH] for i in range(4)]
        + [part_down],
        axis=0,
    ).astype(jnp.bfloat16)


def to_blocks(packed, rows):
    if rows == SLAB:
        return packed
    packed = packed[:, : 12 * rows]
    slabs = packed[:, : 8 * rows].reshape(BLOCKS, -1, 8, rows, WIDTH).transpose(0, 2, 1, 3, 4)
    return jnp.concatenate(
        [
            slabs.reshape(BLOCKS, 8 * SLAB, WIDTH),
            packed[:, 8 * rows :].reshape(BLOCKS, 4 * SLAB, WIDTH),
        ],
        axis=1,
    )


def from_blocks(grads, rows, narrow):
    if rows == SLAB:
        return grads
    slabs = grads[:, : narrow * SLAB].reshape(BLOCKS, narrow, -1, rows, WIDTH)
    slabs = slabs.transpose(0, 2, 1, 3, 4).reshape(-1, narrow * rows, WIDTH)
    if grads.shape[1] == narrow * SLAB:
        return slabs
    wide = grads[:, narrow * SLAB :].reshape(slabs.shape[0], -1, WIDTH)
    return jnp.concatenate([slabs, wide], axis=1)


def swap(array, mask):
    count = lax.axis_size("dp") * lax.axis_size("fsdp")
    return lax.ppermute(array, ("dp", "fsdp"), [(device, device ^ mask) for device in range(count)])


def after(value, *others):
    return lax.optimization_barrier((value, *others))[0]


def gather_by_chips(shards):
    results = []
    steps = [(), ()]
    for shard in shards:
        shard = after(shard, *steps[0])
        steps[0] = [swap(shard, 2 * way) for way in (1, 2, 3)]
        pieces = after(jnp.stack([shard] + steps[0]), *steps[1])
        steps[1] = [swap(pieces, 8 * way) for way in (1, 2, 3)]
        results.append([pieces] + steps[1])
    return results


def gather_cores(pieces, place, name):
    return arrange(place, pieces + [swap(piece, 1) for piece in pieces], "arrange_" + name)


def sum_at(arrays, index):
    total = sum(
        lax.dynamic_index_in_dim(array, index, 0, keepdims=False).astype(jnp.float32)
        for array in arrays
    )
    return total.astype(jnp.bfloat16)


def scatter_cores(pair, place):
    both = [array.reshape(4, 4, -1, WIDTH) for array in (pair[0], swap(pair[1], 1))]
    return [sum_at(both, place[0] ^ way) for way in (0, 3, 1, 2)]


def swap_chips(pieces):
    return [pieces[0]] + [swap(piece, 8 * way) for piece, way in zip(pieces[1:], (3, 1, 2))]


def fold_planes(pieces, place):
    return [sum_at(pieces, place[1] ^ way) for way in (0, 3, 2, 1)]


def scatter_planes(pieces, *others):
    pieces = [pieces[0]] + [swap(piece, 2 * way) for piece, way in zip(pieces[1:], (3, 2, 1))]
    pieces[0] = after(pieces[0], *others)
    return sum(piece.astype(jnp.float32) for piece in pieces)


def scatter_whole(pair, rows, narrow):
    grads = jnp.stack(pair, axis=1).reshape(BLOCKS, -1, WIDTH)
    summed = lax.psum_scatter(
        from_blocks(grads, rows, narrow), ("dp", "fsdp"), scatter_dimension=0, tiled=False
    )
    return summed.astype(jnp.float32)


def body(
    tokens,
    frame_counts,
    cotangent,
    w_qkv,
    w_out,
    w_up,
    w_down,
    norm_params,
    first_qkv,
    first_out,
    first_up,
    first_down,
    first_norm,
    second_qkv,
    second_out,
    second_up,
    second_down,
    second_norm,
):
    masters = (w_qkv, w_out, w_up, w_down)
    axes = ("dp", "fsdp")
    shards = lax.axis_size("dp") * lax.axis_size("fsdp")
    rows = w_out.shape[1]
    by_chips = (lax.axis_size("dp"), lax.axis_size("fsdp")) == (4, 8)
    fsdp = lax.axis_index("fsdp")
    place = jnp.stack([lax.axis_index("dp"), fsdp // 2, fsdp % 2]).astype(jnp.int32)
    norm_rows = jnp.pad(
        norm_params.reshape(1, -1), ((0, rows - 1), (0, WIDTH - 8 * rows))
    )
    if by_chips:
        *shard, second_shard = pack_all(w_qkv, w_out, w_up, w_down, norm_rows)
        early, late_pieces = gather_by_chips(shard)
        early = gather_cores(early, place, "early")
        norm_values = early[:, 4 * rows, : 8 * rows]
    else:
        shard = pack_weights(w_qkv[0], w_out[0], w_up[0], w_down[0])
        second_shard = pack_weights(w_qkv[1], w_out[1], w_up[1], w_down[1])
        shard = jnp.concatenate([shard, norm_rows.astype(jnp.bfloat16)], axis=0)
        gathered = lax.all_gather(shard, axes, axis=0)
        norm_values = gathered[:, 12 * rows, : 8 * rows]
        early = to_blocks(gathered, rows)
    gains = norm_values.reshape(shards, 2, 4, rows)
    gains = gains.transpose(1, 2, 0, 3).reshape(2, 4, WIDTH).astype(jnp.float32)
    weights_second = to_blocks(lax.all_gather(second_shard, axes, axis=0), rows)

    normed, projected, probs, attended, middle, hidden_in = first_attention(tokens, early, gains[0])
    if by_chips:
        late_pieces = [after(piece, hidden_in) for piece in late_pieces]
        late, late_at = gather_cores(late_pieces, place, "late"), 0
    else:
        late, late_at = early, 1
    hidden, slopes, stream = first_mlp(middle, hidden_in, late, late_at)
    core = place[2:] if by_chips else jnp.zeros((1,), jnp.int32)
    block_out, upstream, sums_second, pair_second = second_block(
        frame_counts, core, stream, cotangent, weights_second, gains[1]
    )
    if by_chips:
        second = scatter_cores(pair_second, place)
        upstream = after(upstream, *second)
        second = swap_chips(second)
    middle_grad, sums_late, projected_grad, pair_first = first_back(
        core, upstream, slopes, middle, early, late, late_at, gains[0], hidden, hidden_in, attended,
        projected, probs, normed,
    )
    if by_chips:
        second[0], *pair_first = lax.optimization_barrier((second[0], *pair_first, *second[1:]))[:3]
        first = scatter_cores(pair_first, place)
        projected_grad = after(projected_grad, *first)
        first = swap_chips(first)
        reduced_second = scatter_planes(fold_planes(second, place))
    tokens_grad, sums_early = first_input_back(
        projected_grad, tokens, middle_grad, early, gains[0]
    )
    if by_chips:
        first[0] = after(first[0], tokens_grad)
        reduced_first = scatter_planes(fold_planes(first, place))
    else:
        reduced_second = scatter_whole(pair_second, rows, 8)
        reduced_first = scatter_whole(pair_first, rows, 8)

    def columns(packed, first, last):
        return jnp.concatenate(
            [packed[rows * index : rows * index + rows] for index in range(first, last)], axis=1
        )

    reduced_first, reduced_second = (
        (columns(both, 5, 8), columns(both, 4, 5), columns(both, 0, 4), both[8 * rows :])
        for both in (reduced_first, reduced_second)
    )

    norm_parts = jnp.concatenate(
        [jnp.sum(part, axis=1) for part in (sums_early, sums_late, sums_second)]
    )
    norm_parts = norm_parts.reshape(8, shards, rows).transpose(1, 0, 2).reshape(shards, -1)
    stacked = [jnp.stack(pair) for pair in zip(reduced_first, reduced_second)]
    firsts = (first_qkv, first_out, first_up, first_down)
    seconds = (second_qkv, second_out, second_up, second_down)
    updates = [adam_parts(*parts) for parts in zip(stacked, firsts, seconds)]
    directions = [update[2] + DECAY_RATE * master for update, master in zip(updates, masters)]
    local_squares = jnp.stack(
        [
            jnp.stack([jnp.sum(matrix * matrix, axis=(1, 2)) for matrix in group], axis=1)
            for group in (masters, directions)
        ],
        axis=2,
    )
    message = jnp.concatenate(
        [norm_parts, jnp.broadcast_to(local_squares.reshape(1, 16), (shards, 16))], axis=1
    )
    arrived = jnp.sum(lax.all_to_all(message, axes, 0, 0, tiled=True), axis=0)
    matrix_norms = jnp.sqrt(arrived[-16:].reshape(2, 4, 2))
    norm_update = adam_parts(arrived[:-16].reshape(2, 2, 2, rows), first_norm, second_norm)
    updates.append(norm_update)
    updated = [
        masters[index]
        - RATE
        * (matrix_norms[:, index, 0] / matrix_norms[:, index, 1])[:, None, None]
        * directions[index]
        for index in range(4)
    ]
    return (
        block_out,
        tokens_grad,
        *updated,
        norm_params - RATE * norm_update[2],
        *(array.astype(jnp.bfloat16) for array in updated),
        *(update[0] for update in updates),
        *(update[1] for update in updates),
        matrix_norms,
    )


def solution(mesh):
    in_specs = (
        P(("dp", "fsdp"), None),
        P(("dp", "fsdp")),
        P(("dp", "fsdp"), None),
        P(None, ("dp", "fsdp"), None),
        P(None, ("dp", "fsdp"), None),
        P(None, ("dp", "fsdp"), None),
        P(None, ("dp", "fsdp"), None),
        P(None, None, None, ("dp", "fsdp")),
        P(None, ("dp", "fsdp"), None),
        P(None, ("dp", "fsdp"), None),
        P(None, ("dp", "fsdp"), None),
        P(None, ("dp", "fsdp"), None),
        P(None, None, None, ("dp", "fsdp")),
        P(None, ("dp", "fsdp"), None),
        P(None, ("dp", "fsdp"), None),
        P(None, ("dp", "fsdp"), None),
        P(None, ("dp", "fsdp"), None),
        P(None, None, None, ("dp", "fsdp")),
    )
    out_specs = (
        P(("dp", "fsdp"), None),
        P(("dp", "fsdp"), None),
        P(None, ("dp", "fsdp"), None),
        P(None, ("dp", "fsdp"), None),
        P(None, ("dp", "fsdp"), None),
        P(None, ("dp", "fsdp"), None),
        P(None, None, None, ("dp", "fsdp")),
        P(None, ("dp", "fsdp"), None),
        P(None, ("dp", "fsdp"), None),
        P(None, ("dp", "fsdp"), None),
        P(None, ("dp", "fsdp"), None),
        P(None, ("dp", "fsdp"), None),
        P(None, ("dp", "fsdp"), None),
        P(None, ("dp", "fsdp"), None),
        P(None, ("dp", "fsdp"), None),
        P(None, None, None, ("dp", "fsdp")),
        P(None, ("dp", "fsdp"), None),
        P(None, ("dp", "fsdp"), None),
        P(None, ("dp", "fsdp"), None),
        P(None, ("dp", "fsdp"), None),
        P(None, None, None, ("dp", "fsdp")),
        P(),
    )
    return jax.shard_map(body, mesh=mesh, in_specs=in_specs, out_specs=out_specs, check_vma=False)
```

```python
import jax
import jax.numpy as jnp
from jax import lax
from jax.experimental import pallas as pl
from jax.experimental.pallas import tpu as pltpu
from jax.sharding import PartitionSpec as P

HEADS = 8
HEAD_DIM = 64
FRAMES = 17
WIN = 64
STEP = 5
WIDTH = 512
BLOCKS = 32
SLAB = WIDTH // BLOCKS
TILES = 4
TILE = FRAMES * WIN // TILES
SPOTS = WIN // TILES
HALF = TILE // 2
SCALE = HEAD_DIM ** (-0.5)
VMEM_BYTES = 56 * 2**20
COST = pl.CostEstimate(flops=10**8, bytes_accessed=10**5, transcendentals=0)

NORM_EPS = 1e-05
ADAM_EPS = 1e-06
BETA_FIRST = 0.5
BETA_SECOND = 0.5
RATE = 0.25
DECAY_RATE = 0.01
MASKED = -1e30


def row_norm(inputs):
    center = inputs - jnp.mean(inputs, axis=-1, keepdims=True)
    spread = jnp.mean(center * center, axis=-1, keepdims=True)
    scale = lax.rsqrt(spread + NORM_EPS)
    return center * scale, scale


def row_norm_back(grad, gain_row, normal, scale):
    scaled = grad * gain_row
    first = jnp.mean(scaled, axis=-1, keepdims=True)
    second = jnp.mean(scaled * normal, axis=-1, keepdims=True)
    return scale * (scaled - first - normal * second)


def fold_rows(array):
    return jnp.sum(array.reshape(-1, 8, array.shape[-1]), axis=0)


def gelu_pair(upward):
    bell = jnp.exp(-0.5 * upward * upward)
    place = 1.0 / (1.0 + 0.23164189 * jnp.abs(upward))
    tail = 0.5 * 1.061405429
    for factor in (-1.453152027, 1.421413741, -0.284496736, 0.254829592):
        tail = tail * place + 0.5 * factor
    tail = tail * place * bell
    cumulative = jnp.where(upward >= 0.0, 1.0 - tail, tail)
    return upward * cumulative, cumulative + 0.3989422804014327 * upward * bell


def dot_nn(left, right):
    return lax.dot_general(
        left, right, (((1,), (0,)), ((), ())), preferred_element_type=jnp.float32
    )


def dot_nt(left, right):
    return lax.dot_general(
        left, right, (((1,), (1,)), ((), ())), preferred_element_type=jnp.float32
    )


def dot_tn(left, right):
    return lax.dot_general(
        left, right, (((0,), (0,)), ((), ())), preferred_element_type=jnp.float32
    )


def slab(weights, index):
    return weights[:, SLAB * index : SLAB * index + SLAB, :].reshape(WIDTH, WIDTH)


def down_rows(weights, index):
    part = BLOCKS // 4
    return weights[part * index : part * index + part].reshape(WIDTH, WIDTH)


def weight_spec(array, index):
    return pl.BlockSpec(
        (BLOCKS, 4 * SLAB, WIDTH), lambda i: (0, index, 0), pipeline_mode=pl.Buffered(1)
    )


def stack_heads(pair):
    lane = lax.broadcasted_iota(jnp.int32, pair.shape, 1)
    zero = jnp.zeros_like(pair)
    return jnp.concatenate(
        [jnp.where(lane < HEAD_DIM, pair, zero), jnp.where(lane < HEAD_DIM, zero, pair)], axis=0
    )


def merge_heads(stacked):
    rows = stacked.shape[0] // 2
    lane = lax.broadcasted_iota(jnp.int32, (rows, 2 * HEAD_DIM), 1)
    return jnp.where(lane < HEAD_DIM, stacked[:rows], stacked[rows:])


def soft_weights(scores, axis):
    raised = jnp.exp(scores - jnp.max(scores, axis=axis, keepdims=True))
    return raised * (1.0 / jnp.sum(raised, axis=axis, keepdims=True))


def pair_caps():
    row = lax.broadcasted_iota(jnp.int32, (4 * WIN, 2 * WIN), 0)
    column = lax.broadcasted_iota(jnp.int32, (4 * WIN, 2 * WIN), 1)
    return jnp.where(row // WIN % 2 == column // WIN, 3.0e38, MASKED)


def frame_pairs():
    return [min(2 * index, FRAMES - 2) for index in range((FRAMES + 1) // 2)]


def outer_store(core, left, right, mine, other, block, row, rows):
    first = core[0] == 0
    count = 128 // rows
    for half in range(2):
        part = dot_tn(left[:, 256 * half : 256 * half + 256], right).astype(jnp.bfloat16)
        part = part.reshape(count, 2, rows, WIDTH)
        even, odd = part[:, 0], part[:, 1]
        place = pl.ds(block + count * half, count), pl.ds(row, rows)
        mine[place] = jnp.where(first, even, odd)
        other[place] = jnp.where(first, odd, even)


def slab_row(step, first):
    return pl.multiple_of((step - first) * SLAB, SLAB)


def grad_specs(rows):
    return [pl.BlockSpec((BLOCKS // 2, rows, WIDTH), lambda i: (0, 0, 0))] * 2


def grad_shapes(rows):
    return [jax.ShapeDtypeStruct((BLOCKS // 2, rows, WIDTH), jnp.bfloat16)] * 2


def part_of(step, first):
    return pl.ds(pl.multiple_of((step - first) * WIDTH, WIDTH), WIDTH)


def first_attention_kernel(
    tokens, weights, gains, normed_out, projected_out, probs, attended, middle_out, hidden_in_out,
    projected,
):
    step = pl.program_id(0)

    @pl.when(step < TILES)
    def _():
        normal, _ = row_norm(tokens[...].astype(jnp.float32))
        normed = (normal * gains[0:1, :] + gains[1:2, :]).astype(jnp.bfloat16)
        normed_out[...] = normed
        rows = pl.ds(pl.multiple_of(step * TILE, TILE), TILE)
        for index in range(3):
            part = dot_nn(normed, slab(weights, index)).astype(jnp.bfloat16)
            projected[rows, WIDTH * index : WIDTH * index + WIDTH] = part
            projected_out[:, WIDTH * index : WIDTH * index + WIDTH] = part

    @pl.when(step == TILES)
    def _():
        caps = pair_caps()
        for index, frame in enumerate(frame_pairs()):
            rows = slice(WIN * frame, WIN * frame + 2 * WIN)
            lanes = [slice(128 * pair, 128 * pair + 128) for pair in range(HEADS // 2)]
            queries = [stack_heads(projected[rows, lane] * SCALE) for lane in lanes]
            keys = [projected[rows, WIDTH + 128 * pair : WIDTH + 128 * pair + 128] for pair in range(4)]
            scores = [jnp.minimum(dot_nt(*both), caps) for both in zip(queries, keys)]
            shares = [soft_weights(score, -1).astype(jnp.bfloat16) for score in scores]
            for pair, share in enumerate(shares):
                probs[index, pair] = share
                values = projected[rows, 2 * WIDTH + 128 * pair : 2 * WIDTH + 128 * pair + 128]
                attended[rows, lanes[pair]] = merge_heads(dot_nn(share, values)).astype(jnp.bfloat16)

    @pl.when(step > TILES)
    def _():
        rows = pl.ds(pl.multiple_of((step - TILES - 1) * TILE, TILE), TILE)
        middle = tokens[...].astype(jnp.float32) + dot_nn(attended[rows, :], slab(weights, 3))
        middle_out[...] = middle
        normal, _ = row_norm(middle)
        hidden_in_out[...] = (normal * gains[2:3, :] + gains[3:4, :]).astype(jnp.bfloat16)


def first_attention(tokens, weights, gains):
    count = tokens.shape[0]

    def early(width):
        return pl.BlockSpec((TILE, width), lambda i: (jnp.minimum(i, TILES - 1), 0))

    def late(width):
        return pl.BlockSpec((TILE, width), lambda i: (jnp.maximum(i - TILES - 1, 0), 0))

    def whole_out(*shape):
        return pl.BlockSpec(shape, lambda i: (0,) * len(shape))

    def out(width, kind):
        return jax.ShapeDtypeStruct((count, width), kind)

    return pl.pallas_call(
        first_attention_kernel,
        grid=(2 * TILES + 1,),
        in_specs=[
            pl.BlockSpec(
                (TILE, WIDTH), lambda i: (jnp.where(i < TILES, i, jnp.maximum(i - TILES - 1, 0)), 0)
            ),
            weight_spec(weights, 0),
            whole_out(4, WIDTH),
        ],
        out_specs=[
            early(WIDTH),
            early(3 * WIDTH),
            whole_out((FRAMES + 1) // 2, HEADS // 2, 4 * WIN, 2 * WIN),
            whole_out(count, WIDTH),
            late(WIDTH),
            late(WIDTH),
        ],
        out_shape=[
            out(WIDTH, jnp.bfloat16),
            out(3 * WIDTH, jnp.bfloat16),
            jax.ShapeDtypeStruct(((FRAMES + 1) // 2, HEADS // 2, 4 * WIN, 2 * WIN), jnp.bfloat16),
            out(WIDTH, jnp.bfloat16),
            out(WIDTH, jnp.float32),
            out(WIDTH, jnp.bfloat16),
        ],
        scratch_shapes=[pltpu.VMEM((count, 3 * WIDTH), jnp.bfloat16)],
        compiler_params=pltpu.CompilerParams(vmem_limit_bytes=VMEM_BYTES),
        cost_estimate=COST,
        name="first_attention",
    )(tokens, weights, gains)


def first_mlp_kernel(place, middle, hidden_in, *refs):
    pieces = refs[:-6]
    hidden_out, slope_out, result_out, weights_out, weights, store_sem = refs[-6:]
    store = pltpu.make_async_copy(weights, weights_out, store_sem)

    @pl.when(pl.program_id(0) == 0)
    def _():
        if len(pieces) == 1:
            weights[...] = pieces[0][...]
        else:
            place_pieces(place, pieces, weights)
        store.start()

    weights_up = weights.at[:, : 4 * SLAB]
    weights_down = weights.at[:, 4 * SLAB :]
    result = middle[...]
    upward = dot_nn(hidden_in[...], slab(weights_up, 0))
    for index in range(4):
        columns = slice(WIDTH * index, WIDTH * index + WIDTH)
        following = dot_nn(hidden_in[...], slab(weights_up, index + 1)) if index < 3 else None
        value, slope = gelu_pair(upward)
        hidden = value.astype(jnp.bfloat16)
        hidden_out[:, columns] = hidden
        slope_out[:, columns] = slope.astype(jnp.bfloat16)
        result = result + dot_nn(hidden, down_rows(weights_down, index))
        upward = following
    result_out[...] = result

    @pl.when(pl.program_id(0) == TILES - 1)
    def _():
        store.wait()


def first_mlp(place, middle, hidden_in, pieces):
    count = middle.shape[0]

    def tile(width):
        return pl.BlockSpec((TILE, width), lambda i: (i, 0))

    return pl.pallas_call(
        first_mlp_kernel,
        grid=(TILES,),
        in_specs=[
            pl.BlockSpec(memory_space=pltpu.SMEM),
            tile(WIDTH),
            tile(WIDTH),
        ]
        + [
            pl.BlockSpec(piece.shape, lambda i: (0, 0, 0), pipeline_mode=pl.Buffered(1))
            for piece in pieces
        ],
        out_specs=[tile(4 * WIDTH), tile(4 * WIDTH), tile(WIDTH), pl.BlockSpec(memory_space=pl.ANY)],
        out_shape=[
            jax.ShapeDtypeStruct((count, 4 * WIDTH), jnp.bfloat16),
            jax.ShapeDtypeStruct((count, 4 * WIDTH), jnp.bfloat16),
            jax.ShapeDtypeStruct((count, WIDTH), jnp.float32),
            jax.ShapeDtypeStruct((BLOCKS, 8 * SLAB, WIDTH), jnp.bfloat16),
        ],
        scratch_shapes=[
            pltpu.VMEM((BLOCKS, 8 * SLAB, WIDTH), jnp.bfloat16),
            pltpu.SemaphoreType.DMA,
        ],
        compiler_params=pltpu.CompilerParams(vmem_limit_bytes=VMEM_BYTES),
        cost_estimate=COST,
        name="first_mlp",
    )(place, middle, hidden_in, *pieces)


def second_kernel(
    frame_count, core, inputs, cotangent, weights, late_weights, gains, result_out, grad_out, sums,
    mine_out, other_out,
    caps, query_rows, key_rows, value_rows, probs, slopes, normed, projected_grads, attended,
    branch_grads, hidden_in, up_grads, hidden, out_grads,
    weights_up, weights_down, mine, other, load_sems, store_sems,
):
    step = pl.program_id(0)

    def loads():
        return [
            pltpu.make_async_copy(
                late_weights.at[:, 4 * SLAB * index : 4 * SLAB * index + 4 * SLAB, :],
                ref,
                load_sems.at[index - 1],
            )
            for index, ref in ((1, weights_up), (2, weights_down))
        ]

    def stores(unit, place):
        return [
            pltpu.make_async_copy(ref.at[place], out.at[place], store_sems.at[index, unit])
            for index, (ref, out) in enumerate(((mine, mine_out), (other, other_out)))
        ]

    def slab_place(row):
        return slice(None), pl.ds(row, SLAB)

    def down_place(block):
        return pl.ds(block, 4), pl.ds(8 * SLAB, 4 * SLAB)

    @pl.when(step == 0)
    def _():
        for copy in loads():
            copy.start()
        row = lax.broadcasted_iota(jnp.int32, caps.shape, 0)
        column = lax.broadcasted_iota(jnp.int32, caps.shape, 1) % HALF
        soon, late = row // 8, column // 8
        video = (late < frame_count[0]) & (soon < frame_count[0])
        allowed = (row % 8 == column % 8) & ((soon == late) | ((soon < late) & video))
        caps[...] = jnp.where(allowed, 3.0e38, MASKED)
        sums[...] = jnp.zeros_like(sums)

    def flat(ref):
        array = ref[...].astype(jnp.float32)
        return jnp.concatenate(
            [array[:, :8].reshape(HALF, WIDTH), array[:, 8:].reshape(HALF, WIDTH)], axis=0
        )

    def keep(ref, value):
        halves = [value[HALF * half : HALF * half + HALF] for half in range(2)]
        ref[...] = jnp.concatenate(
            [half.reshape(FRAMES, 8, WIDTH) for half in halves], axis=1
        ).astype(ref.dtype)

    @pl.when(step < TILES)
    def _():
        rows = pl.ds(pl.multiple_of(step * TILE, TILE), TILE)
        inside = lax.broadcasted_iota(jnp.int32, (TILE, 1), 0) % HALF // 8 < frame_count[0]
        gate = jnp.where(inside, 1.0, 0.0)
        stream = flat(inputs)
        normal_first, scale_first = row_norm(stream)
        normed_tile = (normal_first * gains[0:1, :] + gains[1:2, :]).astype(jnp.bfloat16)
        normed[rows, :] = normed_tile
        for index, ref in enumerate((query_rows, key_rows, value_rows)):
            part = dot_nn(normed_tile, slab(weights, index))
            for half in range(2):
                piece = part[HALF * half : HALF * half + HALF]
                if index == 0:
                    for pair in range(HEADS // 2):
                        stacked = stack_heads(piece[:, 128 * pair : 128 * pair + 128] * SCALE)
                        ref[half, pair] = stacked.astype(jnp.bfloat16)
                else:
                    ref[half] = piece.astype(jnp.bfloat16)
        units = [
            (half, pair, slice(128 * pair, 128 * pair + 128))
            for half in range(2)
            for pair in range(HEADS // 2)
        ]
        scores = [
            dot_nt(key_rows[half, :, lanes], query_rows[half, pair]) for half, pair, lanes in units
        ]
        shares = [
            soft_weights(jnp.minimum(score, caps[...]), 0).astype(jnp.bfloat16) for score in scores
        ]
        for share, (half, pair, _) in zip(shares, units):
            probs[half, pair] = share
        parts = [
            merge_heads(dot_tn(share, value_rows[half, :, lanes]))
            for share, (half, _, lanes) in zip(shares, units)
        ]
        halves = [jnp.concatenate(parts[4 * half : 4 * half + 4], axis=1) for half in range(2)]
        attended_tile = jnp.concatenate(halves, axis=0).astype(jnp.bfloat16)
        attended[rows, :] = attended_tile
        middle = stream + gate * dot_nn(attended_tile, slab(weights, 3))
        normal_second, scale_second = row_norm(middle)
        hidden_in_tile = (normal_second * gains[2:3, :] + gains[3:4, :]).astype(jnp.bfloat16)
        hidden_in[rows, :] = hidden_in_tile

        @pl.when(step == 0)
        def _():
            for copy in loads():
                copy.wait()

        result = middle
        upward = dot_nn(hidden_in_tile, slab(weights_up, 0))
        for index in range(4):
            columns = slice(WIDTH * index, WIDTH * index + WIDTH)
            following = dot_nn(hidden_in_tile, slab(weights_up, index + 1)) if index < 3 else None
            value, slope = gelu_pair(upward)
            hidden_tile = value.astype(jnp.bfloat16)
            hidden[rows, columns] = hidden_tile
            slopes[:, columns] = slope
            result = result + dot_nn(hidden_tile, down_rows(weights_down, index))
            upward = following
        keep(result_out, result)

        upstream = flat(cotangent)
        out_grad = upstream.astype(jnp.bfloat16)
        out_grads[rows, :] = out_grad
        hidden_in_grad = jnp.zeros((TILE, WIDTH), jnp.float32)
        for index in range(4):
            columns = slice(WIDTH * index, WIDTH * index + WIDTH)
            up_grad = (dot_nt(out_grad, down_rows(weights_down, index)) * slopes[:, columns]).astype(
                jnp.bfloat16
            )
            up_grads[rows, columns] = up_grad
            hidden_in_grad = hidden_in_grad + dot_nt(up_grad, slab(weights_up, index))
        sums[2] += fold_rows(hidden_in_grad * normal_second)
        sums[3] += fold_rows(hidden_in_grad)
        middle_grad = upstream + row_norm_back(
            hidden_in_grad, gains[2:3, :], normal_second, scale_second
        )
        branch_grad = (middle_grad * gate).astype(jnp.bfloat16)
        branch_grads[rows, :] = branch_grad
        attended_grad = dot_nt(branch_grad, slab(weights, 3))
        grads = [
            stack_heads(attended_grad[HALF * half : HALF * half + HALF, lanes]).astype(jnp.bfloat16)
            for half, _, lanes in units
        ]
        share_grads = [
            dot_nt(value_rows[half, :, lanes], grad) for grad, (half, _, lanes) in zip(grads, units)
        ]
        value_grads = [
            dot_nn(probs[half, pair], grad) for grad, (half, pair, _) in zip(grads, units)
        ]
        score_grads = []
        for share_grad, (half, pair, _) in zip(share_grads, units):
            share = probs[half, pair].astype(jnp.float32)
            total = jnp.sum(share_grad * share, axis=0, keepdims=True)
            score_grads.append((share * (share_grad - total)).astype(jnp.bfloat16))
        query_grads = [
            dot_tn(grad, key_rows[half, :, lanes])
            for grad, (half, _, lanes) in zip(score_grads, units)
        ]
        key_grads = [
            dot_nn(grad, query_rows[half, pair]) for grad, (half, pair, _) in zip(score_grads, units)
        ]
        query_grads = [merge_heads(grad) * SCALE for grad in query_grads]
        halves = [
            jnp.concatenate(
                [
                    part
                    for parts in (query_grads, key_grads, value_grads)
                    for part in parts[4 * half : 4 * half + 4]
                ],
                axis=1,
            )
            for half in range(2)
        ]
        projected_grad = jnp.concatenate(halves, axis=0).astype(jnp.bfloat16)
        projected_grads[rows, :] = projected_grad
        normed_grad = jnp.zeros((TILE, WIDTH), jnp.float32)
        for index in range(3):
            part = projected_grad[:, WIDTH * index : WIDTH * index + WIDTH]
            normed_grad = normed_grad + dot_nt(part, slab(weights, index))
        sums[0] += fold_rows(normed_grad * normal_first)
        sums[1] += fold_rows(normed_grad)
        keep(
            grad_out,
            middle_grad + row_norm_back(normed_grad, gains[0:1, :], normal_first, scale_first),
        )

    @pl.when((step >= TILES) & (step < TILES + 4))
    def _():
        right = up_grads[:, part_of(step, TILES)]
        row = slab_row(step, TILES)
        outer_store(core, hidden_in, right, mine, other, 0, row, SLAB)
        for copy in stores(step - TILES, slab_place(row)):
            copy.start()

    @pl.when((step >= TILES + 4) & (step < TILES + 7))
    def _():
        right = projected_grads[:, part_of(step, TILES + 4)]
        row = slab_row(step, TILES - 1)
        outer_store(core, normed, right, mine, other, 0, row, SLAB)
        for copy in stores(step - TILES, slab_place(row)):
            copy.start()

    @pl.when((step >= TILES + 7) & (step < TILES + 11))
    def _():
        left = hidden[:, part_of(step, TILES + 7)]
        block = (step - TILES - 7) * 4
        outer_store(core, left, out_grads[...], mine, other, block, 8 * SLAB, 4 * SLAB)
        for copy in stores(step - TILES, down_place(block)):
            copy.start()

    @pl.when(step == TILES + 11)
    def _():
        outer_store(core, attended, branch_grads[...], mine, other, 0, 4 * SLAB, SLAB)
        for copy in stores(11, slab_place(4 * SLAB)):
            copy.start()
        places = [slab_place(SLAB * index) for index in (0, 1, 2, 3, 5, 6, 7)]
        places += [down_place(4 * index) for index in range(4)] + [slab_place(4 * SLAB)]
        for unit, place in enumerate(places):
            for copy in stores(unit, place):
                copy.wait()


def second_block(frame_counts, core, inputs, cotangent, weights, gains):
    def tile(width):
        return pl.BlockSpec((FRAMES, SPOTS, width), lambda i: (0, jnp.minimum(i, TILES - 1), 0))

    def held(width):
        return pltpu.VMEM((FRAMES * WIN, width * WIDTH), jnp.bfloat16)

    whole = (FRAMES, WIN, WIDTH)
    outs = pl.pallas_call(
        second_kernel,
        grid=(TILES + 12,),
        in_specs=[
            pl.BlockSpec(memory_space=pltpu.SMEM),
            pl.BlockSpec(memory_space=pltpu.SMEM),
            tile(WIDTH),
            tile(WIDTH),
            weight_spec(weights, 0),
            pl.BlockSpec(memory_space=pl.ANY),
            pl.BlockSpec((4, WIDTH), lambda i: (0, 0)),
        ],
        out_specs=[
            tile(WIDTH),
            tile(WIDTH),
            pl.BlockSpec((4, 8, WIDTH), lambda i: (0, 0, 0)),
            pl.BlockSpec(memory_space=pl.ANY),
            pl.BlockSpec(memory_space=pl.ANY),
        ],
        out_shape=[
            jax.ShapeDtypeStruct(whole, jnp.bfloat16),
            jax.ShapeDtypeStruct(whole, jnp.float32),
            jax.ShapeDtypeStruct((4, 8, WIDTH), jnp.float32),
            *grad_shapes(12 * SLAB),
        ],
        scratch_shapes=[
            pltpu.VMEM((HALF, 2 * HALF), jnp.float32),
            pltpu.VMEM((2, HEADS // 2, 2 * HALF, 128), jnp.bfloat16),
            pltpu.VMEM((2, HALF, WIDTH), jnp.bfloat16),
            pltpu.VMEM((2, HALF, WIDTH), jnp.bfloat16),
            pltpu.VMEM((2, HEADS // 2, HALF, 2 * HALF), jnp.bfloat16),
            pltpu.VMEM((TILE, 4 * WIDTH), jnp.float32),
            held(1),
            held(3),
            held(1),
            held(1),
            held(1),
            held(4),
            held(4),
            held(1),
            pltpu.VMEM((BLOCKS, 4 * SLAB, WIDTH), jnp.bfloat16),
            pltpu.VMEM((BLOCKS, 4 * SLAB, WIDTH), jnp.bfloat16),
            pltpu.VMEM((BLOCKS // 2, 12 * SLAB, WIDTH), jnp.bfloat16),
            pltpu.VMEM((BLOCKS // 2, 12 * SLAB, WIDTH), jnp.bfloat16),
            pltpu.SemaphoreType.DMA((2,)),
            pltpu.SemaphoreType.DMA((2, 12)),
        ],
        compiler_params=pltpu.CompilerParams(vmem_limit_bytes=VMEM_BYTES),
        cost_estimate=COST,
        name="second_block",
    )(
        frame_counts,
        core,
        inputs.reshape(whole),
        cotangent.reshape(whole),
        weights,
        weights,
        gains,
    )
    return (
        outs[0].reshape(-1, WIDTH),
        outs[1].reshape(-1, WIDTH),
        outs[2],
        tuple(outs[3:]),
    )


def first_back_kernel(
    core, upstream, slopes, middle, weights, weights_up, weights_down, gains, hidden, hidden_in,
    attended, queries_in, keys_in, values_in, probs, normed, middle_grad_out, sums, projected_grad_out,
    mine, other, up_grads, out_grads, branch_grads, attended_grads, projected_grads,
):
    step = pl.program_id(0)
    heads_at = TILES + 9
    last_at = heads_at + HEADS // 2

    @pl.when(step == 0)
    def _():
        sums[...] = jnp.zeros_like(sums)

    @pl.when(step < TILES)
    def _():
        rows = pl.ds(pl.multiple_of(step * TILE, TILE), TILE)
        out_grad = upstream[...].astype(jnp.bfloat16)
        out_grads[rows, :] = out_grad
        hidden_in_grad = jnp.zeros((TILE, WIDTH), jnp.float32)
        for index in range(4):
            columns = slice(WIDTH * index, WIDTH * index + WIDTH)
            up_grad = (dot_nt(out_grad, down_rows(weights_down, index)) * slopes[:, columns]).astype(
                jnp.bfloat16
            )
            up_grads[rows, columns] = up_grad
            hidden_in_grad = hidden_in_grad + dot_nt(up_grad, slab(weights_up, index))
        normal, scale = row_norm(middle[...])
        sums[0] += fold_rows(hidden_in_grad * normal)
        sums[1] += fold_rows(hidden_in_grad)
        middle_grad = upstream[...] + row_norm_back(hidden_in_grad, gains[2:3, :], normal, scale)
        middle_grad_out[...] = middle_grad
        branch_grad = middle_grad.astype(jnp.bfloat16)
        branch_grads[rows, :] = branch_grad
        attended_grad = dot_nt(branch_grad, slab(weights, 3)).astype(jnp.bfloat16)
        for pair in range(HEADS // 2):
            attended_grads[pair, rows, :] = attended_grad[:, 128 * pair : 128 * pair + 128]

    @pl.when((step >= TILES) & (step < TILES + 4))
    def _():
        right = up_grads[:, part_of(step, TILES)]
        outer_store(core, hidden_in, right, mine, other, 0, slab_row(step, TILES), SLAB)

    @pl.when((step >= TILES + 4) & (step < TILES + 8))
    def _():
        block = (step - TILES - 4) * 4
        outer_store(core, hidden, out_grads[...], mine, other, block, 8 * SLAB, 4 * SLAB)

    @pl.when(step == TILES + 8)
    def _():
        outer_store(core, attended, branch_grads[...], mine, other, 0, 4 * SLAB, SLAB)

    @pl.when((step >= heads_at) & (step < last_at))
    def _():
        pair = step - heads_at
        frames = list(enumerate(frame_pairs()))
        rows = [slice(WIN * frame, WIN * frame + 2 * WIN) for _, frame in frames]
        grads = [stack_heads(attended_grads[pair, row, :]) for row in rows]
        share_grads = [dot_nt(grad, values_in[row, :]) for grad, row in zip(grads, rows)]
        shares = [probs[index, 0] for index, _ in frames]
        value_grads = [dot_tn(share, grad) for share, grad in zip(shares, grads)]
        score_grads = []
        for share, share_grad in zip(shares, share_grads):
            share = share.astype(jnp.float32)
            total = jnp.sum(share_grad * share, axis=-1, keepdims=True)
            score_grads.append((share * (share_grad - total)).astype(jnp.bfloat16))
        query_grads = [dot_nn(grad, keys_in[row, :]) for grad, row in zip(score_grads, rows)]
        key_grads = [
            dot_tn(grad, stack_heads(queries_in[row, :] * SCALE))
            for grad, row in zip(score_grads, rows)
        ]
        query_grads = [merge_heads(grad) * SCALE for grad in query_grads]
        for index, parts in enumerate((query_grads, key_grads, value_grads)):
            lanes = pl.ds(pl.multiple_of(pair * 128 + WIDTH * index, 128), 128)
            for row, part in zip(rows, parts):
                projected_grads[row, lanes] = part.astype(jnp.bfloat16)

    @pl.when(step >= last_at)
    def _():
        right = projected_grads[:, part_of(step, last_at)]
        projected_grad_out[...] = right
        outer_store(core, normed, right, mine, other, 0, slab_row(step, last_at - 5), SLAB)


def first_back(
    core, upstream, slopes, middle, weights, late_weights, late_at, gains, hidden, hidden_in, attended,
    projected, probs, normed,
):
    count = upstream.shape[0]
    pairs = HEADS // 2
    heads_at = TILES + 9
    last_at = heads_at + pairs

    def tile(width):
        return pl.BlockSpec((TILE, width), lambda i: (jnp.minimum(i, TILES - 1), 0))

    def whole(*shape):
        return pl.BlockSpec(shape, lambda i: (0,) * len(shape), pipeline_mode=pl.Buffered(1))

    def pair_of(step):
        return jnp.clip(step - heads_at, 0, pairs - 1)

    def lanes(first):
        return pl.BlockSpec((count, 128), lambda i: (0, first + pair_of(i)))

    def held(width):
        return pltpu.VMEM((count, width * WIDTH), jnp.bfloat16)

    outs = pl.pallas_call(
        first_back_kernel,
        grid=(last_at + 3,),
        in_specs=[
            pl.BlockSpec(memory_space=pltpu.SMEM),
            tile(WIDTH),
            tile(4 * WIDTH),
            tile(WIDTH),
            weight_spec(weights, 0),
            weight_spec(late_weights, late_at),
            weight_spec(late_weights, late_at + 1),
            whole(4, WIDTH),
            pl.BlockSpec((count, WIDTH), lambda i: (0, jnp.clip(i - TILES - 4, 0, 3))),
            whole(count, WIDTH),
            whole(count, WIDTH),
            lanes(0),
            lanes(pairs),
            lanes(2 * pairs),
            pl.BlockSpec(
                ((FRAMES + 1) // 2, 1, 4 * WIN, 2 * WIN), lambda i: (0, pair_of(i), 0, 0)
            ),
            whole(count, WIDTH),
        ],
        out_specs=[
            tile(WIDTH),
            pl.BlockSpec((2, 8, WIDTH), lambda i: (0, 0, 0)),
            pl.BlockSpec((count, WIDTH), lambda i: (0, jnp.clip(i - last_at, 0, 2))),
            *grad_specs(12 * SLAB),
        ],
        out_shape=[
            jax.ShapeDtypeStruct((count, WIDTH), jnp.float32),
            jax.ShapeDtypeStruct((2, 8, WIDTH), jnp.float32),
            jax.ShapeDtypeStruct((count, 3 * WIDTH), jnp.bfloat16),
            *grad_shapes(12 * SLAB),
        ],
        scratch_shapes=[
            held(4),
            held(1),
            held(1),
            pltpu.VMEM((pairs, count, 128), jnp.bfloat16),
            held(3),
        ],
        compiler_params=pltpu.CompilerParams(vmem_limit_bytes=VMEM_BYTES),
        cost_estimate=COST,
        name="first_back",
    )(
        core, upstream, slopes, middle, weights, late_weights, late_weights, gains, hidden, hidden_in,
        attended, projected, projected, projected, probs, normed,
    )
    return (*outs[:3], tuple(outs[3:]))


def first_input_back_kernel(projected_grad, tokens, middle_grad, weights, gains, grad_out, sums):
    @pl.when(pl.program_id(0) == 0)
    def _():
        sums[...] = jnp.zeros_like(sums)

    normed_grad = jnp.zeros((TILE, WIDTH), jnp.float32)
    for index in range(3):
        part = projected_grad[:, WIDTH * index : WIDTH * index + WIDTH]
        normed_grad = normed_grad + dot_nt(part, slab(weights, index))
    normal, scale = row_norm(tokens[...].astype(jnp.float32))
    sums[0] += fold_rows(normed_grad * normal)
    sums[1] += fold_rows(normed_grad)
    grad_out[...] = middle_grad[...] + row_norm_back(normed_grad, gains[0:1, :], normal, scale)


def first_input_back(projected_grad, tokens, middle_grad, weights, gains):
    count = tokens.shape[0]

    def tile(width):
        return pl.BlockSpec((TILE, width), lambda i: (i, 0))

    def whole(*shape):
        return pl.BlockSpec(shape, lambda i: (0,) * len(shape), pipeline_mode=pl.Buffered(1))

    return pl.pallas_call(
        first_input_back_kernel,
        grid=(TILES,),
        in_specs=[
            tile(3 * WIDTH),
            tile(WIDTH),
            tile(WIDTH),
            whole(BLOCKS, 3 * SLAB, WIDTH),
            whole(4, WIDTH),
        ],
        out_specs=[tile(WIDTH), pl.BlockSpec((2, 8, WIDTH), lambda i: (0, 0, 0))],
        out_shape=[
            jax.ShapeDtypeStruct((count, WIDTH), jnp.float32),
            jax.ShapeDtypeStruct((2, 8, WIDTH), jnp.float32),
        ],
        compiler_params=pltpu.CompilerParams(vmem_limit_bytes=VMEM_BYTES),
        cost_estimate=COST,
        name="first_input_back",
    )(projected_grad, tokens, middle_grad, weights, gains)


def place_pieces(place, pieces, out):
    across, plane, core = place[0], place[1], place[2]
    for index, piece in enumerate(pieces):
        column = (across ^ (index % 4)) * 8 + (core ^ (index // 4))
        for way in range(4):
            out[column + (plane ^ way) * 2] = piece[way]


def arrange_kernel(place, *refs):
    place_pieces(place, refs[:-1], refs[-1])


def arrange(place, pieces, name):
    rows = pieces[0].shape[1]
    return pl.pallas_call(
        arrange_kernel,
        in_specs=[pl.BlockSpec(memory_space=pltpu.SMEM)]
        + [pl.BlockSpec(memory_space=pltpu.VMEM)] * 8,
        out_shape=jax.ShapeDtypeStruct((BLOCKS, rows, WIDTH), jnp.bfloat16),
        compiler_params=pltpu.CompilerParams(vmem_limit_bytes=VMEM_BYTES),
        cost_estimate=COST,
        name=name,
    )(place, *pieces)


def pack_kernel(w_qkv, w_out, w_up, w_down, norm, early, late, second):
    def narrow(array):
        return array.astype(jnp.bfloat16)

    for block, (start, rest) in enumerate(((early, late), (second, second))):
        for index in range(3):
            columns = slice(WIDTH * index, WIDTH * index + WIDTH)
            start[SLAB * index : SLAB * index + SLAB, :] = narrow(w_qkv[block, :, columns])
        start[3 * SLAB : 4 * SLAB, :] = narrow(w_out[block])
        first = 4 * SLAB * block
        for index in range(4):
            columns = slice(WIDTH * index, WIDTH * index + WIDTH)
            row = first + SLAB * index
            rest[row : row + SLAB, :] = narrow(w_up[block, :, columns])
        rest[first + 4 * SLAB : first + 8 * SLAB, :] = narrow(w_down[block])
    early[4 * SLAB :, :] = narrow(norm[...])


def pack_all(w_qkv, w_out, w_up, w_down, norm_rows):
    return pl.pallas_call(
        pack_kernel,
        out_shape=[
            jax.ShapeDtypeStruct((rows, WIDTH), jnp.bfloat16)
            for rows in (5 * SLAB, 8 * SLAB, 12 * SLAB)
        ],
        compiler_params=pltpu.CompilerParams(vmem_limit_bytes=VMEM_BYTES),
        cost_estimate=COST,
        name="pack",
    )(w_qkv, w_out, w_up, w_down, norm_rows)


def adam_parts(gradient, first_moment, second_moment):
    first_next = BETA_FIRST * first_moment + (1.0 - BETA_FIRST) * gradient
    second_next = BETA_SECOND * second_moment + (1.0 - BETA_SECOND) * gradient * gradient
    direction = (
        first_next
        / (1.0 - BETA_FIRST**STEP)
        / (jnp.sqrt(second_next / (1.0 - BETA_SECOND**STEP)) + ADAM_EPS)
    )
    return (first_next, second_next, direction)


def pack_weights(part_qkv, part_out, part_up, part_down):
    return jnp.concatenate(
        [part_qkv[:, WIDTH * i : WIDTH * i + WIDTH] for i in range(3)]
        + [part_out]
        + [part_up[:, WIDTH * i : WIDTH * i + WIDTH] for i in range(4)]
        + [part_down],
        axis=0,
    ).astype(jnp.bfloat16)


def to_blocks(packed, rows):
    if rows == SLAB:
        return packed
    packed = packed[:, : 12 * rows]
    slabs = packed[:, : 8 * rows].reshape(BLOCKS, -1, 8, rows, WIDTH).transpose(0, 2, 1, 3, 4)
    return jnp.concatenate(
        [
            slabs.reshape(BLOCKS, 8 * SLAB, WIDTH),
            packed[:, 8 * rows :].reshape(BLOCKS, 4 * SLAB, WIDTH),
        ],
        axis=1,
    )


def from_blocks(grads, rows, narrow):
    if rows == SLAB:
        return grads
    slabs = grads[:, : narrow * SLAB].reshape(BLOCKS, narrow, -1, rows, WIDTH)
    slabs = slabs.transpose(0, 2, 1, 3, 4).reshape(-1, narrow * rows, WIDTH)
    if grads.shape[1] == narrow * SLAB:
        return slabs
    wide = grads[:, narrow * SLAB :].reshape(slabs.shape[0], -1, WIDTH)
    return jnp.concatenate([slabs, wide], axis=1)


def swap(array, mask):
    count = lax.axis_size("dp") * lax.axis_size("fsdp")
    return lax.ppermute(array, ("dp", "fsdp"), [(device, device ^ mask) for device in range(count)])


def after(value, *others):
    return lax.optimization_barrier((value, *others))[0]


def gather_by_chips(shards):
    results = []
    steps = [(), ()]
    for shard in shards:
        shard = after(shard, *steps[0])
        steps[0] = [swap(shard, 2 * way) for way in (1, 2, 3)]
        pieces = after(jnp.stack([shard] + steps[0]), *steps[1])
        steps[1] = [swap(pieces, 8 * way) for way in (1, 2, 3)]
        results.append([pieces] + steps[1])
    return results


def gather_cores(pieces):
    return pieces + [swap(piece, 1) for piece in pieces]


def sum_at(arrays, index):
    total = sum(
        lax.dynamic_index_in_dim(array, index, 0, keepdims=False).astype(jnp.float32)
        for array in arrays
    )
    return total.astype(jnp.bfloat16)


def scatter_cores(pair, place):
    both = [array.reshape(4, 4, -1, WIDTH) for array in (pair[0], swap(pair[1], 1))]
    return [sum_at(both, place[0] ^ way) for way in (0, 3, 1, 2)]


def swap_chips(pieces):
    return [pieces[0]] + [swap(piece, 8 * way) for piece, way in zip(pieces[1:], (3, 1, 2))]


def fold_planes(pieces, place):
    return [sum_at(pieces, place[1] ^ way) for way in (0, 3, 2, 1)]


def scatter_planes(pieces, *others):
    pieces = [pieces[0]] + [swap(piece, 2 * way) for piece, way in zip(pieces[1:], (3, 2, 1))]
    pieces[0] = after(pieces[0], *others)
    return sum(piece.astype(jnp.float32) for piece in pieces)


def scatter_whole(pair, rows, narrow):
    grads = jnp.stack(pair, axis=1).reshape(BLOCKS, -1, WIDTH)
    summed = lax.psum_scatter(
        from_blocks(grads, rows, narrow), ("dp", "fsdp"), scatter_dimension=0, tiled=False
    )
    return summed.astype(jnp.float32)


def body(
    tokens,
    frame_counts,
    cotangent,
    w_qkv,
    w_out,
    w_up,
    w_down,
    norm_params,
    first_qkv,
    first_out,
    first_up,
    first_down,
    first_norm,
    second_qkv,
    second_out,
    second_up,
    second_down,
    second_norm,
):
    masters = (w_qkv, w_out, w_up, w_down)
    axes = ("dp", "fsdp")
    shards = lax.axis_size("dp") * lax.axis_size("fsdp")
    rows = w_out.shape[1]
    by_chips = (lax.axis_size("dp"), lax.axis_size("fsdp")) == (4, 8)
    fsdp = lax.axis_index("fsdp")
    place = jnp.stack([lax.axis_index("dp"), fsdp // 2, fsdp % 2]).astype(jnp.int32)
    norm_rows = jnp.pad(
        norm_params.reshape(1, -1), ((0, rows - 1), (0, WIDTH - 8 * rows))
    )
    if by_chips:
        *shard, second_shard = pack_all(w_qkv, w_out, w_up, w_down, norm_rows)
        early, late_pieces = gather_by_chips(shard)
        early = arrange(place, gather_cores(early), "arrange_early")
        norm_values = early[:, 4 * rows, : 8 * rows]
    else:
        shard = pack_weights(w_qkv[0], w_out[0], w_up[0], w_down[0])
        second_shard = pack_weights(w_qkv[1], w_out[1], w_up[1], w_down[1])
        shard = jnp.concatenate([shard, norm_rows.astype(jnp.bfloat16)], axis=0)
        gathered = lax.all_gather(shard, axes, axis=0)
        norm_values = gathered[:, 12 * rows, : 8 * rows]
        early = to_blocks(gathered, rows)
    gains = norm_values.reshape(shards, 2, 4, rows)
    gains = gains.transpose(1, 2, 0, 3).reshape(2, 4, WIDTH).astype(jnp.float32)
    weights_second = to_blocks(lax.all_gather(second_shard, axes, axis=0), rows)

    normed, projected, probs, attended, middle, hidden_in = first_attention(tokens, early, gains[0])
    if by_chips:
        late_pieces = gather_cores([after(piece, hidden_in) for piece in late_pieces])
    else:
        late_pieces = [early[:, 4 * SLAB : 12 * SLAB]]
    hidden, slopes, stream, late = first_mlp(place, middle, hidden_in, late_pieces)
    core = place[2:] if by_chips else jnp.zeros((1,), jnp.int32)
    block_out, upstream, sums_second, pair_second = second_block(
        frame_counts, core, stream, cotangent, weights_second, gains[1]
    )
    if by_chips:
        second = scatter_cores(pair_second, place)
        upstream = after(upstream, *second)
        second = swap_chips(second)
    middle_grad, sums_late, projected_grad, pair_first = first_back(
        core, upstream, slopes, middle, early, late, 0, gains[0], hidden, hidden_in, attended,
        projected, probs, normed,
    )
    if by_chips:
        second[0], *pair_first = lax.optimization_barrier((second[0], *pair_first, *second[1:]))[:3]
        first = scatter_cores(pair_first, place)
        projected_grad = after(projected_grad, *first)
        first = swap_chips(first)
        reduced_second = scatter_planes(fold_planes(second, place))
    tokens_grad, sums_early = first_input_back(
        projected_grad, tokens, middle_grad, early, gains[0]
    )
    if by_chips:
        first[0] = after(first[0], tokens_grad)
        reduced_first = scatter_planes(fold_planes(first, place))
    else:
        reduced_second = scatter_whole(pair_second, rows, 8)
        reduced_first = scatter_whole(pair_first, rows, 8)

    def columns(packed, first, last):
        return jnp.concatenate(
            [packed[rows * index : rows * index + rows] for index in range(first, last)], axis=1
        )

    reduced_first, reduced_second = (
        (columns(both, 5, 8), columns(both, 4, 5), columns(both, 0, 4), both[8 * rows :])
        for both in (reduced_first, reduced_second)
    )

    norm_parts = jnp.concatenate(
        [jnp.sum(part, axis=1) for part in (sums_early, sums_late, sums_second)]
    )
    norm_parts = norm_parts.reshape(8, shards, rows).transpose(1, 0, 2).reshape(shards, -1)
    stacked = [jnp.stack(pair) for pair in zip(reduced_first, reduced_second)]
    firsts = (first_qkv, first_out, first_up, first_down)
    seconds = (second_qkv, second_out, second_up, second_down)
    updates = [adam_parts(*parts) for parts in zip(stacked, firsts, seconds)]
    directions = [update[2] + DECAY_RATE * master for update, master in zip(updates, masters)]
    local_squares = jnp.stack(
        [
            jnp.stack([jnp.sum(matrix * matrix, axis=(1, 2)) for matrix in group], axis=1)
            for group in (masters, directions)
        ],
        axis=2,
    )
    message = jnp.concatenate(
        [norm_parts, jnp.broadcast_to(local_squares.reshape(1, 16), (shards, 16))], axis=1
    )
    arrived = jnp.sum(lax.all_to_all(message, axes, 0, 0, tiled=True), axis=0)
    matrix_norms = jnp.sqrt(arrived[-16:].reshape(2, 4, 2))
    norm_update = adam_parts(arrived[:-16].reshape(2, 2, 2, rows), first_norm, second_norm)
    updates.append(norm_update)
    updated = [
        masters[index]
        - RATE
        * (matrix_norms[:, index, 0] / matrix_norms[:, index, 1])[:, None, None]
        * directions[index]
        for index in range(4)
    ]
    return (
        block_out,
        tokens_grad,
        *updated,
        norm_params - RATE * norm_update[2],
        *(array.astype(jnp.bfloat16) for array in updated),
        *(update[0] for update in updates),
        *(update[1] for update in updates),
        matrix_norms,
    )


def solution(mesh):
    in_specs = (
        P(("dp", "fsdp"), None),
        P(("dp", "fsdp")),
        P(("dp", "fsdp"), None),
        P(None, ("dp", "fsdp"), None),
        P(None, ("dp", "fsdp"), None),
        P(None, ("dp", "fsdp"), None),
        P(None, ("dp", "fsdp"), None),
        P(None, None, None, ("dp", "fsdp")),
        P(None, ("dp", "fsdp"), None),
        P(None, ("dp", "fsdp"), None),
        P(None, ("dp", "fsdp"), None),
        P(None, ("dp", "fsdp"), None),
        P(None, None, None, ("dp", "fsdp")),
        P(None, ("dp", "fsdp"), None),
        P(None, ("dp", "fsdp"), None),
        P(None, ("dp", "fsdp"), None),
        P(None, ("dp", "fsdp"), None),
        P(None, None, None, ("dp", "fsdp")),
    )
    out_specs = (
        P(("dp", "fsdp"), None),
        P(("dp", "fsdp"), None),
        P(None, ("dp", "fsdp"), None),
        P(None, ("dp", "fsdp"), None),
        P(None, ("dp", "fsdp"), None),
        P(None, ("dp", "fsdp"), None),
        P(None, None, None, ("dp", "fsdp")),
        P(None, ("dp", "fsdp"), None),
        P(None, ("dp", "fsdp"), None),
        P(None, ("dp", "fsdp"), None),
        P(None, ("dp", "fsdp"), None),
        P(None, ("dp", "fsdp"), None),
        P(None, ("dp", "fsdp"), None),
        P(None, ("dp", "fsdp"), None),
        P(None, ("dp", "fsdp"), None),
        P(None, None, None, ("dp", "fsdp")),
        P(None, ("dp", "fsdp"), None),
        P(None, ("dp", "fsdp"), None),
        P(None, ("dp", "fsdp"), None),
        P(None, ("dp", "fsdp"), None),
        P(None, None, None, ("dp", "fsdp")),
        P(),
    )
    return jax.shard_map(body, mesh=mesh, in_specs=in_specs, out_specs=out_specs, check_vma=False)
```

```python
import jax
import jax.numpy as jnp
from jax import lax
from jax.experimental import pallas as pl
from jax.experimental.pallas import tpu as pltpu
from jax.sharding import PartitionSpec as P

HEADS = 8
HEAD_DIM = 64
FRAMES = 17
WIN = 64
STEP = 5
WIDTH = 512
BLOCKS = 32
SLAB = WIDTH // BLOCKS
TILES = 4
TILE = FRAMES * WIN // TILES
SPOTS = WIN // TILES
HALF = TILE // 2
SCALE = HEAD_DIM ** (-0.5)
VMEM_BYTES = 56 * 2**20
COST = pl.CostEstimate(flops=10**8, bytes_accessed=10**5, transcendentals=0)

NORM_EPS = 1e-05
ADAM_EPS = 1e-06
BETA_FIRST = 0.5
BETA_SECOND = 0.5
RATE = 0.25
DECAY_RATE = 0.01
MASKED = -1e30


def row_norm(inputs):
    center = inputs - jnp.mean(inputs, axis=-1, keepdims=True)
    spread = jnp.mean(center * center, axis=-1, keepdims=True)
    scale = lax.rsqrt(spread + NORM_EPS)
    return center * scale, scale


def row_norm_back(grad, gain_row, normal, scale):
    scaled = grad * gain_row
    first = jnp.mean(scaled, axis=-1, keepdims=True)
    second = jnp.mean(scaled * normal, axis=-1, keepdims=True)
    return scale * (scaled - first - normal * second)


def fold_rows(array):
    return jnp.sum(array.reshape(-1, 8, array.shape[-1]), axis=0)


def gelu_pair(upward):
    bell = jnp.exp(-0.5 * upward * upward)
    place = 1.0 / (1.0 + 0.23164189 * jnp.abs(upward))
    tail = 0.5 * 1.061405429
    for factor in (-1.453152027, 1.421413741, -0.284496736, 0.254829592):
        tail = tail * place + 0.5 * factor
    tail = tail * place * bell
    cumulative = jnp.where(upward >= 0.0, 1.0 - tail, tail)
    return upward * cumulative, cumulative + 0.3989422804014327 * upward * bell


def dot_nn(left, right):
    return lax.dot_general(
        left, right, (((1,), (0,)), ((), ())), preferred_element_type=jnp.float32
    )


def dot_nt(left, right):
    return lax.dot_general(
        left, right, (((1,), (1,)), ((), ())), preferred_element_type=jnp.float32
    )


def dot_tn(left, right):
    return lax.dot_general(
        left, right, (((0,), (0,)), ((), ())), preferred_element_type=jnp.float32
    )


def slab(weights, index):
    return weights[:, SLAB * index : SLAB * index + SLAB, :].reshape(WIDTH, WIDTH)


def down_rows(weights, index):
    part = BLOCKS // 4
    return weights[part * index : part * index + part].reshape(WIDTH, WIDTH)


def weight_spec(array, index):
    return pl.BlockSpec(
        (BLOCKS, 4 * SLAB, WIDTH), lambda i: (0, index, 0), pipeline_mode=pl.Buffered(1)
    )


def stack_heads(pair):
    lane = lax.broadcasted_iota(jnp.int32, pair.shape, 1)
    zero = jnp.zeros_like(pair)
    return jnp.concatenate(
        [jnp.where(lane < HEAD_DIM, pair, zero), jnp.where(lane < HEAD_DIM, zero, pair)], axis=0
    )


def merge_heads(stacked):
    rows = stacked.shape[0] // 2
    lane = lax.broadcasted_iota(jnp.int32, (rows, 2 * HEAD_DIM), 1)
    return jnp.where(lane < HEAD_DIM, stacked[:rows], stacked[rows:])


def soft_weights(scores, axis):
    raised = jnp.exp(scores - jnp.max(scores, axis=axis, keepdims=True))
    return raised * (1.0 / jnp.sum(raised, axis=axis, keepdims=True))


def pair_caps():
    row = lax.broadcasted_iota(jnp.int32, (4 * WIN, 2 * WIN), 0)
    column = lax.broadcasted_iota(jnp.int32, (4 * WIN, 2 * WIN), 1)
    return jnp.where(row // WIN % 2 == column // WIN, 3.0e38, MASKED)


def frame_pairs():
    return [min(2 * index, FRAMES - 2) for index in range((FRAMES + 1) // 2)]


def outer_store(core, left, right, mine, other, block, row, rows):
    first = core[0] == 0
    count = 128 // rows
    for half in range(2):
        part = dot_tn(left[:, 256 * half : 256 * half + 256], right).astype(jnp.bfloat16)
        part = part.reshape(count, 2, rows, WIDTH)
        even, odd = part[:, 0], part[:, 1]
        place = pl.ds(block + count * half, count), pl.ds(row, rows)
        mine[place] = jnp.where(first, even, odd)
        other[place] = jnp.where(first, odd, even)


def slab_row(step, first):
    return pl.multiple_of((step - first) * SLAB, SLAB)


def grad_shapes(rows):
    return [jax.ShapeDtypeStruct((BLOCKS // 2, rows, WIDTH), jnp.bfloat16)] * 2


def slab_place(row):
    return slice(None), pl.ds(row, SLAB)


def down_place(block):
    return pl.ds(block, 4), pl.ds(8 * SLAB, 4 * SLAB)


def grad_copies(pairs, sems, unit, place):
    return [
        pltpu.make_async_copy(ref.at[place], out.at[place], sems.at[index, unit])
        for index, (ref, out) in enumerate(pairs)
    ]


def part_of(step, first):
    return pl.ds(pl.multiple_of((step - first) * WIDTH, WIDTH), WIDTH)


def first_attention_kernel(
    tokens, weights, gains, normed_out, projected_out, probs, attended, middle_out, hidden_in_out,
    projected,
):
    step = pl.program_id(0)

    @pl.when(step < TILES)
    def _():
        normal, _ = row_norm(tokens[...].astype(jnp.float32))
        normed = (normal * gains[0:1, :] + gains[1:2, :]).astype(jnp.bfloat16)
        normed_out[...] = normed
        rows = pl.ds(pl.multiple_of(step * TILE, TILE), TILE)
        for index in range(3):
            part = dot_nn(normed, slab(weights, index)).astype(jnp.bfloat16)
            projected[rows, WIDTH * index : WIDTH * index + WIDTH] = part
            projected_out[:, WIDTH * index : WIDTH * index + WIDTH] = part

    @pl.when(step == TILES)
    def _():
        caps = pair_caps()
        for index, frame in enumerate(frame_pairs()):
            rows = slice(WIN * frame, WIN * frame + 2 * WIN)
            lanes = [slice(128 * pair, 128 * pair + 128) for pair in range(HEADS // 2)]
            queries = [stack_heads(projected[rows, lane] * SCALE) for lane in lanes]
            keys = [projected[rows, WIDTH + 128 * pair : WIDTH + 128 * pair + 128] for pair in range(4)]
            scores = [jnp.minimum(dot_nt(*both), caps) for both in zip(queries, keys)]
            shares = [soft_weights(score, -1).astype(jnp.bfloat16) for score in scores]
            for pair, share in enumerate(shares):
                probs[index, pair] = share
                values = projected[rows, 2 * WIDTH + 128 * pair : 2 * WIDTH + 128 * pair + 128]
                attended[rows, lanes[pair]] = merge_heads(dot_nn(share, values)).astype(jnp.bfloat16)

    @pl.when(step > TILES)
    def _():
        rows = pl.ds(pl.multiple_of((step - TILES - 1) * TILE, TILE), TILE)
        middle = tokens[...].astype(jnp.float32) + dot_nn(attended[rows, :], slab(weights, 3))
        middle_out[...] = middle
        normal, _ = row_norm(middle)
        hidden_in_out[...] = (normal * gains[2:3, :] + gains[3:4, :]).astype(jnp.bfloat16)


def first_attention(tokens, weights, gains):
    count = tokens.shape[0]

    def early(width):
        return pl.BlockSpec((TILE, width), lambda i: (jnp.minimum(i, TILES - 1), 0))

    def late(width):
        return pl.BlockSpec((TILE, width), lambda i: (jnp.maximum(i - TILES - 1, 0), 0))

    def whole_out(*shape):
        return pl.BlockSpec(shape, lambda i: (0,) * len(shape))

    def out(width, kind):
        return jax.ShapeDtypeStruct((count, width), kind)

    return pl.pallas_call(
        first_attention_kernel,
        grid=(2 * TILES + 1,),
        in_specs=[
            pl.BlockSpec(
                (TILE, WIDTH), lambda i: (jnp.where(i < TILES, i, jnp.maximum(i - TILES - 1, 0)), 0)
            ),
            weight_spec(weights, 0),
            whole_out(4, WIDTH),
        ],
        out_specs=[
            early(WIDTH),
            early(3 * WIDTH),
            whole_out((FRAMES + 1) // 2, HEADS // 2, 4 * WIN, 2 * WIN),
            whole_out(count, WIDTH),
            late(WIDTH),
            late(WIDTH),
        ],
        out_shape=[
            out(WIDTH, jnp.bfloat16),
            out(3 * WIDTH, jnp.bfloat16),
            jax.ShapeDtypeStruct(((FRAMES + 1) // 2, HEADS // 2, 4 * WIN, 2 * WIN), jnp.bfloat16),
            out(WIDTH, jnp.bfloat16),
            out(WIDTH, jnp.float32),
            out(WIDTH, jnp.bfloat16),
        ],
        scratch_shapes=[pltpu.VMEM((count, 3 * WIDTH), jnp.bfloat16)],
        compiler_params=pltpu.CompilerParams(vmem_limit_bytes=VMEM_BYTES),
        cost_estimate=COST,
        name="first_attention",
    )(tokens, weights, gains)


def first_mlp_kernel(place, middle, hidden_in, *refs):
    pieces = refs[:-6]
    hidden_out, slope_out, result_out, weights_out, weights, store_sem = refs[-6:]
    store = pltpu.make_async_copy(weights, weights_out, store_sem)

    @pl.when(pl.program_id(0) == 0)
    def _():
        if len(pieces) == 1:
            weights[...] = pieces[0][...]
        else:
            place_pieces(place, pieces, weights)
        store.start()

    weights_up = weights.at[:, : 4 * SLAB]
    weights_down = weights.at[:, 4 * SLAB :]
    result = middle[...]
    upward = dot_nn(hidden_in[...], slab(weights_up, 0))
    for index in range(4):
        columns = slice(WIDTH * index, WIDTH * index + WIDTH)
        following = dot_nn(hidden_in[...], slab(weights_up, index + 1)) if index < 3 else None
        value, slope = gelu_pair(upward)
        hidden = value.astype(jnp.bfloat16)
        hidden_out[:, columns] = hidden
        slope_out[:, columns] = slope.astype(jnp.bfloat16)
        result = result + dot_nn(hidden, down_rows(weights_down, index))
        upward = following
    result_out[...] = result

    @pl.when(pl.program_id(0) == TILES - 1)
    def _():
        store.wait()


def first_mlp(place, middle, hidden_in, pieces):
    count = middle.shape[0]

    def tile(width):
        return pl.BlockSpec((TILE, width), lambda i: (i, 0))

    return pl.pallas_call(
        first_mlp_kernel,
        grid=(TILES,),
        in_specs=[
            pl.BlockSpec(memory_space=pltpu.SMEM),
            tile(WIDTH),
            tile(WIDTH),
        ]
        + [
            pl.BlockSpec(piece.shape, lambda i: (0, 0, 0), pipeline_mode=pl.Buffered(1))
            for piece in pieces
        ],
        out_specs=[tile(4 * WIDTH), tile(4 * WIDTH), tile(WIDTH), pl.BlockSpec(memory_space=pl.ANY)],
        out_shape=[
            jax.ShapeDtypeStruct((count, 4 * WIDTH), jnp.bfloat16),
            jax.ShapeDtypeStruct((count, 4 * WIDTH), jnp.bfloat16),
            jax.ShapeDtypeStruct((count, WIDTH), jnp.float32),
            jax.ShapeDtypeStruct((BLOCKS, 8 * SLAB, WIDTH), jnp.bfloat16),
        ],
        scratch_shapes=[
            pltpu.VMEM((BLOCKS, 8 * SLAB, WIDTH), jnp.bfloat16),
            pltpu.SemaphoreType.DMA,
        ],
        compiler_params=pltpu.CompilerParams(vmem_limit_bytes=VMEM_BYTES),
        cost_estimate=COST,
        name="first_mlp",
    )(place, middle, hidden_in, *pieces)


def second_kernel(
    frame_count, core, inputs, cotangent, weights, late_weights, gains, result_out, grad_out, sums,
    mine_out, other_out,
    caps, query_rows, key_rows, value_rows, probs, slopes, normed, projected_grads, attended,
    branch_grads, hidden_in, up_grads, hidden, out_grads,
    weights_up, weights_down, mine, other, load_sems, store_sems,
):
    step = pl.program_id(0)

    def loads():
        return [
            pltpu.make_async_copy(
                late_weights.at[:, 4 * SLAB * index : 4 * SLAB * index + 4 * SLAB, :],
                ref,
                load_sems.at[index - 1],
            )
            for index, ref in ((1, weights_up), (2, weights_down))
        ]

    def stores(unit, place):
        return grad_copies(((mine, mine_out), (other, other_out)), store_sems, unit, place)

    @pl.when(step == 0)
    def _():
        for copy in loads():
            copy.start()
        row = lax.broadcasted_iota(jnp.int32, caps.shape, 0)
        column = lax.broadcasted_iota(jnp.int32, caps.shape, 1) % HALF
        soon, late = row // 8, column // 8
        video = (late < frame_count[0]) & (soon < frame_count[0])
        allowed = (row % 8 == column % 8) & ((soon == late) | ((soon < late) & video))
        caps[...] = jnp.where(allowed, 3.0e38, MASKED)
        sums[...] = jnp.zeros_like(sums)

    def flat(ref):
        array = ref[...].astype(jnp.float32)
        return jnp.concatenate(
            [array[:, :8].reshape(HALF, WIDTH), array[:, 8:].reshape(HALF, WIDTH)], axis=0
        )

    def keep(ref, value):
        halves = [value[HALF * half : HALF * half + HALF] for half in range(2)]
        ref[...] = jnp.concatenate(
            [half.reshape(FRAMES, 8, WIDTH) for half in halves], axis=1
        ).astype(ref.dtype)

    @pl.when(step < TILES)
    def _():
        rows = pl.ds(pl.multiple_of(step * TILE, TILE), TILE)
        inside = lax.broadcasted_iota(jnp.int32, (TILE, 1), 0) % HALF // 8 < frame_count[0]
        gate = jnp.where(inside, 1.0, 0.0)
        stream = flat(inputs)
        normal_first, scale_first = row_norm(stream)
        normed_tile = (normal_first * gains[0:1, :] + gains[1:2, :]).astype(jnp.bfloat16)
        normed[rows, :] = normed_tile
        for index, ref in enumerate((query_rows, key_rows, value_rows)):
            part = dot_nn(normed_tile, slab(weights, index))
            for half in range(2):
                piece = part[HALF * half : HALF * half + HALF]
                if index == 0:
                    for pair in range(HEADS // 2):
                        stacked = stack_heads(piece[:, 128 * pair : 128 * pair + 128] * SCALE)
                        ref[half, pair] = stacked.astype(jnp.bfloat16)
                else:
                    ref[half] = piece.astype(jnp.bfloat16)
        units = [
            (half, pair, slice(128 * pair, 128 * pair + 128))
            for half in range(2)
            for pair in range(HEADS // 2)
        ]
        scores = [
            dot_nt(key_rows[half, :, lanes], query_rows[half, pair]) for half, pair, lanes in units
        ]
        shares = [
            soft_weights(jnp.minimum(score, caps[...]), 0).astype(jnp.bfloat16) for score in scores
        ]
        for share, (half, pair, _) in zip(shares, units):
            probs[half, pair] = share
        parts = [
            merge_heads(dot_tn(share, value_rows[half, :, lanes]))
            for share, (half, _, lanes) in zip(shares, units)
        ]
        halves = [jnp.concatenate(parts[4 * half : 4 * half + 4], axis=1) for half in range(2)]
        attended_tile = jnp.concatenate(halves, axis=0).astype(jnp.bfloat16)
        attended[rows, :] = attended_tile
        middle = stream + gate * dot_nn(attended_tile, slab(weights, 3))
        normal_second, scale_second = row_norm(middle)
        hidden_in_tile = (normal_second * gains[2:3, :] + gains[3:4, :]).astype(jnp.bfloat16)
        hidden_in[rows, :] = hidden_in_tile

        @pl.when(step == 0)
        def _():
            for copy in loads():
                copy.wait()

        result = middle
        upward = dot_nn(hidden_in_tile, slab(weights_up, 0))
        for index in range(4):
            columns = slice(WIDTH * index, WIDTH * index + WIDTH)
            following = dot_nn(hidden_in_tile, slab(weights_up, index + 1)) if index < 3 else None
            value, slope = gelu_pair(upward)
            hidden_tile = value.astype(jnp.bfloat16)
            hidden[rows, columns] = hidden_tile
            slopes[:, columns] = slope
            result = result + dot_nn(hidden_tile, down_rows(weights_down, index))
            upward = following
        keep(result_out, result)

        upstream = flat(cotangent)
        out_grad = upstream.astype(jnp.bfloat16)
        out_grads[rows, :] = out_grad
        hidden_in_grad = jnp.zeros((TILE, WIDTH), jnp.float32)
        for index in range(4):
            columns = slice(WIDTH * index, WIDTH * index + WIDTH)
            up_grad = (dot_nt(out_grad, down_rows(weights_down, index)) * slopes[:, columns]).astype(
                jnp.bfloat16
            )
            up_grads[rows, columns] = up_grad
            hidden_in_grad = hidden_in_grad + dot_nt(up_grad, slab(weights_up, index))
        sums[2] += fold_rows(hidden_in_grad * normal_second)
        sums[3] += fold_rows(hidden_in_grad)
        middle_grad = upstream + row_norm_back(
            hidden_in_grad, gains[2:3, :], normal_second, scale_second
        )
        branch_grad = (middle_grad * gate).astype(jnp.bfloat16)
        branch_grads[rows, :] = branch_grad
        attended_grad = dot_nt(branch_grad, slab(weights, 3))
        grads = [
            stack_heads(attended_grad[HALF * half : HALF * half + HALF, lanes]).astype(jnp.bfloat16)
            for half, _, lanes in units
        ]
        share_grads = [
            dot_nt(value_rows[half, :, lanes], grad) for grad, (half, _, lanes) in zip(grads, units)
        ]
        value_grads = [
            dot_nn(probs[half, pair], grad) for grad, (half, pair, _) in zip(grads, units)
        ]
        score_grads = []
        for share_grad, (half, pair, _) in zip(share_grads, units):
            share = probs[half, pair].astype(jnp.float32)
            total = jnp.sum(share_grad * share, axis=0, keepdims=True)
            score_grads.append((share * (share_grad - total)).astype(jnp.bfloat16))
        query_grads = [
            dot_tn(grad, key_rows[half, :, lanes])
            for grad, (half, _, lanes) in zip(score_grads, units)
        ]
        key_grads = [
            dot_nn(grad, query_rows[half, pair]) for grad, (half, pair, _) in zip(score_grads, units)
        ]
        query_grads = [merge_heads(grad) * SCALE for grad in query_grads]
        halves = [
            jnp.concatenate(
                [
                    part
                    for parts in (query_grads, key_grads, value_grads)
                    for part in parts[4 * half : 4 * half + 4]
                ],
                axis=1,
            )
            for half in range(2)
        ]
        projected_grad = jnp.concatenate(halves, axis=0).astype(jnp.bfloat16)
        projected_grads[rows, :] = projected_grad
        normed_grad = jnp.zeros((TILE, WIDTH), jnp.float32)
        for index in range(3):
            part = projected_grad[:, WIDTH * index : WIDTH * index + WIDTH]
            normed_grad = normed_grad + dot_nt(part, slab(weights, index))
        sums[0] += fold_rows(normed_grad * normal_first)
        sums[1] += fold_rows(normed_grad)
        keep(
            grad_out,
            middle_grad + row_norm_back(normed_grad, gains[0:1, :], normal_first, scale_first),
        )

    @pl.when((step >= TILES) & (step < TILES + 4))
    def _():
        right = up_grads[:, part_of(step, TILES)]
        row = slab_row(step, TILES)
        outer_store(core, hidden_in, right, mine, other, 0, row, SLAB)
        for copy in stores(step - TILES, slab_place(row)):
            copy.start()

    @pl.when((step >= TILES + 4) & (step < TILES + 7))
    def _():
        right = projected_grads[:, part_of(step, TILES + 4)]
        row = slab_row(step, TILES - 1)
        outer_store(core, normed, right, mine, other, 0, row, SLAB)
        for copy in stores(step - TILES, slab_place(row)):
            copy.start()

    @pl.when((step >= TILES + 7) & (step < TILES + 11))
    def _():
        left = hidden[:, part_of(step, TILES + 7)]
        block = (step - TILES - 7) * 4
        outer_store(core, left, out_grads[...], mine, other, block, 8 * SLAB, 4 * SLAB)
        for copy in stores(step - TILES, down_place(block)):
            copy.start()

    @pl.when(step == TILES + 11)
    def _():
        outer_store(core, attended, branch_grads[...], mine, other, 0, 4 * SLAB, SLAB)
        for copy in stores(11, slab_place(4 * SLAB)):
            copy.start()
        places = [slab_place(SLAB * index) for index in (0, 1, 2, 3, 5, 6, 7)]
        places += [down_place(4 * index) for index in range(4)] + [slab_place(4 * SLAB)]
        for unit, place in enumerate(places):
            for copy in stores(unit, place):
                copy.wait()


def second_block(frame_counts, core, inputs, cotangent, weights, gains):
    def tile(width):
        return pl.BlockSpec((FRAMES, SPOTS, width), lambda i: (0, jnp.minimum(i, TILES - 1), 0))

    def held(width):
        return pltpu.VMEM((FRAMES * WIN, width * WIDTH), jnp.bfloat16)

    whole = (FRAMES, WIN, WIDTH)
    outs = pl.pallas_call(
        second_kernel,
        grid=(TILES + 12,),
        in_specs=[
            pl.BlockSpec(memory_space=pltpu.SMEM),
            pl.BlockSpec(memory_space=pltpu.SMEM),
            tile(WIDTH),
            tile(WIDTH),
            weight_spec(weights, 0),
            pl.BlockSpec(memory_space=pl.ANY),
            pl.BlockSpec((4, WIDTH), lambda i: (0, 0)),
        ],
        out_specs=[
            tile(WIDTH),
            tile(WIDTH),
            pl.BlockSpec((4, 8, WIDTH), lambda i: (0, 0, 0)),
            pl.BlockSpec(memory_space=pl.ANY),
            pl.BlockSpec(memory_space=pl.ANY),
        ],
        out_shape=[
            jax.ShapeDtypeStruct(whole, jnp.bfloat16),
            jax.ShapeDtypeStruct(whole, jnp.float32),
            jax.ShapeDtypeStruct((4, 8, WIDTH), jnp.float32),
            *grad_shapes(12 * SLAB),
        ],
        scratch_shapes=[
            pltpu.VMEM((HALF, 2 * HALF), jnp.float32),
            pltpu.VMEM((2, HEADS // 2, 2 * HALF, 128), jnp.bfloat16),
            pltpu.VMEM((2, HALF, WIDTH), jnp.bfloat16),
            pltpu.VMEM((2, HALF, WIDTH), jnp.bfloat16),
            pltpu.VMEM((2, HEADS // 2, HALF, 2 * HALF), jnp.bfloat16),
            pltpu.VMEM((TILE, 4 * WIDTH), jnp.float32),
            held(1),
            held(3),
            held(1),
            held(1),
            held(1),
            held(4),
            held(4),
            held(1),
            pltpu.VMEM((BLOCKS, 4 * SLAB, WIDTH), jnp.bfloat16),
            pltpu.VMEM((BLOCKS, 4 * SLAB, WIDTH), jnp.bfloat16),
            pltpu.VMEM((BLOCKS // 2, 12 * SLAB, WIDTH), jnp.bfloat16),
            pltpu.VMEM((BLOCKS // 2, 12 * SLAB, WIDTH), jnp.bfloat16),
            pltpu.SemaphoreType.DMA((2,)),
            pltpu.SemaphoreType.DMA((2, 12)),
        ],
        compiler_params=pltpu.CompilerParams(vmem_limit_bytes=VMEM_BYTES),
        cost_estimate=COST,
        name="second_block",
    )(
        frame_counts,
        core,
        inputs.reshape(whole),
        cotangent.reshape(whole),
        weights,
        weights,
        gains,
    )
    return (
        outs[0].reshape(-1, WIDTH),
        outs[1].reshape(-1, WIDTH),
        outs[2],
        tuple(outs[3:]),
    )


def first_back_kernel(
    core, upstream, slopes, middle, weights, weights_up, weights_down, gains, hidden, hidden_in,
    attended, queries_in, keys_in, values_in, probs, normed, middle_grad_out, sums, projected_grad_out,
    mine_out, other_out, up_grads, out_grads, branch_grads, attended_grads, projected_grads,
    mine, other, store_sems,
):
    step = pl.program_id(0)
    heads_at = TILES + 9
    last_at = heads_at + HEADS // 2

    def stores(unit, place):
        return grad_copies(((mine, mine_out), (other, other_out)), store_sems, unit, place)

    @pl.when(step == 0)
    def _():
        sums[...] = jnp.zeros_like(sums)

    @pl.when(step < TILES)
    def _():
        rows = pl.ds(pl.multiple_of(step * TILE, TILE), TILE)
        out_grad = upstream[...].astype(jnp.bfloat16)
        out_grads[rows, :] = out_grad
        hidden_in_grad = jnp.zeros((TILE, WIDTH), jnp.float32)
        for index in range(4):
            columns = slice(WIDTH * index, WIDTH * index + WIDTH)
            up_grad = (dot_nt(out_grad, down_rows(weights_down, index)) * slopes[:, columns]).astype(
                jnp.bfloat16
            )
            up_grads[rows, columns] = up_grad
            hidden_in_grad = hidden_in_grad + dot_nt(up_grad, slab(weights_up, index))
        normal, scale = row_norm(middle[...])
        sums[0] += fold_rows(hidden_in_grad * normal)
        sums[1] += fold_rows(hidden_in_grad)
        middle_grad = upstream[...] + row_norm_back(hidden_in_grad, gains[2:3, :], normal, scale)
        middle_grad_out[...] = middle_grad
        branch_grad = middle_grad.astype(jnp.bfloat16)
        branch_grads[rows, :] = branch_grad
        attended_grad = dot_nt(branch_grad, slab(weights, 3)).astype(jnp.bfloat16)
        for pair in range(HEADS // 2):
            attended_grads[pair, rows, :] = attended_grad[:, 128 * pair : 128 * pair + 128]

    @pl.when((step >= TILES) & (step < TILES + 4))
    def _():
        right = up_grads[:, part_of(step, TILES)]
        row = slab_row(step, TILES)
        outer_store(core, hidden_in, right, mine, other, 0, row, SLAB)
        for copy in stores(step - TILES, slab_place(row)):
            copy.start()

    @pl.when((step >= TILES + 4) & (step < TILES + 8))
    def _():
        block = (step - TILES - 4) * 4
        outer_store(core, hidden, out_grads[...], mine, other, block, 8 * SLAB, 4 * SLAB)
        for copy in stores(step - TILES, down_place(block)):
            copy.start()

    @pl.when(step == TILES + 8)
    def _():
        outer_store(core, attended, branch_grads[...], mine, other, 0, 4 * SLAB, SLAB)
        for copy in stores(8, slab_place(4 * SLAB)):
            copy.start()

    @pl.when((step >= heads_at) & (step < last_at))
    def _():
        pair = step - heads_at
        frames = list(enumerate(frame_pairs()))
        rows = [slice(WIN * frame, WIN * frame + 2 * WIN) for _, frame in frames]
        grads = [stack_heads(attended_grads[pair, row, :]) for row in rows]
        share_grads = [dot_nt(grad, values_in[row, :]) for grad, row in zip(grads, rows)]
        shares = [probs[index, 0] for index, _ in frames]
        value_grads = [dot_tn(share, grad) for share, grad in zip(shares, grads)]
        score_grads = []
        for share, share_grad in zip(shares, share_grads):
            share = share.astype(jnp.float32)
            total = jnp.sum(share_grad * share, axis=-1, keepdims=True)
            score_grads.append((share * (share_grad - total)).astype(jnp.bfloat16))
        query_grads = [dot_nn(grad, keys_in[row, :]) for grad, row in zip(score_grads, rows)]
        key_grads = [
            dot_tn(grad, stack_heads(queries_in[row, :] * SCALE))
            for grad, row in zip(score_grads, rows)
        ]
        query_grads = [merge_heads(grad) * SCALE for grad in query_grads]
        for index, parts in enumerate((query_grads, key_grads, value_grads)):
            lanes = pl.ds(pl.multiple_of(pair * 128 + WIDTH * index, 128), 128)
            for row, part in zip(rows, parts):
                projected_grads[row, lanes] = part.astype(jnp.bfloat16)

    @pl.when(step >= last_at)
    def _():
        right = projected_grads[:, part_of(step, last_at)]
        projected_grad_out[...] = right
        row = slab_row(step, last_at - 5)
        outer_store(core, normed, right, mine, other, 0, row, SLAB)
        for copy in stores(step - last_at + 9, slab_place(row)):
            copy.start()

    @pl.when(step == last_at + 2)
    def _():
        places = [slab_place(SLAB * index) for index in range(4)]
        places += [down_place(4 * index) for index in range(4)]
        places += [slab_place(SLAB * index) for index in range(4, 8)]
        for unit, place in enumerate(places):
            for copy in stores(unit, place):
                copy.wait()


def first_back(
    core, upstream, slopes, middle, weights, late_weights, late_at, gains, hidden, hidden_in, attended,
    projected, probs, normed,
):
    count = upstream.shape[0]
    pairs = HEADS // 2
    heads_at = TILES + 9
    last_at = heads_at + pairs

    def tile(width):
        return pl.BlockSpec((TILE, width), lambda i: (jnp.minimum(i, TILES - 1), 0))

    def whole(*shape):
        return pl.BlockSpec(shape, lambda i: (0,) * len(shape), pipeline_mode=pl.Buffered(1))

    def pair_of(step):
        return jnp.clip(step - heads_at, 0, pairs - 1)

    def lanes(first):
        return pl.BlockSpec((count, 128), lambda i: (0, first + pair_of(i)))

    def held(width):
        return pltpu.VMEM((count, width * WIDTH), jnp.bfloat16)

    outs = pl.pallas_call(
        first_back_kernel,
        grid=(last_at + 3,),
        in_specs=[
            pl.BlockSpec(memory_space=pltpu.SMEM),
            tile(WIDTH),
            tile(4 * WIDTH),
            tile(WIDTH),
            weight_spec(weights, 0),
            weight_spec(late_weights, late_at),
            weight_spec(late_weights, late_at + 1),
            whole(4, WIDTH),
            pl.BlockSpec((count, WIDTH), lambda i: (0, jnp.clip(i - TILES - 4, 0, 3))),
            whole(count, WIDTH),
            whole(count, WIDTH),
            lanes(0),
            lanes(pairs),
            lanes(2 * pairs),
            pl.BlockSpec(
                ((FRAMES + 1) // 2, 1, 4 * WIN, 2 * WIN), lambda i: (0, pair_of(i), 0, 0)
            ),
            whole(count, WIDTH),
        ],
        out_specs=[
            tile(WIDTH),
            pl.BlockSpec((2, 8, WIDTH), lambda i: (0, 0, 0)),
            pl.BlockSpec((count, WIDTH), lambda i: (0, jnp.clip(i - last_at, 0, 2))),
            pl.BlockSpec(memory_space=pl.ANY),
            pl.BlockSpec(memory_space=pl.ANY),
        ],
        out_shape=[
            jax.ShapeDtypeStruct((count, WIDTH), jnp.float32),
            jax.ShapeDtypeStruct((2, 8, WIDTH), jnp.float32),
            jax.ShapeDtypeStruct((count, 3 * WIDTH), jnp.bfloat16),
            *grad_shapes(12 * SLAB),
        ],
        scratch_shapes=[
            held(4),
            held(1),
            held(1),
            pltpu.VMEM((pairs, count, 128), jnp.bfloat16),
            held(3),
            pltpu.VMEM((BLOCKS // 2, 12 * SLAB, WIDTH), jnp.bfloat16),
            pltpu.VMEM((BLOCKS // 2, 12 * SLAB, WIDTH), jnp.bfloat16),
            pltpu.SemaphoreType.DMA((2, 12)),
        ],
        compiler_params=pltpu.CompilerParams(vmem_limit_bytes=VMEM_BYTES),
        cost_estimate=COST,
        name="first_back",
    )(
        core, upstream, slopes, middle, weights, late_weights, late_weights, gains, hidden, hidden_in,
        attended, projected, projected, projected, probs, normed,
    )
    return (*outs[:3], tuple(outs[3:]))


def first_input_back_kernel(projected_grad, tokens, middle_grad, weights, gains, grad_out, sums):
    @pl.when(pl.program_id(0) == 0)
    def _():
        sums[...] = jnp.zeros_like(sums)

    normed_grad = jnp.zeros((TILE, WIDTH), jnp.float32)
    for index in range(3):
        part = projected_grad[:, WIDTH * index : WIDTH * index + WIDTH]
        normed_grad = normed_grad + dot_nt(part, slab(weights, index))
    normal, scale = row_norm(tokens[...].astype(jnp.float32))
    sums[0] += fold_rows(normed_grad * normal)
    sums[1] += fold_rows(normed_grad)
    grad_out[...] = middle_grad[...] + row_norm_back(normed_grad, gains[0:1, :], normal, scale)


def first_input_back(projected_grad, tokens, middle_grad, weights, gains):
    count = tokens.shape[0]

    def tile(width):
        return pl.BlockSpec((TILE, width), lambda i: (i, 0))

    def whole(*shape):
        return pl.BlockSpec(shape, lambda i: (0,) * len(shape), pipeline_mode=pl.Buffered(1))

    return pl.pallas_call(
        first_input_back_kernel,
        grid=(TILES,),
        in_specs=[
            tile(3 * WIDTH),
            tile(WIDTH),
            tile(WIDTH),
            whole(BLOCKS, 3 * SLAB, WIDTH),
            whole(4, WIDTH),
        ],
        out_specs=[tile(WIDTH), pl.BlockSpec((2, 8, WIDTH), lambda i: (0, 0, 0))],
        out_shape=[
            jax.ShapeDtypeStruct((count, WIDTH), jnp.float32),
            jax.ShapeDtypeStruct((2, 8, WIDTH), jnp.float32),
        ],
        compiler_params=pltpu.CompilerParams(vmem_limit_bytes=VMEM_BYTES),
        cost_estimate=COST,
        name="first_input_back",
    )(projected_grad, tokens, middle_grad, weights, gains)


def place_pieces(place, pieces, out):
    across, plane, core = place[0], place[1], place[2]
    for index, piece in enumerate(pieces):
        column = (across ^ (index % 4)) * 8 + (core ^ (index // 4))
        for way in range(4):
            out[column + (plane ^ way) * 2] = piece[way]


def arrange_kernel(place, *refs):
    place_pieces(place, refs[:-1], refs[-1])


def arrange(place, pieces, name):
    rows = pieces[0].shape[1]
    return pl.pallas_call(
        arrange_kernel,
        in_specs=[pl.BlockSpec(memory_space=pltpu.SMEM)]
        + [pl.BlockSpec(memory_space=pltpu.VMEM)] * 8,
        out_shape=jax.ShapeDtypeStruct((BLOCKS, rows, WIDTH), jnp.bfloat16),
        compiler_params=pltpu.CompilerParams(vmem_limit_bytes=VMEM_BYTES),
        cost_estimate=COST,
        name=name,
    )(place, *pieces)


def pack_kernel(w_qkv, w_out, w_up, w_down, norm, early, late, second):
    def narrow(array):
        return array.astype(jnp.bfloat16)

    for block, (start, rest) in enumerate(((early, late), (second, second))):
        for index in range(3):
            columns = slice(WIDTH * index, WIDTH * index + WIDTH)
            start[SLAB * index : SLAB * index + SLAB, :] = narrow(w_qkv[block, :, columns])
        start[3 * SLAB : 4 * SLAB, :] = narrow(w_out[block])
        first = 4 * SLAB * block
        for index in range(4):
            columns = slice(WIDTH * index, WIDTH * index + WIDTH)
            row = first + SLAB * index
            rest[row : row + SLAB, :] = narrow(w_up[block, :, columns])
        rest[first + 4 * SLAB : first + 8 * SLAB, :] = narrow(w_down[block])
    row = jnp.concatenate([norm[...]] * (WIDTH // norm.shape[1]), axis=1)
    early[4 * SLAB :, :] = narrow(jnp.broadcast_to(row, (SLAB, WIDTH)))


def pack_all(w_qkv, w_out, w_up, w_down, norm_row):
    return pl.pallas_call(
        pack_kernel,
        out_shape=[
            jax.ShapeDtypeStruct((rows, WIDTH), jnp.bfloat16)
            for rows in (5 * SLAB, 8 * SLAB, 12 * SLAB)
        ],
        compiler_params=pltpu.CompilerParams(vmem_limit_bytes=VMEM_BYTES),
        cost_estimate=COST,
        name="pack",
    )(w_qkv, w_out, w_up, w_down, norm_row)


def adam_parts(gradient, first_moment, second_moment):
    first_next = BETA_FIRST * first_moment + (1.0 - BETA_FIRST) * gradient
    second_next = BETA_SECOND * second_moment + (1.0 - BETA_SECOND) * gradient * gradient
    direction = (
        first_next
        / (1.0 - BETA_FIRST**STEP)
        / (jnp.sqrt(second_next / (1.0 - BETA_SECOND**STEP)) + ADAM_EPS)
    )
    return (first_next, second_next, direction)


def pack_weights(part_qkv, part_out, part_up, part_down):
    return jnp.concatenate(
        [part_qkv[:, WIDTH * i : WIDTH * i + WIDTH] for i in range(3)]
        + [part_out]
        + [part_up[:, WIDTH * i : WIDTH * i + WIDTH] for i in range(4)]
        + [part_down],
        axis=0,
    ).astype(jnp.bfloat16)


def to_blocks(packed, rows):
    if rows == SLAB:
        return packed
    packed = packed[:, : 12 * rows]
    slabs = packed[:, : 8 * rows].reshape(BLOCKS, -1, 8, rows, WIDTH).transpose(0, 2, 1, 3, 4)
    return jnp.concatenate(
        [
            slabs.reshape(BLOCKS, 8 * SLAB, WIDTH),
            packed[:, 8 * rows :].reshape(BLOCKS, 4 * SLAB, WIDTH),
        ],
        axis=1,
    )


def from_blocks(grads, rows, narrow):
    if rows == SLAB:
        return grads
    slabs = grads[:, : narrow * SLAB].reshape(BLOCKS, narrow, -1, rows, WIDTH)
    slabs = slabs.transpose(0, 2, 1, 3, 4).reshape(-1, narrow * rows, WIDTH)
    if grads.shape[1] == narrow * SLAB:
        return slabs
    wide = grads[:, narrow * SLAB :].reshape(slabs.shape[0], -1, WIDTH)
    return jnp.concatenate([slabs, wide], axis=1)


def swap(array, mask):
    count = lax.axis_size("dp") * lax.axis_size("fsdp")
    return lax.ppermute(array, ("dp", "fsdp"), [(device, device ^ mask) for device in range(count)])


def after(value, *others):
    return lax.optimization_barrier((value, *others))[0]


def gather_by_chips(shards):
    results = []
    steps = [(), ()]
    for shard in shards:
        shard = after(shard, *steps[0])
        steps[0] = [swap(shard, 2 * way) for way in (1, 2, 3)]
        pieces = after(jnp.stack([shard] + steps[0]), *steps[1])
        steps[1] = [swap(pieces, 8 * way) for way in (1, 2, 3)]
        results.append([pieces] + steps[1])
    return results


def gather_cores(pieces):
    return pieces + [swap(piece, 1) for piece in pieces]


def sum_at(arrays, index):
    total = sum(
        lax.dynamic_index_in_dim(array, index, 0, keepdims=False).astype(jnp.float32)
        for array in arrays
    )
    return total.astype(jnp.bfloat16)


def scatter_cores(pair, place):
    both = [array.reshape(4, 4, -1, WIDTH) for array in (pair[0], swap(pair[1], 1))]
    return [sum_at(both, place[0] ^ way) for way in (0, 3, 1, 2)]


def swap_chips(pieces):
    return [pieces[0]] + [swap(piece, 8 * way) for piece, way in zip(pieces[1:], (3, 1, 2))]


def fold_planes(pieces, place):
    return [sum_at(pieces, place[1] ^ way) for way in (0, 3, 2, 1)]


def scatter_planes(pieces, *others):
    pieces = [pieces[0]] + [swap(piece, 2 * way) for piece, way in zip(pieces[1:], (3, 2, 1))]
    pieces[0] = after(pieces[0], *others)
    return sum(piece.astype(jnp.float32) for piece in pieces)


def scatter_whole(pair, rows, narrow):
    grads = jnp.stack(pair, axis=1).reshape(BLOCKS, -1, WIDTH)
    summed = lax.psum_scatter(
        from_blocks(grads, rows, narrow), ("dp", "fsdp"), scatter_dimension=0, tiled=False
    )
    return summed.astype(jnp.float32)


def body(
    tokens,
    frame_counts,
    cotangent,
    w_qkv,
    w_out,
    w_up,
    w_down,
    norm_params,
    first_qkv,
    first_out,
    first_up,
    first_down,
    first_norm,
    second_qkv,
    second_out,
    second_up,
    second_down,
    second_norm,
):
    masters = (w_qkv, w_out, w_up, w_down)
    axes = ("dp", "fsdp")
    shards = lax.axis_size("dp") * lax.axis_size("fsdp")
    rows = w_out.shape[1]
    by_chips = (lax.axis_size("dp"), lax.axis_size("fsdp")) == (4, 8)
    fsdp = lax.axis_index("fsdp")
    place = jnp.stack([lax.axis_index("dp"), fsdp // 2, fsdp % 2]).astype(jnp.int32)
    norm_row = norm_params.reshape(1, -1)
    if by_chips:
        *shard, second_shard = pack_all(w_qkv, w_out, w_up, w_down, norm_row)
        early, late_pieces = gather_by_chips(shard)
        early = arrange(place, gather_cores(early), "arrange_early")
        norm_values = early[:, 4 * rows, : 8 * rows]
    else:
        shard = pack_weights(w_qkv[0], w_out[0], w_up[0], w_down[0])
        second_shard = pack_weights(w_qkv[1], w_out[1], w_up[1], w_down[1])
        norm_rows = jnp.pad(norm_row, ((0, rows - 1), (0, WIDTH - 8 * rows)))
        shard = jnp.concatenate([shard, norm_rows.astype(jnp.bfloat16)], axis=0)
        gathered = lax.all_gather(shard, axes, axis=0)
        norm_values = gathered[:, 12 * rows, : 8 * rows]
        early = to_blocks(gathered, rows)
    gains = norm_values.reshape(shards, 2, 4, rows)
    gains = gains.transpose(1, 2, 0, 3).reshape(2, 4, WIDTH).astype(jnp.float32)
    weights_second = to_blocks(lax.all_gather(second_shard, axes, axis=0), rows)

    normed, projected, probs, attended, middle, hidden_in = first_attention(tokens, early, gains[0])
    if by_chips:
        late_pieces = gather_cores([after(piece, hidden_in) for piece in late_pieces])
    else:
        late_pieces = [early[:, 4 * SLAB : 12 * SLAB]]
    hidden, slopes, stream, late = first_mlp(place, middle, hidden_in, late_pieces)
    core = place[2:] if by_chips else jnp.zeros((1,), jnp.int32)
    block_out, upstream, sums_second, pair_second = second_block(
        frame_counts, core, stream, cotangent, weights_second, gains[1]
    )
    if by_chips:
        second = scatter_cores(pair_second, place)
        upstream = after(upstream, *second)
        second = swap_chips(second)
    middle_grad, sums_late, projected_grad, pair_first = first_back(
        core, upstream, slopes, middle, early, late, 0, gains[0], hidden, hidden_in, attended,
        projected, probs, normed,
    )
    if by_chips:
        second[0], *pair_first = lax.optimization_barrier((second[0], *pair_first, *second[1:]))[:3]
        first = scatter_cores(pair_first, place)
        projected_grad = after(projected_grad, *first)
        first = swap_chips(first)
        reduced_second = scatter_planes(fold_planes(second, place))
    tokens_grad, sums_early = first_input_back(
        projected_grad, tokens, middle_grad, early, gains[0]
    )
    if by_chips:
        first[0] = after(first[0], tokens_grad)
        reduced_first = scatter_planes(fold_planes(first, place))
    else:
        reduced_second = scatter_whole(pair_second, rows, 8)
        reduced_first = scatter_whole(pair_first, rows, 8)

    def columns(packed, first, last):
        return jnp.concatenate(
            [packed[rows * index : rows * index + rows] for index in range(first, last)], axis=1
        )

    reduced_first, reduced_second = (
        (columns(both, 5, 8), columns(both, 4, 5), columns(both, 0, 4), both[8 * rows :])
        for both in (reduced_first, reduced_second)
    )

    norm_parts = jnp.concatenate(
        [jnp.sum(part, axis=1) for part in (sums_early, sums_late, sums_second)]
    )
    norm_parts = norm_parts.reshape(8, shards, rows).transpose(1, 0, 2).reshape(shards, -1)
    stacked = [jnp.stack(pair) for pair in zip(reduced_first, reduced_second)]
    firsts = (first_qkv, first_out, first_up, first_down)
    seconds = (second_qkv, second_out, second_up, second_down)
    updates = [adam_parts(*parts) for parts in zip(stacked, firsts, seconds)]
    directions = [update[2] + DECAY_RATE * master for update, master in zip(updates, masters)]
    local_squares = jnp.stack(
        [
            jnp.stack([jnp.sum(matrix * matrix, axis=(1, 2)) for matrix in group], axis=1)
            for group in (masters, directions)
        ],
        axis=2,
    )
    message = jnp.concatenate(
        [norm_parts, jnp.broadcast_to(local_squares.reshape(1, 16), (shards, 16))], axis=1
    )
    arrived = jnp.sum(lax.all_to_all(message, axes, 0, 0, tiled=True), axis=0)
    matrix_norms = jnp.sqrt(arrived[-16:].reshape(2, 4, 2))
    norm_update = adam_parts(arrived[:-16].reshape(2, 2, 2, rows), first_norm, second_norm)
    updates.append(norm_update)
    updated = [
        masters[index]
        - RATE
        * (matrix_norms[:, index, 0] / matrix_norms[:, index, 1])[:, None, None]
        * directions[index]
        for index in range(4)
    ]
    return (
        block_out,
        tokens_grad,
        *updated,
        norm_params - RATE * norm_update[2],
        *(array.astype(jnp.bfloat16) for array in updated),
        *(update[0] for update in updates),
        *(update[1] for update in updates),
        matrix_norms,
    )


def solution(mesh):
    in_specs = (
        P(("dp", "fsdp"), None),
        P(("dp", "fsdp")),
        P(("dp", "fsdp"), None),
        P(None, ("dp", "fsdp"), None),
        P(None, ("dp", "fsdp"), None),
        P(None, ("dp", "fsdp"), None),
        P(None, ("dp", "fsdp"), None),
        P(None, None, None, ("dp", "fsdp")),
        P(None, ("dp", "fsdp"), None),
        P(None, ("dp", "fsdp"), None),
        P(None, ("dp", "fsdp"), None),
        P(None, ("dp", "fsdp"), None),
        P(None, None, None, ("dp", "fsdp")),
        P(None, ("dp", "fsdp"), None),
        P(None, ("dp", "fsdp"), None),
        P(None, ("dp", "fsdp"), None),
        P(None, ("dp", "fsdp"), None),
        P(None, None, None, ("dp", "fsdp")),
    )
    out_specs = (
        P(("dp", "fsdp"), None),
        P(("dp", "fsdp"), None),
        P(None, ("dp", "fsdp"), None),
        P(None, ("dp", "fsdp"), None),
        P(None, ("dp", "fsdp"), None),
        P(None, ("dp", "fsdp"), None),
        P(None, None, None, ("dp", "fsdp")),
        P(None, ("dp", "fsdp"), None),
        P(None, ("dp", "fsdp"), None),
        P(None, ("dp", "fsdp"), None),
        P(None, ("dp", "fsdp"), None),
        P(None, ("dp", "fsdp"), None),
        P(None, ("dp", "fsdp"), None),
        P(None, ("dp", "fsdp"), None),
        P(None, ("dp", "fsdp"), None),
        P(None, None, None, ("dp", "fsdp")),
        P(None, ("dp", "fsdp"), None),
        P(None, ("dp", "fsdp"), None),
        P(None, ("dp", "fsdp"), None),
        P(None, ("dp", "fsdp"), None),
        P(None, None, None, ("dp", "fsdp")),
        P(),
    )
    return jax.shard_map(body, mesh=mesh, in_specs=in_specs, out_specs=out_specs, check_vma=False)
```
